32 devices in a mesh: wrap: 4 (over z), normal: 8 (over y, x, core).
Axes of the slice: x: 2, y: 2, z: 4, core: 2. Of those that a mesh axis runs over, the one named last changes fastest.
Arguments:
- state: float32 [5, 4, 64, 512], P(None, None, 'normal', 'wrap'), may hold values from -2 to 3, as said below
- metrics: float32 [4, 4, 64, 512], P(None, None, 'normal', 'wrap'), may hold values from 0.5 to 1.5
- time_step: float32 [4, 64, 512], P(None, 'normal', 'wrap'), may hold values from 40 to 400
- dissipation: float32 [2, 4, 64, 512], P(None, None, 'normal', 'wrap'), may hold values from 0.05 to 0.5
Outputs:
- increment: float32 [5, 4, 64, 512], P(None, None, 'normal', 'wrap')
The draws below stay inside these ranges and needn't reach their ends.
Inputs may be any that keep to these rules, and one draw needn't show every extreme that they name: `state`: component 0 (density) lies in 0.7 to 1.4 and component 4 (energy) in 2 to 3; components 1 to 3 are momenta.
All inputs are finite; a program needn't handle non-finite values. Where the reference program divides by a largest or mean magnitude, that divisor is 1e-20 or more.
Results may differ from the reference program's by a relative error of at most 0.00017.
Values sent between devices are 32-bit elements; how exact they have to be, the bound alone decides.
No kernel may reach another device: no remote copies, remote signals or barrier semaphores. Data moves between devices by JAX's collectives and lax.ppermute only.
A program may use at most 128 MiB of HBM per device.

```python
import math
import jax
import jax.numpy as jnp
from jax import lax

SPAN = 4
NXI = 512
NETA = 64


def draw_state(key, part):
    subkeys = jax.random.split(key, 3)
    grid_shape = (SPAN, NETA, NXI)
    density = jax.random.uniform(subkeys[0], grid_shape, jnp.float32, 0.7, 1.4)
    energy = jax.random.uniform(subkeys[1], grid_shape, jnp.float32, 2.0, 3.0)
    momentum = jnp.clip(0.5 * jax.random.normal(subkeys[2], (3,) + grid_shape, jnp.float32), -2.0, 2.0)
    return jnp.concatenate([density[None], momentum, energy[None]], axis=0)


def shard_levels(rng, shape, pieces, least, top_value):
    level = 1.0
    for dim, parts in pieces:
        heights = jax.random.uniform(jax.random.fold_in(jax.random.fold_in(rng, 6), dim), (parts,), jnp.float32, least / len(pieces), top_value / len(pieces))
        level = level * jnp.repeat(jnp.exp(heights), shape[dim] // parts).reshape((-1,) + (1,) * (len(shape) - 1 - dim))
    return level


def setup_inputs(seed: int = 0) -> dict:
    streams_of = jax.random.split(jax.random.key(seed), 5)
    state = draw_state(jax.random.fold_in(streams_of[4], 71), 0)
    metrics = jnp.clip(0.5 + 1.0 * jax.random.uniform(streams_of[1], (4, SPAN, NETA, NXI), jnp.float32) ** shard_levels(streams_of[1], (4, SPAN, NETA, NXI), ((2, 8), (3, 4)), -0.2, 0.2), 0.5, 1.5)
    time_step = jnp.clip(jnp.exp(math.log(400.0) - 2.3025851 * jax.random.uniform(streams_of[2], (SPAN, NETA, NXI), jnp.float32) ** shard_levels(streams_of[2], (SPAN, NETA, NXI), ((1, 8), (2, 4)), -0.2, 0.2)), 40.0, 400.0)
    dissipation = jnp.clip(jnp.exp(math.log(0.5) - 2.3025851 * jax.random.uniform(streams_of[3], (2, SPAN, NETA, NXI), jnp.float32) ** shard_levels(streams_of[3], (2, SPAN, NETA, NXI), ((2, 8), (3, 4)), -0.2, 0.2)), 0.05, 0.5)
    return {"state": state, "metrics": metrics, "time_step": time_step, "dissipation": dissipation}


GAMMA = 1.4

def flux_jacobian(face_state, metric_x, metric_y):
    density = face_state[0]
    vel_u = face_state[1] / density
    vel_v = face_state[2] / density
    vel_w = face_state[3] / density
    energy = face_state[4] / density
    gamma_less = GAMMA - 1.0
    contra = metric_x * vel_u + metric_y * vel_v
    kinetic = 0.5 * gamma_less * (vel_u * vel_u + vel_v * vel_v + vel_w * vel_w)
    blank = jnp.zeros_like(density)
    enthalpy = GAMMA * energy - kinetic
    entries = [[blank, metric_x, metric_y, blank, blank], [metric_x * kinetic - vel_u * contra, contra - (GAMMA - 2.0) * metric_x * vel_u, metric_y * vel_u - gamma_less * metric_x * vel_v, -gamma_less * metric_x * vel_w, gamma_less * metric_x], [metric_y * kinetic - vel_v * contra, metric_x * vel_v - gamma_less * metric_y * vel_u, contra - (GAMMA - 2.0) * metric_y * vel_v, -gamma_less * metric_y * vel_w, gamma_less * metric_y], [-vel_w * contra, metric_x * vel_w, metric_y * vel_w, contra, blank], [contra * (2.0 * kinetic - GAMMA * energy), metric_x * enthalpy - gamma_less * vel_u * contra, metric_y * enthalpy - gamma_less * vel_v * contra, -gamma_less * vel_w * contra, GAMMA * contra]]
    return jnp.stack([jnp.stack(entry_row) for entry_row in entries])

def block_product(left, right):
    return jnp.sum(left[:, :, None] * right[None, :, :], axis=1)

def block_apply(matrix, vector):
    return jnp.sum(matrix * vector[None], axis=1)

def face_terms(extended, metric_at, spread_at):
    state = extended[0:5]
    face_state = 0.5 * (state[:, :-1] + state[:, 1:])
    metric = extended[metric_at:metric_at + 2]
    face_metric = 0.5 * (metric[:, :-1] + metric[:, 1:])
    step_size = extended[9, :-1]
    spread = extended[spread_at, :-1]
    jacobian = flux_jacobian(face_state, face_metric[0], face_metric[1])
    row_scale = jnp.max(jnp.sum(jnp.abs(jacobian), axis=1), axis=0)
    normed = jacobian / row_scale
    flipped = jnp.swapaxes(normed, 0, 1)
    identity = jnp.eye(5, dtype=jnp.float32)[:, :, None, None]
    convect = step_size * (0.5 * (normed + flipped))
    damping = step_size * spread * (0.5 * (identity + block_product(flipped, normed)))
    face_flux = block_apply(convect, face_state) - block_apply(damping, state[:, 1:] - state[:, :-1])
    residual = -(face_flux[:, 1:] - face_flux[:, :-1])
    lower = -0.5 * convect[:, :, :-1] - damping[:, :, :-1]
    middle = identity + damping[:, :, :-1] + damping[:, :, 1:]
    upper = 0.5 * convect[:, :, 1:] - damping[:, :, 1:]
    return (residual, lower, middle, upper)

def thomas_forms(lower, middle, upper, rhs):
    cell_count = rhs.shape[1]
    line_count = rhs.shape[2]
    lower_t = jnp.transpose(lower, (2, 3, 0, 1))
    middle_t = jnp.transpose(middle, (2, 3, 0, 1))
    upper_t = jnp.transpose(upper, (2, 3, 0, 1))
    load_col = jnp.transpose(rhs, (1, 2, 0))[..., None]
    position = jnp.arange(cell_count).reshape(cell_count, 1, 1, 1)
    at_first = position == 0
    at_last = position == cell_count - 1
    left_cols = jnp.where(at_first, -lower_t, jnp.zeros_like(lower_t))
    right_cols = jnp.where(at_last, -upper_t, jnp.zeros_like(upper_t))
    lower_t = jnp.where(at_first, jnp.zeros_like(lower_t), lower_t)
    upper_t = jnp.where(at_last, jnp.zeros_like(upper_t), upper_t)
    load_cols = jnp.concatenate([load_col, left_cols, right_cols], axis=-1)

    def forward(carry, inputs):
        prev_weight, prev_partial = carry
        low_block, mid_block, upp_block, load_block = inputs
        pivot_block = mid_block - jnp.einsum('lij,ljk->lik', low_block, prev_weight, precision=lax.Precision.HIGHEST)
        weight = jnp.linalg.solve(pivot_block, upp_block)
        partial_value = jnp.linalg.solve(pivot_block, load_block - jnp.einsum('lij,ljk->lik', low_block, prev_partial, precision=lax.Precision.HIGHEST))
        return ((weight, partial_value), (weight, partial_value))
    initial = (jnp.zeros((line_count, 5, 5), jnp.float32), jnp.zeros((line_count, 5, 11), jnp.float32))
    unused, (weights, partials) = lax.scan(forward, initial, (lower_t, middle_t, upper_t, load_cols))

    def backward(later, inputs):
        weight, partial_value = inputs
        solved = partial_value - jnp.einsum('lij,ljk->lik', weight, later, precision=lax.Precision.HIGHEST)
        return (solved, solved)
    unused_last, solved = lax.scan(backward, jnp.zeros((line_count, 5, 11), jnp.float32), (weights, partials), reverse=True)
    return solved

def cycle_solution(lower, middle, upper, rhs):
    solved = thomas_forms(lower, middle, upper, rhs)
    baseline = solved[..., 0]
    from_left = solved[..., 1:6]
    from_right = solved[..., 6:11]
    identity = jnp.eye(5, dtype=jnp.float32)
    top_rows = jnp.concatenate([identity - from_right[0], -from_left[0]], axis=-1)
    bottom_rows = jnp.concatenate([-from_right[-1], identity - from_left[-1]], axis=-1)
    closure = jnp.concatenate([top_rows, bottom_rows], axis=-2)
    targets = jnp.concatenate([baseline[0], baseline[-1]], axis=-1)[..., None]
    ends = jnp.linalg.solve(closure, targets)[..., 0]
    first_val = ends[:, 0:5]
    last_val = ends[:, 5:10]
    field = baseline + jnp.einsum('nlij,lj->nli', from_left, last_val, precision=lax.Precision.HIGHEST)
    field = field + jnp.einsum('nlij,lj->nli', from_right, first_val, precision=lax.Precision.HIGHEST)
    return jnp.transpose(field, (2, 0, 1))

def open_solution(lower, middle, upper, rhs):
    solved = thomas_forms(lower, middle, upper, rhs)
    return jnp.transpose(solved[..., 0], (2, 0, 1))

def station(cells):
    cycle_ext = jnp.concatenate([cells[:, :, -1:], cells, cells[:, :, :1]], axis=2)
    cycle_ext = jnp.transpose(cycle_ext, (0, 2, 1))
    wall_ext = jnp.pad(cells, ((0, 0), (1, 1), (0, 0)))
    cycle_res, cycle_low, cycle_mid, cycle_upp = face_terms(cycle_ext, 5, 10)
    wall_res, wall_low, wall_mid, wall_upp = face_terms(wall_ext, 7, 11)
    total = cycle_res + jnp.transpose(wall_res, (0, 2, 1))
    swept = cycle_solution(cycle_low, cycle_mid, cycle_upp, total)
    return open_solution(wall_low, wall_mid, wall_upp, jnp.transpose(swept, (0, 2, 1)))

def reference(state, metrics, time_step, dissipation):
    cells = jnp.concatenate([state, metrics, time_step[None], dissipation], axis=0)
    result = lax.map(station, jnp.transpose(cells, (1, 0, 2, 3)))
    return jnp.transpose(result, (1, 0, 2, 3))
```

```python
import jax
import jax.numpy as jnp
from jax import lax
from jax.experimental import pallas as pl
from jax.experimental.pallas import tpu as pltpu
from jax.sharding import PartitionSpec as P

GAMMA = 1.4
LESS = GAMMA - 1.0
VMEM_LIMIT = 16 * 1024 * 1024
TILE = (8, 128)
LANES = 128


def mat_mul(a, b):
    out = []
    for i in range(5):
        row = []
        for j in range(5):
            total = a[i][0] * b[0][j]
            for k in range(1, 5):
                total = total + a[i][k] * b[k][j]
            row.append(total)
        out.append(row)
    return out


def mat_vec(a, x):
    out = []
    for i in range(5):
        total = a[i][0] * x[0]
        for k in range(1, 5):
            total = total + a[i][k] * x[k]
        out.append(total)
    return out


def mat_map(fn, *mats):
    return [[fn(*(m[i][j] for m in mats)) for j in range(5)] for i in range(5)]


def vec_map(fn, *vecs):
    return [fn(*(v[i] for v in vecs)) for i in range(5)]


def mat_add(a, b):
    return mat_map(lambda x, y: x + y, a, b)


def mat_sub(a, b):
    return mat_map(lambda x, y: x - y, a, b)


def mat_neg(a):
    return mat_map(lambda x: -x, a)


def vec_add(a, b):
    return vec_map(lambda x, y: x + y, a, b)


def vec_sub(a, b):
    return vec_map(lambda x, y: x - y, a, b)


def plus_eye(a):
    return [[a[i][j] + 1.0 if i == j else a[i][j] for j in range(5)] for i in range(5)]


def mat_inv(matrix):
    a = [list(row) for row in matrix]
    for k in range(5):
        pivot = 1.0 / a[k][k]
        row = [a[k][j] * pivot if j != k else pivot for j in range(5)]
        for i in range(5):
            if i == k:
                continue
            factor = a[i][k]
            for j in range(5):
                a[i][j] = -(factor * pivot) if j == k else a[i][j] - factor * row[j]
        a[k] = row
    return a


def face_values(left, right):
    state = [0.5 * (left[i] + right[i]) for i in range(5)]
    m1 = 0.5 * (left[5] + right[5])
    m2 = 0.5 * (left[6] + right[6])
    step, spread = left[7], left[8]
    over = 1.0 / state[0]
    u, v, w, e = (state[i] * over for i in range(1, 5))
    t = m1 * u + m2 * v
    f = (0.5 * LESS) * (u * u + v * v + w * w)
    h = GAMMA * e - f
    jac = [
        [None, m1, m2, None, None],
        [
            m1 * f - u * t,
            t - (GAMMA - 2.0) * m1 * u,
            m2 * u - LESS * m1 * v,
            -LESS * m1 * w,
            LESS * m1,
        ],
        [
            m2 * f - v * t,
            m1 * v - LESS * m2 * u,
            t - (GAMMA - 2.0) * m2 * v,
            -LESS * m2 * w,
            LESS * m2,
        ],
        [-w * t, m1 * w, m2 * w, t, None],
        [
            t * (2.0 * f - GAMMA * e),
            m1 * h - LESS * u * t,
            m2 * h - LESS * v * t,
            -LESS * w * t,
            GAMMA * t,
        ],
    ]
    widest = None
    for row in jac:
        total = None
        for x in row:
            if x is not None:
                total = jnp.abs(x) if total is None else total + jnp.abs(x)
        widest = total if widest is None else jnp.maximum(widest, total)
    scale = 1.0 / widest
    norm = [[None if x is None else x * scale for x in row] for row in jac]
    half_step = 0.5 * step
    weight = half_step * spread
    convect = [[None] * 5 for _ in range(5)]
    damping = [[None] * 5 for _ in range(5)]
    for i in range(5):
        for j in range(i, 5):
            parts = [x for x in (norm[i][j], norm[j][i]) if x is not None]
            if parts:
                c = half_step * (parts[0] + parts[1] if len(parts) == 2 else parts[0])
            else:
                c = jnp.zeros_like(step)
            total = None
            for k in range(5):
                if norm[k][i] is None or norm[k][j] is None:
                    continue
                term = norm[k][i] * norm[k][j]
                total = term if total is None else total + term
            if i == j:
                total = total + 1.0
            d = weight * total
            convect[i][j] = convect[j][i] = c
            damping[i][j] = damping[j][i] = d
    jump = [right[i] - left[i] for i in range(5)]
    flux = vec_sub(mat_vec(convect, state), mat_vec(damping, jump))
    lower = mat_map(lambda c, d: -0.5 * c - d, convect, damping)
    upper = mat_map(lambda c, d: 0.5 * c - d, convect, damping)
    for i in range(5):
        for j in range(i):
            lower[i][j] = lower[j][i]
            upper[i][j] = upper[j][i]
    return damping, lower, upper, flux


def put_mat(ref, at, a, lead=()):
    for i in range(5):
        for j in range(5):
            ref[lead + (at + 5 * i + j,)] = a[i][j]


def get_mat(ref, at, lead=()):
    return [[ref[lead + (at + 5 * i + j,)] for j in range(5)] for i in range(5)]


def put_vec(ref, at, x, lead=()):
    for i in range(5):
        ref[lead + (at + i,)] = x[i]


def get_vec(ref, at, lead=()):
    return [ref[lead + (at + i,)] for i in range(5)]


class Line:
    def __init__(self, dim):
        self.dim = dim
        self.n = TILE[dim]
        self.count = self.n // 4
        self.at = lax.broadcasted_iota(jnp.int32, TILE, dim)
        self.even1 = (self.at & 1) == 0
        self.even2 = (self.at & 2) == 0
        self.inner = self.at < self.n - 2
        self.group = self.at >> 2

    def roll(self, x, by):
        if isinstance(by, int):
            by = by % self.n
            if by == 0:
                return x
        return pltpu.roll(x, by, self.dim)

    def vroll(self, v, by):
        return [self.roll(x, by) for x in v]

    def mroll(self, m, by):
        return [self.vroll(row, by) for row in m]

    def pack1(self, a, b):
        first = jnp.where(self.even1, a, self.roll(b, 1))
        second = jnp.where(self.even1, self.roll(a, -1), b)
        return first, second

    def unpack1(self, first, second):
        a = jnp.where(self.even1, first, self.roll(second, 1))
        b = jnp.where(self.even1, self.roll(first, -1), second)
        return a, b

    def pack2(self, a, b):
        first = jnp.where(self.even2, a, self.roll(b, 2))
        second = jnp.where(self.even2, self.roll(a, -2), b)
        return first, second

    def unpack2(self, first, second):
        a = jnp.where(self.even2, first, self.roll(second, 2))
        b = jnp.where(self.even2, self.roll(first, -2), second)
        return a, b


def line_faces(line, cells_e, cells_o):
    after_e = face_values(cells_e, cells_o)
    nexts = [line.roll(x, -2) for x in cells_e[:7]]
    after_o = face_values(cells_o, nexts)
    return after_e, after_o


def first_level(line, after_e, after_o, keep_ref, t):
    damp_e, low_e, upp_e, _ = after_e
    damp_o, low_o, upp_o, _ = after_o
    inverse = mat_inv(plus_eye(mat_add(damp_e, damp_o)))
    w_low = mat_mul(inverse, low_e)
    w_upp = mat_mul(inverse, upp_o)
    put_mat(keep_ref, 0, inverse, (t,))
    put_mat(keep_ref, 25, upp_e, (t,))
    put_mat(keep_ref, 50, low_o, (t,))
    put_mat(keep_ref, 75, w_low, (t,))
    put_mat(keep_ref, 100, w_upp, (t,))
    inner = line.inner
    low = mat_map(lambda x, y: jnp.where(inner, -x, y), mat_mul(low_o, w_low), low_e)
    mid_l = mat_map(
        lambda x, y, z: jnp.where(inner, y - x, z), mat_mul(low_o, w_upp), damp_o, damp_e
    )
    upp = mat_map(lambda x, y: jnp.where(inner, -x, y), mat_mul(upp_e, w_upp), upp_e)
    mid_r = mat_map(
        lambda x, y: jnp.where(inner, y - x, y), mat_mul(upp_e, w_low), plus_eye(damp_e)
    )
    return line.mroll(low, 2), line.mroll(mid_l, 2), mid_r, upp


def second_level(line, level_a, level_b, keep_ref):
    packed = [
        [[line.pack2(x, y) for x, y in zip(ra, rb)] for ra, rb in zip(ma, mb)]
        for ma, mb in zip(level_a, level_b)
    ]
    evens = [mat_map(lambda p: p[0], m) for m in packed]
    odds = [mat_map(lambda p: p[1], m) for m in packed]
    inverse = mat_inv(mat_add(odds[1], odds[2]))
    w_low = mat_mul(inverse, odds[0])
    w_upp = mat_mul(inverse, odds[3])
    put_mat(keep_ref, 0, inverse)
    put_mat(keep_ref, 25, evens[3])
    put_mat(keep_ref, 50, evens[0])
    put_mat(keep_ref, 75, w_low)
    put_mat(keep_ref, 100, w_upp)
    left_low = line.mroll(w_low, 4)
    left_upp = line.mroll(w_upp, 4)
    low = mat_neg(mat_mul(evens[0], left_low))
    mid_l = mat_sub(evens[1], mat_mul(evens[0], left_upp))
    mid_r = mat_sub(evens[2], mat_mul(evens[3], w_low))
    upp = mat_neg(mat_mul(evens[3], w_upp))
    return low, mid_l, mid_r, upp


def later_level(line, low, mid_l, mid_r, upp, reach, keep_ref, level):
    left_ok = (line.group > reach) | (line.group == 0)
    right_ok = line.group + reach < line.count
    inverse = mat_inv(mat_add(mid_l, mid_r))
    w_low = mat_mul(inverse, low)
    w_upp = mat_mul(inverse, upp)
    low_in = mat_map(lambda x: jnp.where(left_ok, x, 0.0), low)
    upp_in = mat_map(lambda x: jnp.where(right_ok, x, 0.0), upp)
    put_mat(keep_ref, 0, inverse, (level,))
    put_mat(keep_ref, 25, low_in, (level,))
    put_mat(keep_ref, 50, upp_in, (level,))
    back = 4 * reach
    ahead = line.n - 4 * reach
    left_low, left_upp = line.mroll(w_low, back), line.mroll(w_upp, back)
    right_low, right_upp = line.mroll(w_low, ahead), line.mroll(w_upp, ahead)
    new_low = mat_map(
        lambda x, y: jnp.where(left_ok, -x, y), mat_mul(low_in, left_low), low
    )
    new_mid_l = mat_sub(mid_l, mat_mul(low_in, left_upp))
    new_upp = mat_map(
        lambda x, y: jnp.where(right_ok, -x, y), mat_mul(upp_in, right_upp), upp
    )
    new_mid_r = mat_sub(mid_r, mat_mul(upp_in, right_low))
    return new_low, new_mid_l, new_mid_r, new_upp


def line_levels(line, states, keep1, keep2, keep3, ends, work):
    low, mid_l, mid_r, upp = second_level(line, states[0], states[1], keep2)
    steps = line.count.bit_length() - 1
    if steps == 1:
        low, mid_l, mid_r, upp = later_level(line, low, mid_l, mid_r, upp, 1, keep3, 0)
    else:
        for at, m in enumerate((low, mid_l, mid_r, upp)):
            put_mat(work, 25 * at, m)

        def body(level, carry):
            now = [get_mat(work, 25 * at) for at in range(4)]
            reach = lax.shift_left(jnp.int32(1), level)
            new = later_level(line, *now, reach, keep3, level)
            for at, m in enumerate(new):
                put_mat(work, 25 * at, m)
            return carry

        lax.fori_loop(0, steps, body, 0)
        low, mid_l, mid_r, upp = (get_mat(work, 25 * at) for at in range(4))
    for at, m in enumerate((low, mid_l, mid_r, upp)):
        put_mat(ends, 25 * at, m)
    inverse = mat_inv(mat_add(mid_l, mid_r))
    put_mat(keep3, 0, inverse, (steps,))
    put_mat(keep3, 25, mat_mul(inverse, low), (steps,))
    put_mat(keep3, 50, mat_mul(inverse, upp), (steps,))


def line_forward(line, rhs_e, rhs_o, keep1, keep2, keep3, zs):
    right, left = [], []
    for t in range(2):
        z = mat_vec(get_mat(keep1, 0, (t,)), rhs_o[t])
        put_vec(zs, 5 * t, z)
        from_r = mat_vec(get_mat(keep1, 25, (t,)), z)
        from_l = mat_vec(get_mat(keep1, 50, (t,)), z)
        right.append(
            vec_map(lambda r, x: jnp.where(line.inner, r - x, r), rhs_e[t], from_r)
        )
        left.append(
            line.vroll(vec_map(lambda r, x: jnp.where(line.inner, -x, r), rhs_o[t], from_l), 2)
        )
    pair_r = [line.pack2(x, y) for x, y in zip(right[0], right[1])]
    pair_l = [line.pack2(x, y) for x, y in zip(left[0], left[1])]
    odd = [x[1] + y[1] for x, y in zip(pair_r, pair_l)]
    z = mat_vec(get_mat(keep2, 0), odd)
    put_vec(zs, 10, z)
    r_r = vec_sub([x[0] for x in pair_r], mat_vec(get_mat(keep2, 25), z))
    r_l = vec_sub([x[0] for x in pair_l], mat_vec(get_mat(keep2, 50), line.vroll(z, 4)))
    steps = line.count.bit_length() - 1
    for level in range(steps):
        z = mat_vec(get_mat(keep3, 0, (level,)), vec_add(r_l, r_r))
        back = 4 << level
        r_l = vec_sub(r_l, mat_vec(get_mat(keep3, 25, (level,)), line.vroll(z, back)))
        r_r = vec_sub(r_r, mat_vec(get_mat(keep3, 50, (level,)), line.vroll(z, -back)))
    put_vec(zs, 15, mat_vec(get_mat(keep3, 0, (steps,)), vec_add(r_l, r_r)))
    return r_r, r_l


def line_backward(line, first, last, keep1, keep2, keep3, zs):
    steps = line.count.bit_length() - 1
    inner = vec_sub(
        get_vec(zs, 15),
        vec_add(
            mat_vec(get_mat(keep3, 25, (steps,)), first),
            mat_vec(get_mat(keep3, 50, (steps,)), last),
        ),
    )
    even = vec_map(lambda x, y: jnp.where(line.group == 0, y, x), inner, first)
    ahead = vec_map(
        lambda x, y: jnp.where(line.at >= line.n - 4, y, x), line.vroll(even, -4), last
    )
    odd = vec_sub(
        get_vec(zs, 10),
        vec_add(
            mat_vec(get_mat(keep2, 75), even), mat_vec(get_mat(keep2, 100), ahead)
        ),
    )
    pairs = [line.unpack2(x, y) for x, y in zip(even, odd)]
    out = []
    for t in range(2):
        even = [p[t] for p in pairs]
        ends = line.vroll(last, 2) if t == 0 else last
        ahead = line.vroll(even, -2)
        odd = vec_sub(
            get_vec(zs, 5 * t),
            vec_add(
                mat_vec(get_mat(keep1, 75, (t,)), even),
                mat_vec(get_mat(keep1, 100, (t,)), ahead),
            ),
        )
        odd = vec_map(lambda x, y: jnp.where(line.inner, x, y), odd, ends)
        spans = [line.unpack1(x, y) for x, y in zip(even, odd)]
        out.append([s[0] for s in spans])
        out.append([s[1] for s in spans])
    return out


def halo_kernel(state, metrics, step, spread, up, down):
    for s in range(4):
        for c in range(5):
            up[c, s : s + 1, :] = state[c, s, 7:8, :]
            down[c, s : s + 1, :] = state[c, s, 0:1, :]
        for c in range(2):
            up[5 + c, s : s + 1, :] = metrics[2 + c, s, 7:8, :]
            down[5 + c, s : s + 1, :] = metrics[2 + c, s, 0:1, :]
        up[7, s : s + 1, :] = step[s, 7:8, :]
        up[8, s : s + 1, :] = spread[1, s, 7:8, :]


def load_cells(line, state, metrics, step, spread, t, metric_at, spread_at):
    first, second = 2 * t, 2 * t + 1
    pairs = [(state[c, first], state[c, second]) for c in range(5)]
    pairs += [(metrics[metric_at + c, first], metrics[metric_at + c, second]) for c in range(2)]
    pairs += [(step[first], step[second]), (spread[spread_at, first], spread[spread_at, second])]
    packed = [line.pack1(a, b) for a, b in pairs]
    return [p[0] for p in packed], [p[1] for p in packed]


def line_residual(line, after_e, after_o):
    flux_e, flux_o = after_e[3], after_o[3]
    flux_o = vec_map(lambda x: jnp.where(line.inner, x, 0.0), flux_o)
    return vec_sub(line.vroll(flux_o, 2), flux_e), vec_sub(flux_e, flux_o)


def wrap_kernel(state, metrics, step, spread, keep1, keep2, keep3, rhs, note, ends, work):
    line = Line(1)
    states = []
    note[...] = jnp.zeros_like(note)
    packed = [jnp.zeros(TILE, jnp.float32) for _ in range(4)]
    lane_group = line.group
    for t in range(2):
        cells_e, cells_o = load_cells(line, state, metrics, step, spread, t, 0, 0)
        pick = line.at & 3
        mine = (pick >> 1) == t
        for c in range(9):
            k, g = divmod(100 + c, 32)
            moved = line.roll(cells_o[c], 4 * g + 2 * t - (line.n - 2))
            packed[k] = jnp.where((lane_group == g) & mine, moved, packed[k])
        for c in range(7):
            k, g = divmod(109 + c, 32)
            moved = line.roll(cells_e[c], 4 * g + 2 * t)
            packed[k] = jnp.where((lane_group == g) & mine, moved, packed[k])
        after_e, after_o = line_faces(line, cells_e, cells_o)
        rhs_e, rhs_o = line_residual(line, after_e, after_o)
        put_vec(rhs, 0, rhs_e, (t,))
        put_vec(rhs, 5, rhs_o, (t,))
        states.append(first_level(line, after_e, after_o, keep1, t))
    line_levels(line, states, keep1, keep2, keep3, ends, work)
    for place, at in enumerate((50, 75, 0, 25)):
        for c in range(25):
            k, g = divmod(25 * place + c, 32)
            packed[k] = jnp.where(lane_group == g, line.roll(ends[at + c], 4 * g), packed[k])
    for k in range(4):
        note[k] = packed[k]


def wall_faces_kernel(state, metrics, step, spread, coefs, rhs):
    line = Line(0)
    for t in range(2):
        cells_e, cells_o = load_cells(line, state, metrics, step, spread, t, 2, 1)
        after_e, after_o = line_faces(line, cells_e, cells_o)
        rhs_e, rhs_o = line_residual(line, after_e, after_o)
        for c in range(5):
            a, b = line.unpack1(rhs_e[c], rhs_o[c])
            rhs[2 * t, c] = a
            rhs[2 * t + 1, c] = b
        for half, face in enumerate((after_e, after_o)):
            for which in range(3):
                at = 0
                for i in range(5):
                    for j in range(i, 5):
                        coefs[t, half, 15 * which + at] = face[which][i][j]
                        at += 1


def get_face(ref, lead):
    out = []
    for which in range(3):
        m = [[None] * 5 for _ in range(5)]
        at = 0
        for i in range(5):
            for j in range(i, 5):
                m[i][j] = m[j][i] = ref[lead + (15 * which + at,)]
                at += 1
        out.append(m)
    return out + [None]


def wrap_rhs_kernel(
    below, above, up, down, rhs_wall, rhs_wrap, note, keep1, keep2, keep3, zs, sent, edge
):
    line, wall = Line(1), Line(0)
    left = [jnp.concatenate([below[c], up[c]], axis=0) for c in range(9)]
    right = [jnp.concatenate([down[c], above[c]], axis=0) for c in range(7)]
    face = face_values(left, right)
    for which in range(3):
        at = 0
        for i in range(5):
            for j in range(i, 5):
                edge[15 * which + at] = wall.roll(face[which][i][j], 4)
                at += 1
    flux = face[3]
    rhs_e, rhs_o = [], []
    for t in range(2):
        spans = []
        for s in (2 * t, 2 * t + 1):
            values = []
            for c in range(5):
                x = rhs_wall[s, c]
                x = jnp.where(wall.at == 0, x + wall.roll(flux[c], -s), x)
                x = jnp.where(wall.at == 7, x - wall.roll(flux[c], 3 - s), x)
                values.append(x)
            spans.append(values)
        packed = [line.pack1(a, b) for a, b in zip(*spans)]
        rhs_e.append([packed[c][0] + rhs_wrap[t, c] for c in range(5)])
        rhs_o.append([packed[c][1] + rhs_wrap[t, 5 + c] for c in range(5)])
    r_r, r_l = line_forward(line, rhs_e, rhs_o, keep1, keep2, keep3, zs)
    for k in range(3):
        sent[k] = note[k]
    tail = note[3]
    for c in range(10):
        g = 116 + c - 96
        value = r_r[c] if c < 5 else r_l[c - 5]
        tail = jnp.where(line.group == g, line.roll(value, 4 * g), tail)
    sent[3] = tail


def transpose_blocks(rows, count):
    width = LANES // count
    at = lax.broadcasted_iota(jnp.int32, rows[0].shape, 1)
    block = at // width
    bit = 1
    while bit < count:
        clear = (block & bit) == 0
        new = [None] * count
        for m in range(count):
            if m & bit:
                continue
            a, b = rows[m], rows[m | bit]
            new[m] = jnp.where(clear, a, pltpu.roll(b, bit * width, 1))
            new[m | bit] = jnp.where(clear, pltpu.roll(a, LANES - bit * width, 1), b)
        rows = new
        bit *= 2
    return rows


def wall_kernel(coefs, edge, keep1, keep2, keep3, close, parcel, ends, *, count):
    line = Line(0)
    states = []
    for t in range(2):
        after_e = get_face(coefs, (t, 0))
        after_o = get_face(coefs, (t, 1))
        states.append(first_level(line, after_e, after_o, keep1, t))
    line_levels(line, states, keep1, keep2, keep3, ends, None)
    low, mid_l, mid_r, upp = (get_mat(ends, 25 * at) for at in range(4))
    damp_f, low_f, upp_f, _ = get_face(edge, ())
    inverse = mat_inv(plus_eye(mat_add(mid_l, damp_f)))
    w_low = mat_mul(inverse, low)
    w_upp = mat_mul(inverse, upp_f)
    put_mat(close, 0, inverse)
    put_mat(close, 25, upp)
    put_mat(close, 50, low_f)
    put_mat(close, 75, w_low)
    put_mat(close, 100, w_upp)
    final = [
        mat_sub(mid_r, mat_mul(upp, w_low)),
        mat_neg(mat_mul(upp, w_upp)),
        mat_neg(mat_mul(low_f, w_low)),
        mat_sub(damp_f, mat_mul(low_f, w_upp)),
    ]
    rows = [x[0:4] for m in final for r in m for x in r]
    zero = jnp.zeros((4, LANES), jnp.float32)
    rows += [zero] * (-len(rows) % count)
    for k in range(len(rows) // count):
        out = transpose_blocks(rows[k * count : (k + 1) * count], count)
        for d in range(count):
            parcel[d, k] = out[d]


def cycle_kernel(
    *refs, count, wall_count
):
    notes = refs[:count]
    (keep1, keep2, keep3, zs, wkeep1, wkeep2, wkeep3, close, parcel) = refs[count : count + 9]
    sent, wzs, closed = refs[count + 9 :]
    line = Line(1)
    period = 4 * count
    repeat = line.at % period
    channels = [None] * 126
    for k in range(4):
        rolled = [line.roll(notes[q][k], 4 * q) for q in range(count)]
        for a in range(count):
            which = (line.group - a) % count
            mixed = rolled[0]
            for q in range(1, count):
                mixed = jnp.where(which == q, rolled[q], mixed)
            for c in range(a, 32, count):
                if 32 * k + c < 126:
                    index = (repeat + 4 * c) & (LANES - 1)
                    channels[32 * k + c] = jnp.take_along_axis(mixed, index, axis=1)

    def mat_at(at):
        return [[channels[at + 5 * i + j] for j in range(5)] for i in range(5)]

    mid_r, upp, low, mid_l = (mat_at(25 * i) for i in range(4))
    left = channels[100:109]
    right = line.vroll(channels[109:116], -4)
    r_r, r_l = channels[116:121], channels[121:126]
    damp_f, low_f, upp_f, flux = face_values(left, right)
    inverse = mat_inv(plus_eye(mat_add(mid_l, damp_f)))
    w_low = mat_mul(inverse, low)
    w_upp = mat_mul(inverse, upp_f)
    zb = mat_vec(inverse, vec_sub(r_l, flux))
    mid = mat_add(
        mat_sub(mid_r, mat_mul(upp, w_low)),
        line.mroll(mat_sub(damp_f, mat_mul(low_f, w_upp)), 4),
    )
    ahead = mat_neg(mat_mul(upp, w_upp))
    back = mat_neg(line.mroll(mat_mul(low_f, w_low), 4))
    load = vec_add(
        vec_sub(r_r, mat_vec(upp, zb)), line.vroll(vec_sub(flux, mat_vec(low_f, zb)), 4)
    )
    reach = 1
    while 2 * reach < count:
        inverse = mat_inv(mid)
        wb, wa, z = mat_mul(inverse, back), mat_mul(inverse, ahead), mat_vec(inverse, load)
        by = 4 * reach
        mid = mat_sub(
            mid,
            mat_add(
                mat_mul(back, line.mroll(wa, by)), mat_mul(ahead, line.mroll(wb, -by))
            ),
        )
        load = vec_sub(
            load,
            vec_add(mat_vec(back, line.vroll(z, by)), mat_vec(ahead, line.vroll(z, -by))),
        )
        back, ahead = (
            mat_neg(mat_mul(back, line.mroll(wb, by))),
            mat_neg(mat_mul(ahead, line.mroll(wa, -by))),
        )
        reach *= 2
    both = mat_add(back, ahead)
    inverse = mat_inv(mid)
    w, z = mat_mul(inverse, both), mat_vec(inverse, load)
    by = 4 * reach
    mid = mat_sub(mid, mat_mul(both, line.mroll(w, by)))
    load = vec_sub(load, mat_vec(both, line.vroll(z, by)))
    x = mat_vec(mat_inv(mid), load)
    b = vec_sub(zb, vec_add(mat_vec(w_low, x), mat_vec(w_upp, line.vroll(x, -4))))
    spread = line.at & 3
    first = [jnp.take_along_axis(y, spread, axis=1) for y in x]
    last = [jnp.take_along_axis(y, spread, axis=1) for y in b]
    swept = line_backward(line, first, last, keep1, keep2, keep3, zs)

    wall = Line(0)
    rhs_e, rhs_o = [], []
    for t in range(2):
        packed = [wall.pack1(p, q) for p, q in zip(swept[2 * t], swept[2 * t + 1])]
        rhs_e.append([p[0] for p in packed])
        rhs_o.append([p[1] for p in packed])
    r_r, r_l = line_forward_wall(wall, rhs_e, rhs_o, wkeep1, wkeep2, wkeep3, wzs)
    zb = mat_vec(get_mat(close, 0), r_l)
    put_vec(closed, 0, zb)
    out_r = vec_sub(r_r, mat_vec(get_mat(close, 25), zb))
    out_l = vec_map(lambda y: -y, mat_vec(get_mat(close, 50), zb))
    rows = [y[0:4] for y in out_r + out_l]
    zero = jnp.zeros((4, LANES), jnp.float32)
    rows += [zero] * (-len(rows) % wall_count)
    base = parcel.shape[1]
    for k in range(base):
        for d in range(wall_count):
            sent[d, k] = parcel[d, k]
    for k in range(len(rows) // wall_count):
        out = transpose_blocks(rows[k * wall_count : (k + 1) * wall_count], wall_count)
        for d in range(wall_count):
            sent[d, base + k] = out[d]


def line_forward_wall(wall, rhs_e, rhs_o, keep1, keep2, keep3, zs):
    return line_forward(wall, rhs_e, rhs_o, keep1, keep2, keep3, zs)


def open_kernel(got, reply, *, count):
    width = LANES // count
    base = -(-100 // count)

    def unpack(k):
        return transpose_blocks([got[q, k] for q in range(count)], count)

    flat = [x for k in range(base) for x in unpack(k)][:100]
    tail = [x for k in range(base, got.shape[1]) for x in unpack(k)][:10]

    def mat_at(at):
        return [[flat[at + 5 * i + j] for j in range(5)] for i in range(5)]

    mid_r, upp, low, mid_l = (mat_at(25 * i) for i in range(4))
    at = lax.broadcasted_iota(jnp.int32, (4, LANES), 1)
    not_first = at >= width
    not_last = at < LANES - width

    def shift(x, by):
        return pltpu.roll(x, by % LANES, 1)

    def from_back(x):
        return jnp.where(not_first, shift(x, width), 0.0)

    mid = mat_add(mid_r, mat_map(from_back, mid_l))
    back = mat_map(from_back, low)
    ahead = mat_map(lambda x: jnp.where(not_last, x, 0.0), upp)
    load = vec_add(tail[0:5], vec_map(from_back, tail[5:10]))
    reach = 1
    while reach < count:
        by = width * reach
        inverse = mat_inv(mid)
        wb, wa, z = mat_mul(inverse, back), mat_mul(inverse, ahead), mat_vec(inverse, load)
        behind = lambda m: mat_map(lambda x: shift(x, by), m)
        beyond = lambda m: mat_map(lambda x: shift(x, -by), m)
        mid = mat_sub(mid, mat_add(mat_mul(back, behind(wa)), mat_mul(ahead, beyond(wb))))
        load = vec_sub(
            load,
            vec_add(
                mat_vec(back, [shift(x, by) for x in z]),
                mat_vec(ahead, [shift(x, -by) for x in z]),
            ),
        )
        if 2 * reach < count:
            back, ahead = (
                mat_neg(mat_mul(back, behind(wb))),
                mat_neg(mat_mul(ahead, beyond(wa))),
            )
        reach *= 2
    x = mat_vec(mat_inv(mid), load)
    nexts = [jnp.where(not_last, shift(y, -width), 0.0) for y in x]
    rows = x + nexts
    rows += [jnp.zeros((4, LANES), jnp.float32)] * (-len(rows) % count)
    for k in range(len(rows) // count):
        out = transpose_blocks(rows[k * count : (k + 1) * count], count)
        for d in range(count):
            reply[d, k] = out[d]


def finish_kernel(got, keep1, keep2, keep3, close, closed, zs, field, *, count):
    line = Line(0)
    rows = [
        x
        for k in range(got.shape[1])
        for x in transpose_blocks([got[q, k] for q in range(count)], count)
    ]
    twice = [jnp.concatenate([x, x], axis=0) for x in rows[:10]]
    first, nexts = twice[0:5], twice[5:10]
    last = vec_sub(
        get_vec(closed, 0),
        vec_add(mat_vec(get_mat(close, 75), first), mat_vec(get_mat(close, 100), nexts)),
    )
    last = [jnp.where(line.at < 4, x, line.roll(x, 4)) for x in last]
    out = line_backward(line, first, last, keep1, keep2, keep3, zs)
    for s in range(4):
        for c in range(5):
            field[c, s] = out[s][c]


def call(kernel, name, shapes, flops, *args, scratch=()):
    spec = pl.BlockSpec(memory_space=pltpu.VMEM)
    return pl.pallas_call(
        kernel,
        name=name,
        out_shape=[jax.ShapeDtypeStruct(s, jnp.float32) for s in shapes],
        in_specs=[spec] * len(args),
        out_specs=[spec] * len(shapes),
        scratch_shapes=[pltpu.VMEM(s, jnp.float32) for s in scratch],
        compiler_params=pltpu.CompilerParams(vmem_limit_bytes=VMEM_LIMIT),
        cost_estimate=pl.CostEstimate(flops=flops, bytes_accessed=1 << 20, transcendentals=0),
    )(*args)


def on_device(state, metrics, time_step, dissipation, *, wrap_count, wall_count):
    inputs = (state, metrics, time_step, dissipation)
    up, down = call(
        halo_kernel, "halo", [(9, 4, LANES), (7, 4, LANES)], 1 << 12, *inputs
    )
    rises = [(i, i + 1) for i in range(wall_count - 1)]
    falls = [(i + 1, i) for i in range(wall_count - 1)]
    below = lax.ppermute(up, "normal", rises)
    above = lax.ppermute(down, "normal", falls)
    keep1, keep2, keep3, rhs_wrap, note = call(
        wrap_kernel,
        "wrap",
        [(2, 125) + TILE, (125,) + TILE, (6, 75) + TILE, (2, 10) + TILE, (4,) + TILE],
        40 << 20,
        *inputs,
        scratch=[(100,) + TILE, (100,) + TILE],
    )
    coefs, rhs_wall = call(
        wall_faces_kernel,
        "wall_faces",
        [(2, 2, 45) + TILE, (4, 5) + TILE],
        8 << 20,
        *inputs,
    )
    zs, own, edge = call(
        wrap_rhs_kernel,
        "wrap_rhs",
        [(20,) + TILE, (4,) + TILE, (45,) + TILE],
        8 << 20,
        below,
        above,
        up,
        down,
        rhs_wall,
        rhs_wrap,
        note,
        keep1,
        keep2,
        keep3,
    )
    notes = [own]
    for by in range(1, wrap_count):
        pairs = [((i + by) % wrap_count, i) for i in range(wrap_count)]
        notes.append(lax.ppermute(own, "wrap", pairs))
    groups = -(-100 // wall_count)
    tails = -(-10 // wall_count)
    wkeep1, wkeep2, wkeep3, close, parcel = call(
        lambda *refs: wall_kernel(*refs, count=wall_count),
        "wall",
        [
            (2, 125) + TILE,
            (125,) + TILE,
            (2, 75) + TILE,
            (125,) + TILE,
            (wall_count, groups, 4, LANES),
        ],
        20 << 20,
        coefs,
        edge,
        scratch=[(100,) + TILE],
    )
    sent, wzs, closed = call(
        lambda *refs: cycle_kernel(*refs, count=wrap_count, wall_count=wall_count),
        "cycle",
        [(wall_count, groups + tails, 4, LANES), (20,) + TILE, (5,) + TILE],
        10 << 20,
        *notes,
        keep1,
        keep2,
        keep3,
        zs,
        wkeep1,
        wkeep2,
        wkeep3,
        close,
        parcel,
    )
    got = lax.all_to_all(sent, "normal", 0, 0)
    (reply,) = call(
        lambda *refs: open_kernel(*refs, count=wall_count),
        "open",
        [(wall_count, tails, 4, LANES)],
        10 << 20,
        got,
    )
    answer = lax.all_to_all(reply, "normal", 0, 0)
    (field,) = call(
        lambda *refs: finish_kernel(*refs, count=wall_count),
        "finish",
        [(5, 4) + TILE],
        4 << 20,
        answer,
        wkeep1,
        wkeep2,
        wkeep3,
        close,
        closed,
        wzs,
    )
    return field


def solution(mesh):
    placed = (
        P(None, None, "normal", "wrap"),
        P(None, None, "normal", "wrap"),
        P(None, "normal", "wrap"),
        P(None, None, "normal", "wrap"),
    )

    def body(state, metrics, time_step, dissipation):
        return on_device(
            state,
            metrics,
            time_step,
            dissipation,
            wrap_count=mesh.shape["wrap"],
            wall_count=mesh.shape["normal"],
        )

    return jax.shard_map(
        body,
        mesh=mesh,
        in_specs=placed,
        out_specs=P(None, None, "normal", "wrap"),
        check_vma=False,
    )
```

```python
import jax
import jax.numpy as jnp
from jax import lax
from jax.experimental import pallas as pl
from jax.experimental.pallas import tpu as pltpu
from jax.sharding import PartitionSpec as P

GAMMA = 1.4
LESS = GAMMA - 1.0
VMEM_LIMIT = 16 * 1024 * 1024
TILE = (8, 128)
LANES = 128


def mat_mul(a, b):
    out = []
    for i in range(5):
        row = []
        for j in range(5):
            total = a[i][0] * b[0][j]
            for k in range(1, 5):
                total = total + a[i][k] * b[k][j]
            row.append(total)
        out.append(row)
    return out


def mat_vec(a, x):
    out = []
    for i in range(5):
        total = a[i][0] * x[0]
        for k in range(1, 5):
            total = total + a[i][k] * x[k]
        out.append(total)
    return out


def mat_map(fn, *mats):
    return [[fn(*(m[i][j] for m in mats)) for j in range(5)] for i in range(5)]


def vec_map(fn, *vecs):
    return [fn(*(v[i] for v in vecs)) for i in range(5)]


def mat_add(a, b):
    return mat_map(lambda x, y: x + y, a, b)


def mat_sub(a, b):
    return mat_map(lambda x, y: x - y, a, b)


def mat_neg(a):
    return mat_map(lambda x: -x, a)


def vec_add(a, b):
    return vec_map(lambda x, y: x + y, a, b)


def vec_sub(a, b):
    return vec_map(lambda x, y: x - y, a, b)


def plus_eye(a):
    return [[a[i][j] + 1.0 if i == j else a[i][j] for j in range(5)] for i in range(5)]


def mat_inv(matrix):
    a = [list(row) for row in matrix]
    for k in range(5):
        pivot = 1.0 / a[k][k]
        row = [a[k][j] * pivot if j != k else pivot for j in range(5)]
        for i in range(5):
            if i == k:
                continue
            factor = a[i][k]
            for j in range(5):
                a[i][j] = -(factor * pivot) if j == k else a[i][j] - factor * row[j]
        a[k] = row
    return a


def face_values(left, right):
    state = [0.5 * (left[i] + right[i]) for i in range(5)]
    m1 = 0.5 * (left[5] + right[5])
    m2 = 0.5 * (left[6] + right[6])
    step, spread = left[7], left[8]
    over = 1.0 / state[0]
    u, v, w, e = (state[i] * over for i in range(1, 5))
    t = m1 * u + m2 * v
    f = (0.5 * LESS) * (u * u + v * v + w * w)
    h = GAMMA * e - f
    jac = [
        [None, m1, m2, None, None],
        [
            m1 * f - u * t,
            t - (GAMMA - 2.0) * m1 * u,
            m2 * u - LESS * m1 * v,
            -LESS * m1 * w,
            LESS * m1,
        ],
        [
            m2 * f - v * t,
            m1 * v - LESS * m2 * u,
            t - (GAMMA - 2.0) * m2 * v,
            -LESS * m2 * w,
            LESS * m2,
        ],
        [-w * t, m1 * w, m2 * w, t, None],
        [
            t * (2.0 * f - GAMMA * e),
            m1 * h - LESS * u * t,
            m2 * h - LESS * v * t,
            -LESS * w * t,
            GAMMA * t,
        ],
    ]
    widest = None
    for row in jac:
        total = None
        for x in row:
            if x is not None:
                total = jnp.abs(x) if total is None else total + jnp.abs(x)
        widest = total if widest is None else jnp.maximum(widest, total)
    scale = 1.0 / widest
    norm = [[None if x is None else x * scale for x in row] for row in jac]
    half_step = 0.5 * step
    weight = half_step * spread
    convect = [[None] * 5 for _ in range(5)]
    damping = [[None] * 5 for _ in range(5)]
    for i in range(5):
        for j in range(i, 5):
            parts = [x for x in (norm[i][j], norm[j][i]) if x is not None]
            if parts:
                c = half_step * (parts[0] + parts[1] if len(parts) == 2 else parts[0])
            else:
                c = jnp.zeros_like(step)
            total = None
            for k in range(5):
                if norm[k][i] is None or norm[k][j] is None:
                    continue
                term = norm[k][i] * norm[k][j]
                total = term if total is None else total + term
            if i == j:
                total = total + 1.0
            d = weight * total
            convect[i][j] = convect[j][i] = c
            damping[i][j] = damping[j][i] = d
    jump = [right[i] - left[i] for i in range(5)]
    flux = vec_sub(mat_vec(convect, state), mat_vec(damping, jump))
    lower = mat_map(lambda c, d: -0.5 * c - d, convect, damping)
    upper = mat_map(lambda c, d: 0.5 * c - d, convect, damping)
    for i in range(5):
        for j in range(i):
            lower[i][j] = lower[j][i]
            upper[i][j] = upper[j][i]
    return damping, lower, upper, flux


def put_mat(ref, at, a, lead=()):
    for i in range(5):
        for j in range(5):
            ref[lead + (at + 5 * i + j,)] = a[i][j]


def get_mat(ref, at, lead=()):
    return [[ref[lead + (at + 5 * i + j,)] for j in range(5)] for i in range(5)]


def put_vec(ref, at, x, lead=()):
    for i in range(5):
        ref[lead + (at + i,)] = x[i]


def get_vec(ref, at, lead=()):
    return [ref[lead + (at + i,)] for i in range(5)]


class Line:
    def __init__(self, dim):
        self.dim = dim
        self.n = TILE[dim]
        self.count = self.n // 4
        self.at = lax.broadcasted_iota(jnp.int32, TILE, dim)
        self.even1 = (self.at & 1) == 0
        self.even2 = (self.at & 2) == 0
        self.inner = self.at < self.n - 2
        self.group = self.at >> 2

    def roll(self, x, by):
        if isinstance(by, int):
            by = by % self.n
            if by == 0:
                return x
        return pltpu.roll(x, by, self.dim)

    def vroll(self, v, by):
        return [self.roll(x, by) for x in v]

    def mroll(self, m, by):
        return [self.vroll(row, by) for row in m]

    def pack1(self, a, b):
        first = jnp.where(self.even1, a, self.roll(b, 1))
        second = jnp.where(self.even1, self.roll(a, -1), b)
        return first, second

    def unpack1(self, first, second):
        a = jnp.where(self.even1, first, self.roll(second, 1))
        b = jnp.where(self.even1, self.roll(first, -1), second)
        return a, b

    def pack2(self, a, b):
        first = jnp.where(self.even2, a, self.roll(b, 2))
        second = jnp.where(self.even2, self.roll(a, -2), b)
        return first, second

    def unpack2(self, first, second):
        a = jnp.where(self.even2, first, self.roll(second, 2))
        b = jnp.where(self.even2, self.roll(first, -2), second)
        return a, b


def line_faces(line, cells_e, cells_o):
    after_e = face_values(cells_e, cells_o)
    nexts = [line.roll(x, -2) for x in cells_e[:7]]
    after_o = face_values(cells_o, nexts)
    return after_e, after_o


def first_level(line, after_e, after_o, keep_ref, t):
    damp_e, low_e, upp_e, _ = after_e
    damp_o, low_o, upp_o, _ = after_o
    inverse = mat_inv(plus_eye(mat_add(damp_e, damp_o)))
    w_low = mat_mul(inverse, low_e)
    w_upp = mat_mul(inverse, upp_o)
    put_mat(keep_ref, 0, inverse, (t,))
    put_mat(keep_ref, 25, upp_e, (t,))
    put_mat(keep_ref, 50, low_o, (t,))
    put_mat(keep_ref, 75, w_low, (t,))
    put_mat(keep_ref, 100, w_upp, (t,))
    inner = line.inner
    low = mat_map(lambda x, y: jnp.where(inner, -x, y), mat_mul(low_o, w_low), low_e)
    mid_l = mat_map(
        lambda x, y, z: jnp.where(inner, y - x, z), mat_mul(low_o, w_upp), damp_o, damp_e
    )
    upp = mat_map(lambda x, y: jnp.where(inner, -x, y), mat_mul(upp_e, w_upp), upp_e)
    mid_r = mat_map(
        lambda x, y: jnp.where(inner, y - x, y), mat_mul(upp_e, w_low), plus_eye(damp_e)
    )
    return line.mroll(low, 2), line.mroll(mid_l, 2), mid_r, upp


def second_level(line, level_a, level_b, keep_ref):
    packed = [
        [[line.pack2(x, y) for x, y in zip(ra, rb)] for ra, rb in zip(ma, mb)]
        for ma, mb in zip(level_a, level_b)
    ]
    evens = [mat_map(lambda p: p[0], m) for m in packed]
    odds = [mat_map(lambda p: p[1], m) for m in packed]
    inverse = mat_inv(mat_add(odds[1], odds[2]))
    w_low = mat_mul(inverse, odds[0])
    w_upp = mat_mul(inverse, odds[3])
    put_mat(keep_ref, 0, inverse)
    put_mat(keep_ref, 25, evens[3])
    put_mat(keep_ref, 50, evens[0])
    put_mat(keep_ref, 75, w_low)
    put_mat(keep_ref, 100, w_upp)
    left_low = line.mroll(w_low, 4)
    left_upp = line.mroll(w_upp, 4)
    low = mat_neg(mat_mul(evens[0], left_low))
    mid_l = mat_sub(evens[1], mat_mul(evens[0], left_upp))
    mid_r = mat_sub(evens[2], mat_mul(evens[3], w_low))
    upp = mat_neg(mat_mul(evens[3], w_upp))
    return low, mid_l, mid_r, upp


def later_level(line, low, mid_l, mid_r, upp, reach, keep_ref, level):
    left_ok = (line.group > reach) | (line.group == 0)
    right_ok = line.group + reach < line.count
    inverse = mat_inv(mat_add(mid_l, mid_r))
    w_low = mat_mul(inverse, low)
    w_upp = mat_mul(inverse, upp)
    low_in = mat_map(lambda x: jnp.where(left_ok, x, 0.0), low)
    upp_in = mat_map(lambda x: jnp.where(right_ok, x, 0.0), upp)
    put_mat(keep_ref, 0, inverse, (level,))
    put_mat(keep_ref, 25, low_in, (level,))
    put_mat(keep_ref, 50, upp_in, (level,))
    back = 4 * reach
    ahead = line.n - 4 * reach
    left_low, left_upp = line.mroll(w_low, back), line.mroll(w_upp, back)
    right_low, right_upp = line.mroll(w_low, ahead), line.mroll(w_upp, ahead)
    new_low = mat_map(
        lambda x, y: jnp.where(left_ok, -x, y), mat_mul(low_in, left_low), low
    )
    new_mid_l = mat_sub(mid_l, mat_mul(low_in, left_upp))
    new_upp = mat_map(
        lambda x, y: jnp.where(right_ok, -x, y), mat_mul(upp_in, right_upp), upp
    )
    new_mid_r = mat_sub(mid_r, mat_mul(upp_in, right_low))
    return new_low, new_mid_l, new_mid_r, new_upp


def line_levels(line, states, keep1, keep2, keep3, ends, work):
    low, mid_l, mid_r, upp = second_level(line, states[0], states[1], keep2)
    steps = line.count.bit_length() - 1
    if steps == 1:
        low, mid_l, mid_r, upp = later_level(line, low, mid_l, mid_r, upp, 1, keep3, 0)
    else:
        for at, m in enumerate((low, mid_l, mid_r, upp)):
            put_mat(work, 25 * at, m)

        def body(level, carry):
            now = [get_mat(work, 25 * at) for at in range(4)]
            reach = lax.shift_left(jnp.int32(1), level)
            new = later_level(line, *now, reach, keep3, level)
            for at, m in enumerate(new):
                put_mat(work, 25 * at, m)
            return carry

        lax.fori_loop(0, steps, body, 0)
        low, mid_l, mid_r, upp = (get_mat(work, 25 * at) for at in range(4))
    for at, m in enumerate((low, mid_l, mid_r, upp)):
        put_mat(ends, 25 * at, m)


def line_forward(line, rhs_e, rhs_o, keep1, keep2, keep3, zs):
    right, left = [], []
    for t in range(2):
        z = mat_vec(get_mat(keep1, 0, (t,)), rhs_o[t])
        put_vec(zs, 5 * t, z)
        from_r = mat_vec(get_mat(keep1, 25, (t,)), z)
        from_l = mat_vec(get_mat(keep1, 50, (t,)), z)
        right.append(
            vec_map(lambda r, x: jnp.where(line.inner, r - x, r), rhs_e[t], from_r)
        )
        left.append(
            line.vroll(vec_map(lambda r, x: jnp.where(line.inner, -x, r), rhs_o[t], from_l), 2)
        )
    pair_r = [line.pack2(x, y) for x, y in zip(right[0], right[1])]
    pair_l = [line.pack2(x, y) for x, y in zip(left[0], left[1])]
    odd = [x[1] + y[1] for x, y in zip(pair_r, pair_l)]
    z = mat_vec(get_mat(keep2, 0), odd)
    put_vec(zs, 10, z)
    r_r = vec_sub([x[0] for x in pair_r], mat_vec(get_mat(keep2, 25), z))
    r_l = vec_sub([x[0] for x in pair_l], mat_vec(get_mat(keep2, 50), line.vroll(z, 4)))
    steps = line.count.bit_length() - 1
    for level in range(steps):
        z = mat_vec(get_mat(keep3, 0, (level,)), vec_add(r_l, r_r))
        back = 4 << level
        r_l = vec_sub(r_l, mat_vec(get_mat(keep3, 25, (level,)), line.vroll(z, back)))
        r_r = vec_sub(r_r, mat_vec(get_mat(keep3, 50, (level,)), line.vroll(z, -back)))
    put_vec(zs, 15, vec_add(r_l, r_r))
    return r_r, r_l


def line_backward(line, first, last, keep1, keep2, tail, zs):
    inner = vec_sub(
        mat_vec(get_mat(tail, 0), get_vec(zs, 15)),
        vec_add(mat_vec(get_mat(tail, 25), first), mat_vec(get_mat(tail, 50), last)),
    )
    even = vec_map(lambda x, y: jnp.where(line.group == 0, y, x), inner, first)
    ahead = vec_map(
        lambda x, y: jnp.where(line.at >= line.n - 4, y, x), line.vroll(even, -4), last
    )
    odd = vec_sub(
        get_vec(zs, 10),
        vec_add(
            mat_vec(get_mat(keep2, 75), even), mat_vec(get_mat(keep2, 100), ahead)
        ),
    )
    pairs = [line.unpack2(x, y) for x, y in zip(even, odd)]
    out = []
    for t in range(2):
        even = [p[t] for p in pairs]
        ends = line.vroll(last, 2) if t == 0 else last
        ahead = line.vroll(even, -2)
        odd = vec_sub(
            get_vec(zs, 5 * t),
            vec_add(
                mat_vec(get_mat(keep1, 75, (t,)), even),
                mat_vec(get_mat(keep1, 100, (t,)), ahead),
            ),
        )
        odd = vec_map(lambda x, y: jnp.where(line.inner, x, y), odd, ends)
        spans = [line.unpack1(x, y) for x, y in zip(even, odd)]
        out.append([s[0] for s in spans])
        out.append([s[1] for s in spans])
    return out


def tails_kernel(ends_wrap, ends_wall, after, tail_wrap, tail_wall):
    for ends, tail in ((ends_wrap, tail_wrap), (ends_wall, tail_wall)):
        low, mid_l, mid_r, upp = (get_mat(ends, 25 * at) for at in range(4))
        inverse = mat_inv(mat_add(mid_l, mid_r))
        put_mat(tail, 0, inverse)
        put_mat(tail, 25, mat_mul(inverse, low))
        put_mat(tail, 50, mat_mul(inverse, upp))


def odd_device(axis):
    return (lax.axis_index(axis) & 1) == 1


def either(flag, a, b):
    return jnp.where(flag, a, b)


def split_cells(cells):
    return cells.at[0:5], cells.at[5:9], cells.at[9], cells.at[10:12]


def enter_kernel(cells, pair, cross):
    state, metrics, step, spread = split_cells(cells)
    odd = odd_device("normal")

    def send(c, s, rows):
        first, last = rows(0), rows(7)
        pair[c, s : s + 1, :] = either(odd, first, last)
        cross[c, s : s + 1, :] = either(odd, last, first)

    for s in range(4):
        for c in range(5):
            send(c, s, lambda k: state[c, s, k : k + 1, :])
        for c in range(2):
            send(5 + c, s, lambda k: metrics[2 + c, s, k : k + 1, :])
        send(7, s, lambda k: step[s, k : k + 1, :])
        send(8, s, lambda k: spread[1, s, k : k + 1, :])


def load_cells(line, state, metrics, step, spread, t, metric_at, spread_at):
    first, second = 2 * t, 2 * t + 1
    pairs = [(state[c, first], state[c, second]) for c in range(5)]
    pairs += [(metrics[metric_at + c, first], metrics[metric_at + c, second]) for c in range(2)]
    pairs += [(step[first], step[second]), (spread[spread_at, first], spread[spread_at, second])]
    packed = [line.pack1(a, b) for a, b in pairs]
    return [p[0] for p in packed], [p[1] for p in packed]


def line_residual(line, after_e, after_o):
    flux_e, flux_o = after_e[3], after_o[3]
    flux_o = vec_map(lambda x: jnp.where(line.inner, x, 0.0), flux_o)
    return vec_sub(line.vroll(flux_o, 2), flux_e), vec_sub(flux_e, flux_o)


def wrap_kernel(cells, keep1, keep2, keep3, rhs, note, ends, work):
    state, metrics, step, spread = split_cells(cells)
    line = Line(1)
    states = []
    note[...] = jnp.zeros_like(note)
    packed = [jnp.zeros(TILE, jnp.float32) for _ in range(4)]
    lane_group = line.group
    for t in range(2):
        cells_e, cells_o = load_cells(line, state, metrics, step, spread, t, 0, 0)
        pick = line.at & 3
        mine = (pick >> 1) == t
        for c in range(9):
            k, g = divmod(100 + c, 32)
            moved = line.roll(cells_o[c], 4 * g + 2 * t - (line.n - 2))
            packed[k] = jnp.where((lane_group == g) & mine, moved, packed[k])
        for c in range(7):
            k, g = divmod(109 + c, 32)
            moved = line.roll(cells_e[c], 4 * g + 2 * t)
            packed[k] = jnp.where((lane_group == g) & mine, moved, packed[k])
        after_e, after_o = line_faces(line, cells_e, cells_o)
        rhs_e, rhs_o = line_residual(line, after_e, after_o)
        put_vec(rhs, 0, rhs_e, (t,))
        put_vec(rhs, 5, rhs_o, (t,))
        states.append(first_level(line, after_e, after_o, keep1, t))
    line_levels(line, states, keep1, keep2, keep3, ends, work)
    for place, at in enumerate((50, 75, 0, 25)):
        for c in range(25):
            k, g = divmod(25 * place + c, 32)
            packed[k] = jnp.where(lane_group == g, line.roll(ends[at + c], 4 * g), packed[k])
    for k in range(4):
        note[k] = packed[k]


def wall_kernel(cells, keep1, keep2, keep3, rhs, ends):
    state, metrics, step, spread = split_cells(cells)
    line = Line(0)
    states = []
    for t in range(2):
        cells_e, cells_o = load_cells(line, state, metrics, step, spread, t, 2, 1)
        after_e, after_o = line_faces(line, cells_e, cells_o)
        rhs_e, rhs_o = line_residual(line, after_e, after_o)
        for c in range(5):
            a, b = line.unpack1(rhs_e[c], rhs_o[c])
            rhs[2 * t, c] = a
            rhs[2 * t + 1, c] = b
        states.append(first_level(line, after_e, after_o, keep1, t))
    line_levels(line, states, keep1, keep2, keep3, ends, None)


def close_kernel(pair, cross, from_pair, from_cross, ends, after, flux, close, segment):
    odd = odd_device("normal")
    left, right = [], []
    for c in range(9):
        below = either(odd, from_pair[c], from_cross[c])
        own = either(odd, cross[c], pair[c])
        left.append(jnp.concatenate([below, own], axis=0))
    for c in range(7):
        above = either(odd, from_cross[c], from_pair[c])
        own = either(odd, pair[c], cross[c])
        right.append(jnp.concatenate([own, above], axis=0))
    damp, lower, upper, through = face_values(left, right)
    put_vec(flux, 0, through)
    wall = Line(0)
    damp_f, low_f, upp_f = (
        mat_map(lambda x: wall.roll(x, 4), m) for m in (damp, lower, upper)
    )
    low, mid_l, mid_r, upp = (get_mat(ends, 25 * at) for at in range(4))
    inverse = mat_inv(plus_eye(mat_add(mid_l, damp_f)))
    w_low = mat_mul(inverse, low)
    w_upp = mat_mul(inverse, upp_f)
    put_mat(close, 0, inverse)
    put_mat(close, 25, upp)
    put_mat(close, 50, low_f)
    put_mat(close, 75, w_low)
    put_mat(close, 100, w_upp)
    mid_r = mat_sub(mid_r, mat_mul(upp, w_low))
    upp = mat_neg(mat_mul(upp, w_upp))
    low = mat_neg(mat_mul(low_f, w_low))
    mid_l = mat_sub(damp_f, mat_mul(low_f, w_upp))
    for at, m in enumerate((mid_r, upp, low, mid_l)):
        put_mat(segment, 25 * at, mat_map(lambda x: x[0:4], m))


def segment_mats(ref):
    return [get_mat(ref, 25 * at) for at in range(4)]


def tree_bit(level):
    return ((lax.axis_index("normal") >> level) & 1) == 1


def tree_nodes(level):
    nodes = []
    for at in range(level):
        nodes = [(at, 0)] + nodes + [(i, k + (1 << at)) for i, k in nodes]
    return nodes


def merge_kernel(own, other, after, node, message, *extra, level, shared, last):
    upside = tree_bit(level)
    mine, theirs = segment_mats(own), segment_mats(other)
    lower = [mat_map(lambda a, b: either(upside, b, a), m, t) for m, t in zip(mine, theirs)]
    upper = [mat_map(lambda a, b: either(upside, a, b), m, t) for m, t in zip(mine, theirs)]
    inverse = mat_inv(mat_add(lower[3], upper[0]))
    w_low = mat_mul(inverse, lower[2])
    up_in = mat_mul(lower[1], inverse)
    low_in = mat_mul(upper[2], inverse)
    w_upp = mat_mul(inverse, upper[1])
    for at, m in enumerate((inverse, up_in, low_in, w_low, w_upp)):
        put_mat(node, 25 * at, m)
    mid_r = mat_sub(lower[0], mat_mul(lower[1], w_low))
    upp = mat_neg(mat_mul(lower[1], w_upp))
    low = mat_neg(mat_mul(upper[2], w_low))
    mid_l = mat_sub(upper[3], mat_mul(upper[2], w_upp))
    at = 100
    if last:
        top = tree_bit(level + 1)
        first = mat_inv(mid_r)
        through = mat_map(lambda x: either(top, 0.0, x), mat_mul(low, first))
        core = mat_map(
            lambda a, b: either(top, a, b), mid_r, mat_sub(mid_l, mat_mul(through, upp))
        )
        put_mat(extra[0], 0, core)
        put_mat(extra[0], 25, through)
        put_mat(extra[0], 50, first)
        put_mat(extra[0], 75, upp)
        put_mat(message, 0, core)
        put_mat(message, 25, through)
        put_mat(
            message,
            50,
            mat_map(
                lambda a, b: either(top, a, b), up_in, mat_sub(low_in, mat_mul(through, up_in))
            ),
        )
        at = 75
    else:
        for i, m in enumerate((mid_r, upp, low, mid_l)):
            put_mat(message, 25 * i, m)
        if shared is not None:
            put_mat(message, at, up_in)
            put_mat(message, at + 25, low_in)
            at += 50
    for source in (own, other):
        for c in range(50 * (shared or 0)):
            message[at] = source[100 + c]
            at += 1


def middle_kernel(own, other, inverse):
    put_mat(inverse, 0, mat_inv(mat_add(get_mat(own, 0), get_mat(other, 0))))


def merge_loads(upside, up_in, low_in, mine, theirs):
    lower = [vec_map(lambda a, b: either(upside, b, a), m, t) for m, t in zip(mine, theirs)]
    upper = [vec_map(lambda a, b: either(upside, a, b), m, t) for m, t in zip(mine, theirs)]
    load = vec_add(lower[1], upper[0])
    right = vec_sub(lower[0], mat_vec(up_in, load))
    left = vec_sub(upper[1], mat_vec(low_in, load))
    return load, (right, left)


def in_order(position, count):
    def pick(values, q):
        ks = sorted({c ^ ((c + q) % count) for c in range(count)})
        wanted = position ^ ((position + q) % count)
        out = values[ks[0]]
        for k in ks[1:]:
            out = jnp.where(wanted == k, values[k], out)
        return out

    return pick


def wrap_rhs_kernel(flux, rhs_wall, rhs_wrap, note, keep1, keep2, keep3, zs, sent):
    line, wall = Line(1), Line(0)
    through = get_vec(flux, 0)
    rhs_e, rhs_o = [], []
    for t in range(2):
        spans = []
        for s in (2 * t, 2 * t + 1):
            values = []
            for c in range(5):
                x = rhs_wall[s, c]
                x = jnp.where(wall.at == 0, x + wall.roll(through[c], -s), x)
                x = jnp.where(wall.at == 7, x - wall.roll(through[c], 3 - s), x)
                values.append(x)
            spans.append(values)
        packed = [line.pack1(a, b) for a, b in zip(*spans)]
        rhs_e.append([packed[c][0] + rhs_wrap[t, c] for c in range(5)])
        rhs_o.append([packed[c][1] + rhs_wrap[t, 5 + c] for c in range(5)])
    r_r, r_l = line_forward(line, rhs_e, rhs_o, keep1, keep2, keep3, zs)
    for k in range(3):
        sent[k] = note[k]
    tail = note[3]
    for c in range(10):
        g = 116 + c - 96
        value = r_r[c] if c < 5 else r_l[c - 5]
        tail = jnp.where(line.group == g, line.roll(value, 4 * g), tail)
    sent[3] = tail


def cycle_kernel(*refs, count):
    arrived = refs[:count]
    (keep1, keep2, tail, zs, wkeep1, wkeep2, wkeep3, close) = refs[count : count + 8]
    sent, wzs, closed = refs[count + 8 :]
    pick = in_order(lax.axis_index("wrap"), count)
    notes = [
        [pick([ref[k] for ref in arrived], q) for k in range(4)] for q in range(count)
    ]
    line = Line(1)
    period = 4 * count
    repeat = line.at % period
    channels = [None] * 126
    for k in range(4):
        rolled = [line.roll(notes[q][k], 4 * q) for q in range(count)]
        for a in range(count):
            which = (line.group - a) % count
            mixed = rolled[0]
            for q in range(1, count):
                mixed = jnp.where(which == q, rolled[q], mixed)
            for c in range(a, 32, count):
                if 32 * k + c < 126:
                    index = (repeat + 4 * c) & (LANES - 1)
                    channels[32 * k + c] = jnp.take_along_axis(mixed, index, axis=1)

    def mat_at(at):
        return [[channels[at + 5 * i + j] for j in range(5)] for i in range(5)]

    mid_r, upp, low, mid_l = (mat_at(25 * i) for i in range(4))
    left = channels[100:109]
    right = line.vroll(channels[109:116], -4)
    r_r, r_l = channels[116:121], channels[121:126]
    damp_f, low_f, upp_f, flux = face_values(left, right)
    inverse = mat_inv(plus_eye(mat_add(mid_l, damp_f)))
    w_low = mat_mul(inverse, low)
    w_upp = mat_mul(inverse, upp_f)
    zb = mat_vec(inverse, vec_sub(r_l, flux))
    mid = mat_add(
        mat_sub(mid_r, mat_mul(upp, w_low)),
        line.mroll(mat_sub(damp_f, mat_mul(low_f, w_upp)), 4),
    )
    ahead = mat_neg(mat_mul(upp, w_upp))
    back = mat_neg(line.mroll(mat_mul(low_f, w_low), 4))
    load = vec_add(
        vec_sub(r_r, mat_vec(upp, zb)), line.vroll(vec_sub(flux, mat_vec(low_f, zb)), 4)
    )
    reach = 1
    while 2 * reach < count:
        inverse = mat_inv(mid)
        wb, wa, z = mat_mul(inverse, back), mat_mul(inverse, ahead), mat_vec(inverse, load)
        by = 4 * reach
        mid = mat_sub(
            mid,
            mat_add(
                mat_mul(back, line.mroll(wa, by)), mat_mul(ahead, line.mroll(wb, -by))
            ),
        )
        load = vec_sub(
            load,
            vec_add(mat_vec(back, line.vroll(z, by)), mat_vec(ahead, line.vroll(z, -by))),
        )
        back, ahead = (
            mat_neg(mat_mul(back, line.mroll(wb, by))),
            mat_neg(mat_mul(ahead, line.mroll(wa, -by))),
        )
        reach *= 2
    both = mat_add(back, ahead)
    inverse = mat_inv(mid)
    w, z = mat_mul(inverse, both), mat_vec(inverse, load)
    by = 4 * reach
    mid = mat_sub(mid, mat_mul(both, line.mroll(w, by)))
    load = vec_sub(load, mat_vec(both, line.vroll(z, by)))
    x = mat_vec(mat_inv(mid), load)
    b = vec_sub(zb, vec_add(mat_vec(w_low, x), mat_vec(w_upp, line.vroll(x, -4))))
    spread = line.at & 3
    first = [jnp.take_along_axis(y, spread, axis=1) for y in x]
    last = [jnp.take_along_axis(y, spread, axis=1) for y in b]
    swept = line_backward(line, first, last, keep1, keep2, tail, zs)

    wall = Line(0)
    rhs_e, rhs_o = [], []
    for t in range(2):
        packed = [wall.pack1(p, q) for p, q in zip(swept[2 * t], swept[2 * t + 1])]
        rhs_e.append([p[0] for p in packed])
        rhs_o.append([p[1] for p in packed])
    r_r, r_l = line_forward(wall, rhs_e, rhs_o, wkeep1, wkeep2, wkeep3, wzs)
    zb = mat_vec(get_mat(close, 0), r_l)
    put_vec(closed, 0, zb)
    out_r = vec_sub(r_r, mat_vec(get_mat(close, 25), zb))
    out_l = vec_map(lambda y: -y, mat_vec(get_mat(close, 50), zb))
    put_vec(sent, 0, [y[0:4] for y in out_r])
    put_vec(sent, 5, [y[0:4] for y in out_l])


def joint_rhs_kernel(own, other, joint, middle, sent):
    mine = (get_vec(own, 0), get_vec(own, 5))
    theirs = (get_vec(other, 0), get_vec(other, 5))
    load, (right, left) = merge_loads(
        tree_bit(0), get_mat(joint, 25), get_mat(joint, 50), mine, theirs
    )
    put_vec(middle, 0, mat_vec(get_mat(joint, 0), load))
    put_vec(sent, 0, right)
    put_vec(sent, 5, left)


def finish_kernel(*refs, levels):
    count = 1 << levels
    arrived, refs = refs[:count], refs[count:]
    nodes, others, refs = refs[: levels - 1], refs[levels - 1 : 2 * levels - 1], refs[2 * levels - 1 :]
    (half, centre, joint, middle, keep1, keep2, tail, close, closed, zs, field) = refs
    line = Line(0)
    whole = levels - 1
    shared = {}
    for level in range(whole):
        for at, (i, k) in enumerate(tree_nodes(level)):
            shared[i, k + (1 << level)] = (others[level], 100 + 50 * at)
    for at, (i, k) in enumerate(tree_nodes(whole)[1:]):
        shared[i, k + (1 << whole)] = (others[whole], 75 + 50 * at)
    loads = {k: (get_vec(ref, 0), get_vec(ref, 5)) for k, ref in enumerate(arrived)}
    middles = []
    top = tree_bit(levels)
    for level in range(whole):
        upside = tree_bit(level + 1)
        merged = {}
        for k in range(0, count, 2 << level):
            mine, theirs = loads[k], loads[k + (1 << level)]
            if level == whole - 1 and k:
                low, upp = (
                    [vec_map(lambda a, b: either(upside, b, a), m, t) for m, t in zip(mine, theirs)],
                    [vec_map(lambda a, b: either(upside, a, b), m, t) for m, t in zip(mine, theirs)],
                )
                merged[k] = vec_sub(
                    vec_map(lambda a, b: either(top, a, b), upp[1], low[0]),
                    vec_add(
                        mat_vec(get_mat(others[whole], 50), vec_add(low[1], upp[0])),
                        mat_vec(get_mat(others[whole], 25), low[0]),
                    ),
                )
                continue
            ref, at = shared[level, k] if k else (nodes[level], 25)
            load, merged[k] = merge_loads(
                upside, get_mat(ref, at), get_mat(ref, at + 25), mine, theirs
            )
            if k == 0:
                middles.append(mat_vec(get_mat(nodes[level], 0), load))
        loads = merged
    right, left = loads[0]
    load = vec_add(
        loads[1 << whole],
        vec_map(
            lambda a, b: either(top, a, b),
            right,
            vec_sub(left, mat_vec(get_mat(half, 25), right)),
        ),
    )
    between = mat_vec(get_mat(centre, 0), load)
    below = mat_vec(
        get_mat(half, 50), vec_sub(right, mat_vec(get_mat(half, 75), between))
    )
    below, above = (
        vec_map(lambda a, b: either(top, b, a), below, between),
        vec_map(lambda b: either(top, 0.0, b), between),
    )
    path = [(tree_bit(i + 1), nodes[i], middles[i]) for i in reversed(range(whole))]
    path.append((tree_bit(0), joint, get_vec(middle, 0)))
    for upside, node, z in path:
        between = vec_sub(
            z,
            vec_add(mat_vec(get_mat(node, 75), below), mat_vec(get_mat(node, 100), above)),
        )
        below, above = (
            vec_map(lambda a, b: either(upside, b, a), below, between),
            vec_map(lambda a, b: either(upside, b, a), between, above),
        )
    first, nexts = below, above
    first = [jnp.concatenate([x, x], axis=0) for x in first]
    nexts = [jnp.concatenate([x, x], axis=0) for x in nexts]
    last = vec_sub(
        get_vec(closed, 0),
        vec_add(mat_vec(get_mat(close, 75), first), mat_vec(get_mat(close, 100), nexts)),
    )
    last = [jnp.where(line.at < 4, x, line.roll(x, 4)) for x in last]
    out = line_backward(line, first, last, keep1, keep2, tail, zs)
    for s in range(4):
        for c in range(5):
            field[c, s] = out[s][c]


def call(kernel, name, shapes, flops, *args, scratch=()):
    place = pl.BlockSpec(memory_space=pltpu.VMEM)
    return pl.pallas_call(
        kernel,
        name=name,
        out_shape=[jax.ShapeDtypeStruct(s, jnp.float32) for s in shapes],
        in_specs=[pl.BlockSpec(memory_space=pltpu.VMEM)] * len(args),
        out_specs=[place] * len(shapes),
        scratch_shapes=[
            pltpu.VMEM(s, jnp.float32) if isinstance(s, tuple) else s for s in scratch
        ],
        compiler_params=pltpu.CompilerParams(vmem_limit_bytes=VMEM_LIMIT),
        cost_estimate=pl.CostEstimate(flops=flops, bytes_accessed=1 << 20, transcendentals=0),
    )(*args)


def swapped(x, axis, count, by):
    return lax.ppermute(x, axis, [(i, i ^ by) for i in range(count)])


def on_device(state, metrics, time_step, dissipation, *, wrap_count, wall_count):
    levels = wall_count.bit_length() - 2
    row = (4, LANES)
    cells = jnp.concatenate([state, metrics, time_step[None], dissipation], axis=0)
    pair, cross = call(enter_kernel, "enter", [(9,) + row, (9,) + row], 1 << 12, cells)
    across = [(i, i + 1) for i in range(1, wall_count - 1, 2)]
    across += [(b, a) for a, b in across]
    from_pair = swapped(pair, "normal", wall_count, 1)
    from_cross = lax.ppermute(cross, "normal", across)
    wkeep1, wkeep2, wkeep3, rhs_wall, wends = call(
        wall_kernel,
        "wall",
        [(2, 125) + TILE, (125,) + TILE, (1, 75) + TILE, (4, 5) + TILE, (100,) + TILE],
        20 << 20,
        cells,
    )
    keep1, keep2, keep3, rhs_wrap, note, ends = call(
        wrap_kernel,
        "wrap",
        [
            (2, 125) + TILE,
            (125,) + TILE,
            (5, 75) + TILE,
            (2, 10) + TILE,
            (4,) + TILE,
            (100,) + TILE,
        ],
        40 << 20,
        cells,
        scratch=[(100,) + TILE],
    )
    flux, close, segment = call(
        close_kernel,
        "close",
        [(5,) + TILE, (125,) + TILE, (100,) + row],
        4 << 20,
        pair,
        cross,
        from_pair,
        from_cross,
        wends,
        note,
    )
    beside = swapped(segment, "normal", wall_count, 1)
    zs, own = call(
        wrap_rhs_kernel,
        "wrap_rhs",
        [(20,) + TILE, (4,) + TILE],
        8 << 20,
        flux,
        rhs_wall,
        rhs_wrap,
        note,
        keep1,
        keep2,
        keep3,
    )
    notes = [own] + [swapped(own, "wrap", wrap_count, k) for k in range(1, wrap_count)]
    tail, wtail = call(
        tails_kernel, "tails", [(75,) + TILE, (75,) + TILE], 6 << 20, ends, wends, own
    )
    joint, message = call(
        lambda *refs: merge_kernel(*refs, level=0, shared=None, last=False),
        "merge",
        [(125,) + row, (100,) + row],
        4 << 20,
        segment,
        beside,
        own,
    )
    sent, wzs, closed = call(
        lambda *refs: cycle_kernel(*refs, count=wrap_count),
        "cycle",
        [(10,) + row, (20,) + TILE, (5,) + TILE],
        10 << 20,
        *notes,
        keep1,
        keep2,
        tail,
        zs,
        wkeep1,
        wkeep2,
        wkeep3,
        close,
    )
    nodes, others = [], []
    for level in range(levels - 1):
        other = swapped(message, "normal", wall_count, 2 << level)
        final = level == levels - 2
        shared = len(tree_nodes(level))
        handed = 75 + 100 * shared if final else 150 + 100 * shared
        shapes = [(125,) + row, (handed,) + row] + ([(100,) + row] if final else [])
        node, message, *half = call(
            lambda *refs: merge_kernel(*refs, level=level + 1, shared=shared, last=final),
            "merge_%d" % (level + 1),
            shapes,
            4 << 20,
            message,
            other,
            sent,
        )
        nodes.append(node)
        others.append(other)
    other = swapped(message, "normal", wall_count, 1 << levels)
    others.append(other)
    (centre,) = call(middle_kernel, "middle", [(25,) + row], 1 << 16, message, other)
    partner = swapped(sent, "normal", wall_count, 1)
    middle, load = call(
        joint_rhs_kernel, "joint_rhs", [(5,) + row, (10,) + row], 1 << 16, sent, partner, joint
    )
    loads = [load] + [swapped(load, "normal", wall_count, 2 * k) for k in range(1, 1 << levels)]
    (field,) = call(
        lambda *refs: finish_kernel(*refs, levels=levels),
        "finish",
        [(5, 4) + TILE],
        4 << 20,
        *loads,
        *nodes,
        *others,
        *half,
        centre,
        joint,
        middle,
        wkeep1,
        wkeep2,
        wtail,
        close,
        closed,
        wzs,
    )
    return field


def solution(mesh):
    placed = (
        P(None, None, "normal", "wrap"),
        P(None, None, "normal", "wrap"),
        P(None, "normal", "wrap"),
        P(None, None, "normal", "wrap"),
    )

    def body(state, metrics, time_step, dissipation):
        return on_device(
            state,
            metrics,
            time_step,
            dissipation,
            wrap_count=mesh.shape["wrap"],
            wall_count=mesh.shape["normal"],
        )

    return jax.shard_map(
        body,
        mesh=mesh,
        in_specs=placed,
        out_specs=P(None, None, "normal", "wrap"),
        check_vma=False,
    )
```

```python
import jax
import jax.numpy as jnp
from jax import lax
from jax.experimental import pallas as pl
from jax.experimental.pallas import tpu as pltpu
from jax.sharding import PartitionSpec as P

GAMMA = 1.4
LESS = GAMMA - 1.0
VMEM_LIMIT = 16 * 1024 * 1024
TILE = (8, 128)
LANES = 128


def mat_mul(a, b):
    out = []
    for i in range(5):
        row = []
        for j in range(5):
            total = a[i][0] * b[0][j]
            for k in range(1, 5):
                total = total + a[i][k] * b[k][j]
            row.append(total)
        out.append(row)
    return out


def mat_vec(a, x):
    out = []
    for i in range(5):
        total = a[i][0] * x[0]
        for k in range(1, 5):
            total = total + a[i][k] * x[k]
        out.append(total)
    return out


def mat_map(fn, *mats):
    return [[fn(*(m[i][j] for m in mats)) for j in range(5)] for i in range(5)]


def vec_map(fn, *vecs):
    return [fn(*(v[i] for v in vecs)) for i in range(5)]


def mat_add(a, b):
    return mat_map(lambda x, y: x + y, a, b)


def mat_sub(a, b):
    return mat_map(lambda x, y: x - y, a, b)


def mat_neg(a):
    return mat_map(lambda x: -x, a)


def vec_add(a, b):
    return vec_map(lambda x, y: x + y, a, b)


def vec_sub(a, b):
    return vec_map(lambda x, y: x - y, a, b)


def plus_eye(a):
    return [[a[i][j] + 1.0 if i == j else a[i][j] for j in range(5)] for i in range(5)]


def mat_inv(matrix):
    a = [list(row) for row in matrix]
    for k in range(5):
        pivot = 1.0 / a[k][k]
        row = [a[k][j] * pivot if j != k else pivot for j in range(5)]
        for i in range(5):
            if i == k:
                continue
            factor = a[i][k]
            for j in range(5):
                a[i][j] = -(factor * pivot) if j == k else a[i][j] - factor * row[j]
        a[k] = row
    return a


def face_values(left, right):
    state = [0.5 * (left[i] + right[i]) for i in range(5)]
    m1 = 0.5 * (left[5] + right[5])
    m2 = 0.5 * (left[6] + right[6])
    step, spread = left[7], left[8]
    over = 1.0 / state[0]
    u, v, w, e = (state[i] * over for i in range(1, 5))
    t = m1 * u + m2 * v
    f = (0.5 * LESS) * (u * u + v * v + w * w)
    h = GAMMA * e - f
    jac = [
        [None, m1, m2, None, None],
        [
            m1 * f - u * t,
            t - (GAMMA - 2.0) * m1 * u,
            m2 * u - LESS * m1 * v,
            -LESS * m1 * w,
            LESS * m1,
        ],
        [
            m2 * f - v * t,
            m1 * v - LESS * m2 * u,
            t - (GAMMA - 2.0) * m2 * v,
            -LESS * m2 * w,
            LESS * m2,
        ],
        [-w * t, m1 * w, m2 * w, t, None],
        [
            t * (2.0 * f - GAMMA * e),
            m1 * h - LESS * u * t,
            m2 * h - LESS * v * t,
            -LESS * w * t,
            GAMMA * t,
        ],
    ]
    widest = None
    for row in jac:
        total = None
        for x in row:
            if x is not None:
                total = jnp.abs(x) if total is None else total + jnp.abs(x)
        widest = total if widest is None else jnp.maximum(widest, total)
    scale = 1.0 / widest
    norm = [[None if x is None else x * scale for x in row] for row in jac]
    half_step = 0.5 * step
    weight = half_step * spread
    convect = [[None] * 5 for _ in range(5)]
    damping = [[None] * 5 for _ in range(5)]
    for i in range(5):
        for j in range(i, 5):
            parts = [x for x in (norm[i][j], norm[j][i]) if x is not None]
            if parts:
                c = half_step * (parts[0] + parts[1] if len(parts) == 2 else parts[0])
            else:
                c = jnp.zeros_like(step)
            total = None
            for k in range(5):
                if norm[k][i] is None or norm[k][j] is None:
                    continue
                term = norm[k][i] * norm[k][j]
                total = term if total is None else total + term
            if i == j:
                total = total + 1.0
            d = weight * total
            convect[i][j] = convect[j][i] = c
            damping[i][j] = damping[j][i] = d
    jump = [right[i] - left[i] for i in range(5)]
    flux = vec_sub(mat_vec(convect, state), mat_vec(damping, jump))
    lower = mat_map(lambda c, d: -0.5 * c - d, convect, damping)
    upper = mat_map(lambda c, d: 0.5 * c - d, convect, damping)
    for i in range(5):
        for j in range(i):
            lower[i][j] = lower[j][i]
            upper[i][j] = upper[j][i]
    return damping, lower, upper, flux


def put_mat(ref, at, a, lead=()):
    for i in range(5):
        for j in range(5):
            ref[lead + (at + 5 * i + j,)] = a[i][j]


def get_mat(ref, at, lead=()):
    return [[ref[lead + (at + 5 * i + j,)] for j in range(5)] for i in range(5)]


def put_vec(ref, at, x, lead=()):
    for i in range(5):
        ref[lead + (at + i,)] = x[i]


def get_vec(ref, at, lead=()):
    return [ref[lead + (at + i,)] for i in range(5)]


class Line:
    def __init__(self, dim):
        self.dim = dim
        self.n = TILE[dim]
        self.count = self.n // 4
        self.at = lax.broadcasted_iota(jnp.int32, TILE, dim)
        self.even1 = (self.at & 1) == 0
        self.even2 = (self.at & 2) == 0
        self.inner = self.at < self.n - 2
        self.group = self.at >> 2

    def roll(self, x, by):
        if isinstance(by, int):
            by = by % self.n
            if by == 0:
                return x
        return pltpu.roll(x, by, self.dim)

    def vroll(self, v, by):
        return [self.roll(x, by) for x in v]

    def mroll(self, m, by):
        return [self.vroll(row, by) for row in m]

    def pack1(self, a, b):
        first = jnp.where(self.even1, a, self.roll(b, 1))
        second = jnp.where(self.even1, self.roll(a, -1), b)
        return first, second

    def unpack1(self, first, second):
        a = jnp.where(self.even1, first, self.roll(second, 1))
        b = jnp.where(self.even1, self.roll(first, -1), second)
        return a, b

    def pack2(self, a, b):
        first = jnp.where(self.even2, a, self.roll(b, 2))
        second = jnp.where(self.even2, self.roll(a, -2), b)
        return first, second

    def unpack2(self, first, second):
        a = jnp.where(self.even2, first, self.roll(second, 2))
        b = jnp.where(self.even2, self.roll(first, -2), second)
        return a, b


def line_faces(line, cells_e, cells_o):
    after_e = face_values(cells_e, cells_o)
    nexts = [line.roll(x, -2) for x in cells_e[:7]]
    after_o = face_values(cells_o, nexts)
    return after_e, after_o


def first_level(line, after_e, after_o, keep_ref, t):
    damp_e, low_e, upp_e, _ = after_e
    damp_o, low_o, upp_o, _ = after_o
    inverse = mat_inv(plus_eye(mat_add(damp_e, damp_o)))
    w_low = mat_mul(inverse, low_e)
    w_upp = mat_mul(inverse, upp_o)
    put_mat(keep_ref, 0, inverse, (t,))
    put_mat(keep_ref, 25, upp_e, (t,))
    put_mat(keep_ref, 50, low_o, (t,))
    put_mat(keep_ref, 75, w_low, (t,))
    put_mat(keep_ref, 100, w_upp, (t,))
    inner = line.inner
    low = mat_map(lambda x, y: jnp.where(inner, -x, y), mat_mul(low_o, w_low), low_e)
    mid_l = mat_map(
        lambda x, y, z: jnp.where(inner, y - x, z), mat_mul(low_o, w_upp), damp_o, damp_e
    )
    upp = mat_map(lambda x, y: jnp.where(inner, -x, y), mat_mul(upp_e, w_upp), upp_e)
    mid_r = mat_map(
        lambda x, y: jnp.where(inner, y - x, y), mat_mul(upp_e, w_low), plus_eye(damp_e)
    )
    return line.mroll(low, 2), line.mroll(mid_l, 2), mid_r, upp


def second_level(line, level_a, level_b, keep_ref):
    packed = [
        [[line.pack2(x, y) for x, y in zip(ra, rb)] for ra, rb in zip(ma, mb)]
        for ma, mb in zip(level_a, level_b)
    ]
    evens = [mat_map(lambda p: p[0], m) for m in packed]
    odds = [mat_map(lambda p: p[1], m) for m in packed]
    inverse = mat_inv(mat_add(odds[1], odds[2]))
    w_low = mat_mul(inverse, odds[0])
    w_upp = mat_mul(inverse, odds[3])
    put_mat(keep_ref, 0, inverse)
    put_mat(keep_ref, 25, evens[3])
    put_mat(keep_ref, 50, evens[0])
    put_mat(keep_ref, 75, w_low)
    put_mat(keep_ref, 100, w_upp)
    left_low = line.mroll(w_low, 4)
    left_upp = line.mroll(w_upp, 4)
    low = mat_neg(mat_mul(evens[0], left_low))
    mid_l = mat_sub(evens[1], mat_mul(evens[0], left_upp))
    mid_r = mat_sub(evens[2], mat_mul(evens[3], w_low))
    upp = mat_neg(mat_mul(evens[3], w_upp))
    return low, mid_l, mid_r, upp


def later_level(line, low, mid_l, mid_r, upp, reach, keep_ref, level):
    left_ok = (line.group > reach) | (line.group == 0)
    right_ok = line.group + reach < line.count
    inverse = mat_inv(mat_add(mid_l, mid_r))
    w_low = mat_mul(inverse, low)
    w_upp = mat_mul(inverse, upp)
    low_in = mat_map(lambda x: jnp.where(left_ok, x, 0.0), low)
    upp_in = mat_map(lambda x: jnp.where(right_ok, x, 0.0), upp)
    put_mat(keep_ref, 0, inverse, (level,))
    put_mat(keep_ref, 25, low_in, (level,))
    put_mat(keep_ref, 50, upp_in, (level,))
    back = 4 * reach
    ahead = line.n - 4 * reach
    left_low, left_upp = line.mroll(w_low, back), line.mroll(w_upp, back)
    right_low, right_upp = line.mroll(w_low, ahead), line.mroll(w_upp, ahead)
    new_low = mat_map(
        lambda x, y: jnp.where(left_ok, -x, y), mat_mul(low_in, left_low), low
    )
    new_mid_l = mat_sub(mid_l, mat_mul(low_in, left_upp))
    new_upp = mat_map(
        lambda x, y: jnp.where(right_ok, -x, y), mat_mul(upp_in, right_upp), upp
    )
    new_mid_r = mat_sub(mid_r, mat_mul(upp_in, right_low))
    return new_low, new_mid_l, new_mid_r, new_upp


def line_levels(line, states, keep1, keep2, keep3, ends, work):
    low, mid_l, mid_r, upp = second_level(line, states[0], states[1], keep2)
    steps = line.count.bit_length() - 1
    if steps == 1:
        low, mid_l, mid_r, upp = later_level(line, low, mid_l, mid_r, upp, 1, keep3, 0)
    else:
        for at, m in enumerate((low, mid_l, mid_r, upp)):
            put_mat(work, 25 * at, m)

        def body(level, carry):
            now = [get_mat(work, 25 * at) for at in range(4)]
            reach = lax.shift_left(jnp.int32(1), level)
            new = later_level(line, *now, reach, keep3, level)
            for at, m in enumerate(new):
                put_mat(work, 25 * at, m)
            return carry

        lax.fori_loop(0, steps, body, 0)
        low, mid_l, mid_r, upp = (get_mat(work, 25 * at) for at in range(4))
    for at, m in enumerate((low, mid_l, mid_r, upp)):
        put_mat(ends, 25 * at, m)


def line_forward(line, rhs_e, rhs_o, keep1, keep2, keep3, zs):
    right, left = [], []
    for t in range(2):
        z = mat_vec(get_mat(keep1, 0, (t,)), rhs_o[t])
        put_vec(zs, 5 * t, z)
        from_r = mat_vec(get_mat(keep1, 25, (t,)), z)
        from_l = mat_vec(get_mat(keep1, 50, (t,)), z)
        right.append(
            vec_map(lambda r, x: jnp.where(line.inner, r - x, r), rhs_e[t], from_r)
        )
        left.append(
            line.vroll(vec_map(lambda r, x: jnp.where(line.inner, -x, r), rhs_o[t], from_l), 2)
        )
    pair_r = [line.pack2(x, y) for x, y in zip(right[0], right[1])]
    pair_l = [line.pack2(x, y) for x, y in zip(left[0], left[1])]
    odd = [x[1] + y[1] for x, y in zip(pair_r, pair_l)]
    z = mat_vec(get_mat(keep2, 0), odd)
    put_vec(zs, 10, z)
    r_r = vec_sub([x[0] for x in pair_r], mat_vec(get_mat(keep2, 25), z))
    r_l = vec_sub([x[0] for x in pair_l], mat_vec(get_mat(keep2, 50), line.vroll(z, 4)))
    steps = line.count.bit_length() - 1
    for level in range(steps):
        z = mat_vec(get_mat(keep3, 0, (level,)), vec_add(r_l, r_r))
        back = 4 << level
        r_l = vec_sub(r_l, mat_vec(get_mat(keep3, 25, (level,)), line.vroll(z, back)))
        r_r = vec_sub(r_r, mat_vec(get_mat(keep3, 50, (level,)), line.vroll(z, -back)))
    put_vec(zs, 15, vec_add(r_l, r_r))
    return r_r, r_l


def line_backward(line, first, last, keep1, keep2, tail, zs):
    inner = vec_sub(
        mat_vec(get_mat(tail, 0), get_vec(zs, 15)),
        vec_add(mat_vec(get_mat(tail, 25), first), mat_vec(get_mat(tail, 50), last)),
    )
    even = vec_map(lambda x, y: jnp.where(line.group == 0, y, x), inner, first)
    ahead = vec_map(
        lambda x, y: jnp.where(line.at >= line.n - 4, y, x), line.vroll(even, -4), last
    )
    odd = vec_sub(
        get_vec(zs, 10),
        vec_add(
            mat_vec(get_mat(keep2, 75), even), mat_vec(get_mat(keep2, 100), ahead)
        ),
    )
    pairs = [line.unpack2(x, y) for x, y in zip(even, odd)]
    out = []
    for t in range(2):
        even = [p[t] for p in pairs]
        ends = line.vroll(last, 2) if t == 0 else last
        ahead = line.vroll(even, -2)
        odd = vec_sub(
            get_vec(zs, 5 * t),
            vec_add(
                mat_vec(get_mat(keep1, 75, (t,)), even),
                mat_vec(get_mat(keep1, 100, (t,)), ahead),
            ),
        )
        odd = vec_map(lambda x, y: jnp.where(line.inner, x, y), odd, ends)
        spans = [line.unpack1(x, y) for x, y in zip(even, odd)]
        out.append([s[0] for s in spans])
        out.append([s[1] for s in spans])
    return out


def tails_kernel(ends_wrap, ends_wall, after, tail_wrap, tail_wall):
    for ends, tail in ((ends_wrap, tail_wrap), (ends_wall, tail_wall)):
        low, mid_l, mid_r, upp = (get_mat(ends, 25 * at) for at in range(4))
        inverse = mat_inv(mat_add(mid_l, mid_r))
        put_mat(tail, 0, inverse)
        put_mat(tail, 25, mat_mul(inverse, low))
        put_mat(tail, 50, mat_mul(inverse, upp))


def odd_device(axis):
    return (lax.axis_index(axis) & 1) == 1


def either(flag, a, b):
    return jnp.where(flag, a, b)


def split_cells(cells):
    return cells.at[0:5], cells.at[5:9], cells.at[9], cells.at[10:12]


def enter_kernel(cells, pair, cross):
    state, metrics, step, spread = split_cells(cells)
    odd = odd_device("normal")

    def send(c, s, rows):
        first, last = rows(0), rows(7)
        pair[c, s : s + 1, :] = either(odd, first, last)
        cross[c, s : s + 1, :] = either(odd, last, first)

    for s in range(4):
        for c in range(5):
            send(c, s, lambda k: state[c, s, k : k + 1, :])
        for c in range(2):
            send(5 + c, s, lambda k: metrics[2 + c, s, k : k + 1, :])
        send(7, s, lambda k: step[s, k : k + 1, :])
        send(8, s, lambda k: spread[1, s, k : k + 1, :])


def load_cells(line, state, metrics, step, spread, t, metric_at, spread_at):
    first, second = 2 * t, 2 * t + 1
    pairs = [(state[c, first], state[c, second]) for c in range(5)]
    pairs += [(metrics[metric_at + c, first], metrics[metric_at + c, second]) for c in range(2)]
    pairs += [(step[first], step[second]), (spread[spread_at, first], spread[spread_at, second])]
    packed = [line.pack1(a, b) for a, b in pairs]
    return [p[0] for p in packed], [p[1] for p in packed]


def line_residual(line, after_e, after_o):
    flux_e, flux_o = after_e[3], after_o[3]
    flux_o = vec_map(lambda x: jnp.where(line.inner, x, 0.0), flux_o)
    return vec_sub(line.vroll(flux_o, 2), flux_e), vec_sub(flux_e, flux_o)


def wrap_kernel(cells, keep1, keep2, keep3, rhs, note, ends, work):
    state, metrics, step, spread = split_cells(cells)
    line = Line(1)
    states = []
    note[...] = jnp.zeros_like(note)
    packed = [jnp.zeros(TILE, jnp.float32) for _ in range(4)]
    lane_group = line.group
    for t in range(2):
        cells_e, cells_o = load_cells(line, state, metrics, step, spread, t, 0, 0)
        pick = line.at & 3
        mine = (pick >> 1) == t
        for c in range(9):
            k, g = divmod(100 + c, 32)
            moved = line.roll(cells_o[c], 4 * g + 2 * t - (line.n - 2))
            packed[k] = jnp.where((lane_group == g) & mine, moved, packed[k])
        for c in range(7):
            k, g = divmod(109 + c, 32)
            moved = line.roll(cells_e[c], 4 * g + 2 * t)
            packed[k] = jnp.where((lane_group == g) & mine, moved, packed[k])
        after_e, after_o = line_faces(line, cells_e, cells_o)
        rhs_e, rhs_o = line_residual(line, after_e, after_o)
        put_vec(rhs, 0, rhs_e, (t,))
        put_vec(rhs, 5, rhs_o, (t,))
        states.append(first_level(line, after_e, after_o, keep1, t))
    line_levels(line, states, keep1, keep2, keep3, ends, work)
    for place, at in enumerate((50, 75, 0, 25)):
        for c in range(25):
            k, g = divmod(25 * place + c, 32)
            packed[k] = jnp.where(lane_group == g, line.roll(ends[at + c], 4 * g), packed[k])
    for k in range(4):
        note[k] = packed[k]


def put_face(ref, lead, face):
    for which in range(3):
        at = 0
        for i in range(5):
            for j in range(i, 5):
                ref[lead + (15 * which + at,)] = face[which][i][j]
                at += 1


def get_face(ref, lead):
    out = []
    for which in range(3):
        m = [[None] * 5 for _ in range(5)]
        at = 0
        for i in range(5):
            for j in range(i, 5):
                m[i][j] = m[j][i] = ref[lead + (15 * which + at,)]
                at += 1
        out.append(m)
    return out + [None]


def wall_faces_kernel(cells, coefs, rhs):
    state, metrics, step, spread = split_cells(cells)
    line = Line(0)
    for t in range(2):
        cells_e, cells_o = load_cells(line, state, metrics, step, spread, t, 2, 1)
        after_e, after_o = line_faces(line, cells_e, cells_o)
        rhs_e, rhs_o = line_residual(line, after_e, after_o)
        for c in range(5):
            a, b = line.unpack1(rhs_e[c], rhs_o[c])
            rhs[2 * t, c] = a
            rhs[2 * t + 1, c] = b
        for half, face in enumerate((after_e, after_o)):
            put_face(coefs, (t, half), face)


def edge_faces(pair, cross, from_pair, from_cross):
    odd = odd_device("normal")
    left, right = [], []
    for c in range(9):
        below = either(odd, from_pair[c], from_cross[c])
        own = either(odd, cross[c], pair[c])
        left.append(jnp.concatenate([below, own], axis=0))
    for c in range(7):
        above = either(odd, from_cross[c], from_pair[c])
        own = either(odd, pair[c], cross[c])
        right.append(jnp.concatenate([own, above], axis=0))
    return face_values(left, right)


def wall_kernel(coefs, edge, keep1, keep2, keep3, ends, close, segment):
    line = Line(0)
    states = []
    for t in range(2):
        after_e, after_o = get_face(coefs, (t, 0)), get_face(coefs, (t, 1))
        states.append(first_level(line, after_e, after_o, keep1, t))
    line_levels(line, states, keep1, keep2, keep3, ends, None)
    damp_f, low_f, upp_f, _ = get_face(edge, ())
    low, mid_l, mid_r, upp = (get_mat(ends, 25 * at) for at in range(4))
    inverse = mat_inv(plus_eye(mat_add(mid_l, damp_f)))
    w_low = mat_mul(inverse, low)
    w_upp = mat_mul(inverse, upp_f)
    put_mat(close, 0, inverse)
    put_mat(close, 25, upp)
    put_mat(close, 50, low_f)
    put_mat(close, 75, w_low)
    put_mat(close, 100, w_upp)
    mid_r = mat_sub(mid_r, mat_mul(upp, w_low))
    upp = mat_neg(mat_mul(upp, w_upp))
    low = mat_neg(mat_mul(low_f, w_low))
    mid_l = mat_sub(damp_f, mat_mul(low_f, w_upp))
    for at, m in enumerate((mid_r, upp, low, mid_l)):
        put_mat(segment, 25 * at, mat_map(lambda x: x[0:4], m))


def segment_mats(ref):
    return [get_mat(ref, 25 * at) for at in range(4)]


def tree_bit(level):
    return ((lax.axis_index("normal") >> level) & 1) == 1


def merge_kernel(*refs, level, last):
    node, result = refs[-2:]
    if level == 0:
        lower, upper = segment_mats(refs[0].at[0]), segment_mats(refs[0].at[1])
    else:
        upside = tree_bit(level)
        mine, theirs = segment_mats(refs[0]), segment_mats(refs[1])
        lower = [mat_map(lambda a, b: either(upside, b, a), m, t) for m, t in zip(mine, theirs)]
        upper = [mat_map(lambda a, b: either(upside, a, b), m, t) for m, t in zip(mine, theirs)]
    inverse = mat_inv(mat_add(lower[3], upper[0]))
    w_low = mat_mul(inverse, lower[2])
    up_in = mat_mul(lower[1], inverse)
    low_in = mat_mul(upper[2], inverse)
    w_upp = mat_mul(inverse, upper[1])
    for at, m in enumerate((inverse, up_in, low_in, w_low, w_upp)):
        put_mat(node, 25 * at, m)
    mid_r = mat_sub(lower[0], mat_mul(lower[1], w_low))
    upp = mat_neg(mat_mul(lower[1], w_upp))
    low = mat_neg(mat_mul(upper[2], w_low))
    mid_l = mat_sub(upper[3], mat_mul(upper[2], w_upp))
    if last:
        top = tree_bit(level + 1)
        first = mat_inv(mid_r)
        through = mat_mul(low, first)
        core = mat_map(
            lambda a, b: either(top, a, b), mid_r, mat_sub(mid_l, mat_mul(through, upp))
        )
        parts = (core, through, first, upp)
    else:
        parts = (mid_r, upp, low, mid_l)
    for at, m in enumerate(parts):
        put_mat(result, 25 * at, m)


def merge_loads(upside, up_in, low_in, mine, theirs):
    lower = [vec_map(lambda a, b: either(upside, b, a), m, t) for m, t in zip(mine, theirs)]
    upper = [vec_map(lambda a, b: either(upside, a, b), m, t) for m, t in zip(mine, theirs)]
    load = vec_add(lower[1], upper[0])
    right = vec_sub(lower[0], mat_vec(up_in, load))
    left = vec_sub(upper[1], mat_vec(low_in, load))
    return load, (right, left)


def in_order(position, count):
    def pick(values, q):
        ks = sorted({c ^ ((c + q) % count) for c in range(count)})
        wanted = position ^ ((position + q) % count)
        out = values[ks[0]]
        for k in ks[1:]:
            out = jnp.where(wanted == k, values[k], out)
        return out

    return pick


def wrap_rhs_kernel(
    pair, cross, from_pair, from_cross, rhs_wall, rhs_wrap, note, keep1, keep2, keep3, zs, sent, edge
):
    line, wall = Line(1), Line(0)
    face = edge_faces(pair, cross, from_pair, from_cross)
    through = face[3]
    put_face(edge, (), [mat_map(lambda x: wall.roll(x, 4), m) for m in face[:3]])
    rhs_e, rhs_o = [], []
    for t in range(2):
        spans = []
        for s in (2 * t, 2 * t + 1):
            values = []
            for c in range(5):
                x = rhs_wall[s, c]
                x = jnp.where(wall.at == 0, x + wall.roll(through[c], -s), x)
                x = jnp.where(wall.at == 7, x - wall.roll(through[c], 3 - s), x)
                values.append(x)
            spans.append(values)
        packed = [line.pack1(a, b) for a, b in zip(*spans)]
        rhs_e.append([packed[c][0] + rhs_wrap[t, c] for c in range(5)])
        rhs_o.append([packed[c][1] + rhs_wrap[t, 5 + c] for c in range(5)])
    r_r, r_l = line_forward(line, rhs_e, rhs_o, keep1, keep2, keep3, zs)
    for k in range(3):
        sent[k] = note[k]
    tail = note[3]
    for c in range(10):
        g = 116 + c - 96
        value = r_r[c] if c < 5 else r_l[c - 5]
        tail = jnp.where(line.group == g, line.roll(value, 4 * g), tail)
    sent[3] = tail


def cycle_kernel(*refs, count):
    arrived = refs[:count]
    (keep1, keep2, tail, zs, wkeep1, wkeep2, wkeep3, close) = refs[count : count + 8]
    sent, wzs, closed = refs[count + 8 :]
    pick = in_order(lax.axis_index("wrap"), count)
    notes = [
        [pick([ref[k] for ref in arrived], q) for k in range(4)] for q in range(count)
    ]
    line = Line(1)
    period = 4 * count
    repeat = line.at % period
    channels = [None] * 126
    for k in range(4):
        rolled = [line.roll(notes[q][k], 4 * q) for q in range(count)]
        for a in range(count):
            which = (line.group - a) % count
            mixed = rolled[0]
            for q in range(1, count):
                mixed = jnp.where(which == q, rolled[q], mixed)
            for c in range(a, 32, count):
                if 32 * k + c < 126:
                    index = (repeat + 4 * c) & (LANES - 1)
                    channels[32 * k + c] = jnp.take_along_axis(mixed, index, axis=1)

    def mat_at(at):
        return [[channels[at + 5 * i + j] for j in range(5)] for i in range(5)]

    mid_r, upp, low, mid_l = (mat_at(25 * i) for i in range(4))
    left = channels[100:109]
    right = line.vroll(channels[109:116], -4)
    r_r, r_l = channels[116:121], channels[121:126]
    damp_f, low_f, upp_f, flux = face_values(left, right)
    inverse = mat_inv(plus_eye(mat_add(mid_l, damp_f)))
    w_low = mat_mul(inverse, low)
    w_upp = mat_mul(inverse, upp_f)
    zb = mat_vec(inverse, vec_sub(r_l, flux))
    mid = mat_add(
        mat_sub(mid_r, mat_mul(upp, w_low)),
        line.mroll(mat_sub(damp_f, mat_mul(low_f, w_upp)), 4),
    )
    ahead = mat_neg(mat_mul(upp, w_upp))
    back = mat_neg(line.mroll(mat_mul(low_f, w_low), 4))
    load = vec_add(
        vec_sub(r_r, mat_vec(upp, zb)), line.vroll(vec_sub(flux, mat_vec(low_f, zb)), 4)
    )
    reach = 1
    while 2 * reach < count:
        inverse = mat_inv(mid)
        wb, wa, z = mat_mul(inverse, back), mat_mul(inverse, ahead), mat_vec(inverse, load)
        by = 4 * reach
        mid = mat_sub(
            mid,
            mat_add(
                mat_mul(back, line.mroll(wa, by)), mat_mul(ahead, line.mroll(wb, -by))
            ),
        )
        load = vec_sub(
            load,
            vec_add(mat_vec(back, line.vroll(z, by)), mat_vec(ahead, line.vroll(z, -by))),
        )
        back, ahead = (
            mat_neg(mat_mul(back, line.mroll(wb, by))),
            mat_neg(mat_mul(ahead, line.mroll(wa, -by))),
        )
        reach *= 2
    both = mat_add(back, ahead)
    inverse = mat_inv(mid)
    w, z = mat_mul(inverse, both), mat_vec(inverse, load)
    by = 4 * reach
    mid = mat_sub(mid, mat_mul(both, line.mroll(w, by)))
    load = vec_sub(load, mat_vec(both, line.vroll(z, by)))
    x = mat_vec(mat_inv(mid), load)
    b = vec_sub(zb, vec_add(mat_vec(w_low, x), mat_vec(w_upp, line.vroll(x, -4))))
    spread = line.at & 3
    first = [jnp.take_along_axis(y, spread, axis=1) for y in x]
    last = [jnp.take_along_axis(y, spread, axis=1) for y in b]
    swept = line_backward(line, first, last, keep1, keep2, tail, zs)

    wall = Line(0)
    rhs_e, rhs_o = [], []
    for t in range(2):
        packed = [wall.pack1(p, q) for p, q in zip(swept[2 * t], swept[2 * t + 1])]
        rhs_e.append([p[0] for p in packed])
        rhs_o.append([p[1] for p in packed])
    r_r, r_l = line_forward(wall, rhs_e, rhs_o, wkeep1, wkeep2, wkeep3, wzs)
    zb = mat_vec(get_mat(close, 0), r_l)
    put_vec(closed, 0, zb)
    out_r = vec_sub(r_r, mat_vec(get_mat(close, 25), zb))
    out_l = vec_map(lambda y: -y, mat_vec(get_mat(close, 50), zb))
    put_vec(sent, 0, [y[0:4] for y in out_r])
    put_vec(sent, 5, [y[0:4] for y in out_l])


def joint_rhs_kernel(own, other, node, *refs, level, last):
    mine = (get_vec(own, 0), get_vec(own, 5))
    theirs = (get_vec(other, 0), get_vec(other, 5))
    load, (right, left) = merge_loads(
        tree_bit(level), get_mat(node, 25), get_mat(node, 50), mine, theirs
    )
    if not last:
        middle, sent = refs
        put_vec(middle, 0, mat_vec(get_mat(node, 0), load))
        put_vec(sent, 0, right)
        put_vec(sent, 5, left)
        return
    half, middle, sent = refs
    put_vec(middle, 0, mat_vec(get_mat(node, 0), load))
    put_vec(middle, 5, right)
    top = tree_bit(level + 1)
    closed = vec_sub(left, mat_vec(get_mat(half, 25), right))
    for c in range(25):
        sent[c] = half[c]
    put_vec(sent, 25, vec_map(lambda a, b: either(top, a, b), right, closed))


def mat_solve(matrix, load):
    a = [list(row) + [x] for row, x in zip(matrix, load)]
    for k in range(5):
        over = 1.0 / a[k][k]
        for j in range(k + 1, 6):
            a[k][j] = a[k][j] * over
        for i in range(k + 1, 5):
            for j in range(k + 1, 6):
                a[i][j] = a[i][j] - a[i][k] * a[k][j]
    x = [None] * 5
    for i in reversed(range(5)):
        total = a[i][5]
        for j in range(i + 1, 5):
            total = total - a[i][j] * x[j]
        x[i] = total
    return x


def finish_kernel(own, other, half, *refs, levels):
    nodes, middles = refs[: levels - 1], refs[levels - 1 : 2 * levels - 2]
    (keep1, keep2, tail, close, closed, zs, field) = refs[2 * levels - 2 :]
    line = Line(0)
    between = mat_solve(
        mat_add(get_mat(own, 0), get_mat(other, 0)),
        vec_add(get_vec(own, 25), get_vec(other, 25)),
    )
    below = mat_vec(
        get_mat(half, 50),
        vec_sub(get_vec(middles[-1], 5), mat_vec(get_mat(half, 75), between)),
    )
    top = tree_bit(levels - 1)
    below, above = (
        vec_map(lambda a, b: either(top, b, a), below, between),
        vec_map(lambda b: either(top, 0.0, b), between),
    )
    for level in reversed(range(levels - 1)):
        node = nodes[level]
        between = vec_sub(
            get_vec(middles[level], 0),
            vec_add(mat_vec(get_mat(node, 75), below), mat_vec(get_mat(node, 100), above)),
        )
        upside = tree_bit(level)
        below, above = (
            vec_map(lambda a, b: either(upside, b, a), below, between),
            vec_map(lambda a, b: either(upside, b, a), between, above),
        )
    first, nexts = below, above
    first = [jnp.concatenate([x, x], axis=0) for x in first]
    nexts = [jnp.concatenate([x, x], axis=0) for x in nexts]
    last = vec_sub(
        get_vec(closed, 0),
        vec_add(mat_vec(get_mat(close, 75), first), mat_vec(get_mat(close, 100), nexts)),
    )
    last = [jnp.where(line.at < 4, x, line.roll(x, 4)) for x in last]
    out = line_backward(line, first, last, keep1, keep2, tail, zs)
    for s in range(4):
        for c in range(5):
            field[c, s] = out[s][c]


def call(kernel, name, shapes, flops, *args, scratch=()):
    place = pl.BlockSpec(memory_space=pltpu.VMEM)
    return pl.pallas_call(
        kernel,
        name=name,
        out_shape=[jax.ShapeDtypeStruct(s, jnp.float32) for s in shapes],
        in_specs=[pl.BlockSpec(memory_space=pltpu.VMEM)] * len(args),
        out_specs=[place] * len(shapes),
        scratch_shapes=[
            pltpu.VMEM(s, jnp.float32) if isinstance(s, tuple) else s for s in scratch
        ],
        compiler_params=pltpu.CompilerParams(vmem_limit_bytes=VMEM_LIMIT),
        cost_estimate=pl.CostEstimate(flops=flops, bytes_accessed=1 << 20, transcendentals=0),
    )(*args)


def swapped(x, axis, count, by):
    return lax.ppermute(x, axis, [(i, i ^ by) for i in range(count)])


def on_device(state, metrics, time_step, dissipation, *, wrap_count, wall_count):
    levels = wall_count.bit_length() - 1
    row = (4, LANES)
    cells = jnp.concatenate([state, metrics, time_step[None], dissipation], axis=0)
    pair, cross = call(enter_kernel, "enter", [(9,) + row, (9,) + row], 1 << 12, cells)
    across = [(i, i + 1) for i in range(1, wall_count - 1, 2)]
    across += [(b, a) for a, b in across]
    from_pair = swapped(pair, "normal", wall_count, 1)
    from_cross = lax.ppermute(cross, "normal", across)
    coefs, rhs_wall = call(
        wall_faces_kernel, "wall_faces", [(2, 2, 45) + TILE, (4, 5) + TILE], 8 << 20, cells
    )
    keep1, keep2, keep3, rhs_wrap, note, ends = call(
        wrap_kernel,
        "wrap",
        [
            (2, 125) + TILE,
            (125,) + TILE,
            (5, 75) + TILE,
            (2, 10) + TILE,
            (4,) + TILE,
            (100,) + TILE,
        ],
        40 << 20,
        cells,
        scratch=[(100,) + TILE],
    )
    zs, own, edge = call(
        wrap_rhs_kernel,
        "wrap_rhs",
        [(20,) + TILE, (4,) + TILE, (45,) + TILE],
        8 << 20,
        pair,
        cross,
        from_pair,
        from_cross,
        rhs_wall,
        rhs_wrap,
        note,
        keep1,
        keep2,
        keep3,
    )
    notes = [own] + [swapped(own, "wrap", wrap_count, k) for k in range(1, wrap_count)]
    wkeep1, wkeep2, wkeep3, wends, close, segment = call(
        wall_kernel,
        "wall",
        [
            (2, 125) + TILE,
            (125,) + TILE,
            (1, 75) + TILE,
            (100,) + TILE,
            (125,) + TILE,
            (100,) + row,
        ],
        20 << 20,
        coefs,
        edge,
    )
    joined = [
        lax.all_gather(
            segment, "normal", axis_index_groups=[[i, i + 1] for i in range(0, wall_count, 2)]
        )
    ]
    tail, wtail = call(
        tails_kernel, "tails", [(75,) + TILE, (75,) + TILE], 6 << 20, ends, wends, own
    )
    sent, wzs, closed = call(
        lambda *refs: cycle_kernel(*refs, count=wrap_count),
        "cycle",
        [(10,) + row, (20,) + TILE, (5,) + TILE],
        10 << 20,
        *notes,
        keep1,
        keep2,
        tail,
        zs,
        wkeep1,
        wkeep2,
        wkeep3,
        close,
    )
    nodes = []
    for level in range(levels - 1):
        last = level == levels - 2
        node, result = call(
            lambda *refs: merge_kernel(*refs, level=level, last=last),
            "merge_%d" % level,
            [(125,) + row, (100,) + row],
            4 << 20,
            *joined,
            *(notes[1:] if level == 0 else []),
        )
        nodes.append(node)
        if not last:
            joined = [result, swapped(result, "normal", wall_count, 2 << level)]
    middles = []
    for level in range(levels - 1):
        last = level == levels - 2
        partner = swapped(sent, "normal", wall_count, 1 << level)
        middle, sent = call(
            lambda *refs: joint_rhs_kernel(*refs, level=level, last=last),
            "joint_rhs_%d" % level,
            [(10 if last else 5,) + row, (30 if last else 10,) + row],
            1 << 16,
            sent,
            partner,
            nodes[level],
            *([result] if last else []),
        )
        middles.append(middle)
    partner = swapped(sent, "normal", wall_count, 1 << (levels - 1))
    (field,) = call(
        lambda *refs: finish_kernel(*refs, levels=levels),
        "finish",
        [(5, 4) + TILE],
        4 << 20,
        sent,
        partner,
        result,
        *nodes,
        *middles,
        wkeep1,
        wkeep2,
        wtail,
        close,
        closed,
        wzs,
    )
    return field


def solution(mesh):
    placed = (
        P(None, None, "normal", "wrap"),
        P(None, None, "normal", "wrap"),
        P(None, "normal", "wrap"),
        P(None, None, "normal", "wrap"),
    )

    def body(state, metrics, time_step, dissipation):
        return on_device(
            state,
            metrics,
            time_step,
            dissipation,
            wrap_count=mesh.shape["wrap"],
            wall_count=mesh.shape["normal"],
        )

    return jax.shard_map(
        body,
        mesh=mesh,
        in_specs=placed,
        out_specs=P(None, None, "normal", "wrap"),
        check_vma=False,
    )
```

```python
import jax
import jax.numpy as jnp
from jax import lax
from jax.experimental import pallas as pl
from jax.experimental.pallas import tpu as pltpu
from jax.sharding import PartitionSpec as P

GAMMA = 1.4
LESS = GAMMA - 1.0
VMEM_LIMIT = 16 * 1024 * 1024
TILE = (8, 128)
LANES = 128


def mat_mul(a, b):
    out = []
    for i in range(5):
        row = []
        for j in range(5):
            total = a[i][0] * b[0][j]
            for k in range(1, 5):
                total = total + a[i][k] * b[k][j]
            row.append(total)
        out.append(row)
    return out


def mat_vec(a, x):
    out = []
    for i in range(5):
        total = a[i][0] * x[0]
        for k in range(1, 5):
            total = total + a[i][k] * x[k]
        out.append(total)
    return out


def mat_map(fn, *mats):
    return [[fn(*(m[i][j] for m in mats)) for j in range(5)] for i in range(5)]


def vec_map(fn, *vecs):
    return [fn(*(v[i] for v in vecs)) for i in range(5)]


def mat_add(a, b):
    return mat_map(lambda x, y: x + y, a, b)


def mat_sub(a, b):
    return mat_map(lambda x, y: x - y, a, b)


def mat_neg(a):
    return mat_map(lambda x: -x, a)


def vec_add(a, b):
    return vec_map(lambda x, y: x + y, a, b)


def vec_sub(a, b):
    return vec_map(lambda x, y: x - y, a, b)


def plus_eye(a):
    return [[a[i][j] + 1.0 if i == j else a[i][j] for j in range(5)] for i in range(5)]


def mat_inv(matrix):
    a = [list(row) for row in matrix]
    for k in range(5):
        pivot = 1.0 / a[k][k]
        row = [a[k][j] * pivot if j != k else pivot for j in range(5)]
        for i in range(5):
            if i == k:
                continue
            factor = a[i][k]
            for j in range(5):
                a[i][j] = -(factor * pivot) if j == k else a[i][j] - factor * row[j]
        a[k] = row
    return a


def face_values(left, right):
    state = [0.5 * (left[i] + right[i]) for i in range(5)]
    m1 = 0.5 * (left[5] + right[5])
    m2 = 0.5 * (left[6] + right[6])
    step, spread = left[7], left[8]
    over = 1.0 / state[0]
    u, v, w, e = (state[i] * over for i in range(1, 5))
    t = m1 * u + m2 * v
    f = (0.5 * LESS) * (u * u + v * v + w * w)
    h = GAMMA * e - f
    jac = [
        [None, m1, m2, None, None],
        [
            m1 * f - u * t,
            t - (GAMMA - 2.0) * m1 * u,
            m2 * u - LESS * m1 * v,
            -LESS * m1 * w,
            LESS * m1,
        ],
        [
            m2 * f - v * t,
            m1 * v - LESS * m2 * u,
            t - (GAMMA - 2.0) * m2 * v,
            -LESS * m2 * w,
            LESS * m2,
        ],
        [-w * t, m1 * w, m2 * w, t, None],
        [
            t * (2.0 * f - GAMMA * e),
            m1 * h - LESS * u * t,
            m2 * h - LESS * v * t,
            -LESS * w * t,
            GAMMA * t,
        ],
    ]
    widest = None
    for row in jac:
        total = None
        for x in row:
            if x is not None:
                total = jnp.abs(x) if total is None else total + jnp.abs(x)
        widest = total if widest is None else jnp.maximum(widest, total)
    scale = 1.0 / widest
    norm = [[None if x is None else x * scale for x in row] for row in jac]
    half_step = 0.5 * step
    weight = half_step * spread
    convect = [[None] * 5 for _ in range(5)]
    damping = [[None] * 5 for _ in range(5)]
    for i in range(5):
        for j in range(i, 5):
            parts = [x for x in (norm[i][j], norm[j][i]) if x is not None]
            if parts:
                c = half_step * (parts[0] + parts[1] if len(parts) == 2 else parts[0])
            else:
                c = jnp.zeros_like(step)
            total = None
            for k in range(5):
                if norm[k][i] is None or norm[k][j] is None:
                    continue
                term = norm[k][i] * norm[k][j]
                total = term if total is None else total + term
            if i == j:
                total = total + 1.0
            d = weight * total
            convect[i][j] = convect[j][i] = c
            damping[i][j] = damping[j][i] = d
    jump = [right[i] - left[i] for i in range(5)]
    flux = vec_sub(mat_vec(convect, state), mat_vec(damping, jump))
    lower = mat_map(lambda c, d: -0.5 * c - d, convect, damping)
    upper = mat_map(lambda c, d: 0.5 * c - d, convect, damping)
    for i in range(5):
        for j in range(i):
            lower[i][j] = lower[j][i]
            upper[i][j] = upper[j][i]
    return damping, lower, upper, flux


def put_mat(ref, at, a, lead=()):
    for i in range(5):
        for j in range(5):
            ref[lead + (at + 5 * i + j,)] = a[i][j]


def get_mat(ref, at, lead=()):
    return [[ref[lead + (at + 5 * i + j,)] for j in range(5)] for i in range(5)]


def put_vec(ref, at, x, lead=()):
    for i in range(5):
        ref[lead + (at + i,)] = x[i]


def get_vec(ref, at, lead=()):
    return [ref[lead + (at + i,)] for i in range(5)]


class Line:
    def __init__(self, dim):
        self.dim = dim
        self.n = TILE[dim]
        self.count = self.n // 4
        self.at = lax.broadcasted_iota(jnp.int32, TILE, dim)
        self.even1 = (self.at & 1) == 0
        self.even2 = (self.at & 2) == 0
        self.inner = self.at < self.n - 2
        self.group = self.at >> 2

    def roll(self, x, by):
        if isinstance(by, int):
            by = by % self.n
            if by == 0:
                return x
        return pltpu.roll(x, by, self.dim)

    def vroll(self, v, by):
        return [self.roll(x, by) for x in v]

    def mroll(self, m, by):
        return [self.vroll(row, by) for row in m]

    def pack1(self, a, b):
        first = jnp.where(self.even1, a, self.roll(b, 1))
        second = jnp.where(self.even1, self.roll(a, -1), b)
        return first, second

    def unpack1(self, first, second):
        a = jnp.where(self.even1, first, self.roll(second, 1))
        b = jnp.where(self.even1, self.roll(first, -1), second)
        return a, b

    def pack2(self, a, b):
        first = jnp.where(self.even2, a, self.roll(b, 2))
        second = jnp.where(self.even2, self.roll(a, -2), b)
        return first, second

    def unpack2(self, first, second):
        a = jnp.where(self.even2, first, self.roll(second, 2))
        b = jnp.where(self.even2, self.roll(first, -2), second)
        return a, b


def line_faces(line, cells_e, cells_o):
    after_e = face_values(cells_e, cells_o)
    nexts = [line.roll(x, -2) for x in cells_e[:7]]
    after_o = face_values(cells_o, nexts)
    return after_e, after_o


def first_level(line, after_e, after_o, keep_ref, t):
    damp_e, low_e, upp_e, _ = after_e
    damp_o, low_o, upp_o, _ = after_o
    inverse = mat_inv(plus_eye(mat_add(damp_e, damp_o)))
    w_low = mat_mul(inverse, low_e)
    w_upp = mat_mul(inverse, upp_o)
    put_mat(keep_ref, 0, inverse, (t,))
    put_mat(keep_ref, 25, upp_e, (t,))
    put_mat(keep_ref, 50, low_o, (t,))
    put_mat(keep_ref, 75, w_low, (t,))
    put_mat(keep_ref, 100, w_upp, (t,))
    inner = line.inner
    low = mat_map(lambda x, y: jnp.where(inner, -x, y), mat_mul(low_o, w_low), low_e)
    mid_l = mat_map(
        lambda x, y, z: jnp.where(inner, y - x, z), mat_mul(low_o, w_upp), damp_o, damp_e
    )
    upp = mat_map(lambda x, y: jnp.where(inner, -x, y), mat_mul(upp_e, w_upp), upp_e)
    mid_r = mat_map(
        lambda x, y: jnp.where(inner, y - x, y), mat_mul(upp_e, w_low), plus_eye(damp_e)
    )
    return line.mroll(low, 2), line.mroll(mid_l, 2), mid_r, upp


def second_level(line, level_a, level_b, keep_ref):
    packed = [
        [[line.pack2(x, y) for x, y in zip(ra, rb)] for ra, rb in zip(ma, mb)]
        for ma, mb in zip(level_a, level_b)
    ]
    evens = [mat_map(lambda p: p[0], m) for m in packed]
    odds = [mat_map(lambda p: p[1], m) for m in packed]
    inverse = mat_inv(mat_add(odds[1], odds[2]))
    w_low = mat_mul(inverse, odds[0])
    w_upp = mat_mul(inverse, odds[3])
    put_mat(keep_ref, 0, inverse)
    put_mat(keep_ref, 25, evens[3])
    put_mat(keep_ref, 50, evens[0])
    put_mat(keep_ref, 75, w_low)
    put_mat(keep_ref, 100, w_upp)
    left_low = line.mroll(w_low, 4)
    left_upp = line.mroll(w_upp, 4)
    low = mat_neg(mat_mul(evens[0], left_low))
    mid_l = mat_sub(evens[1], mat_mul(evens[0], left_upp))
    mid_r = mat_sub(evens[2], mat_mul(evens[3], w_low))
    upp = mat_neg(mat_mul(evens[3], w_upp))
    return low, mid_l, mid_r, upp


def later_level(line, low, mid_l, mid_r, upp, reach, keep_ref, level):
    left_ok = (line.group > reach) | (line.group == 0)
    right_ok = line.group + reach < line.count
    inverse = mat_inv(mat_add(mid_l, mid_r))
    w_low = mat_mul(inverse, low)
    w_upp = mat_mul(inverse, upp)
    low_in = mat_map(lambda x: jnp.where(left_ok, x, 0.0), low)
    upp_in = mat_map(lambda x: jnp.where(right_ok, x, 0.0), upp)
    put_mat(keep_ref, 0, inverse, (level,))
    put_mat(keep_ref, 25, low_in, (level,))
    put_mat(keep_ref, 50, upp_in, (level,))
    back = 4 * reach
    ahead = line.n - 4 * reach
    left_low, left_upp = line.mroll(w_low, back), line.mroll(w_upp, back)
    right_low, right_upp = line.mroll(w_low, ahead), line.mroll(w_upp, ahead)
    new_low = mat_map(
        lambda x, y: jnp.where(left_ok, -x, y), mat_mul(low_in, left_low), low
    )
    new_mid_l = mat_sub(mid_l, mat_mul(low_in, left_upp))
    new_upp = mat_map(
        lambda x, y: jnp.where(right_ok, -x, y), mat_mul(upp_in, right_upp), upp
    )
    new_mid_r = mat_sub(mid_r, mat_mul(upp_in, right_low))
    return new_low, new_mid_l, new_mid_r, new_upp


def line_levels(line, states, keep1, keep2, keep3, ends, work):
    low, mid_l, mid_r, upp = second_level(line, states[0], states[1], keep2)
    steps = line.count.bit_length() - 1
    if steps == 1:
        low, mid_l, mid_r, upp = later_level(line, low, mid_l, mid_r, upp, 1, keep3, 0)
    else:
        for at, m in enumerate((low, mid_l, mid_r, upp)):
            put_mat(work, 25 * at, m)

        def body(level, carry):
            now = [get_mat(work, 25 * at) for at in range(4)]
            reach = lax.shift_left(jnp.int32(1), level)
            new = later_level(line, *now, reach, keep3, level)
            for at, m in enumerate(new):
                put_mat(work, 25 * at, m)
            return carry

        lax.fori_loop(0, steps, body, 0)
        low, mid_l, mid_r, upp = (get_mat(work, 25 * at) for at in range(4))
    for at, m in enumerate((low, mid_l, mid_r, upp)):
        put_mat(ends, 25 * at, m)


def line_forward(line, rhs_e, rhs_o, keep1, keep2, keep3, zs):
    right, left = [], []
    for t in range(2):
        z = mat_vec(get_mat(keep1, 0, (t,)), rhs_o[t])
        put_vec(zs, 5 * t, z)
        from_r = mat_vec(get_mat(keep1, 25, (t,)), z)
        from_l = mat_vec(get_mat(keep1, 50, (t,)), z)
        right.append(
            vec_map(lambda r, x: jnp.where(line.inner, r - x, r), rhs_e[t], from_r)
        )
        left.append(
            line.vroll(vec_map(lambda r, x: jnp.where(line.inner, -x, r), rhs_o[t], from_l), 2)
        )
    pair_r = [line.pack2(x, y) for x, y in zip(right[0], right[1])]
    pair_l = [line.pack2(x, y) for x, y in zip(left[0], left[1])]
    odd = [x[1] + y[1] for x, y in zip(pair_r, pair_l)]
    z = mat_vec(get_mat(keep2, 0), odd)
    put_vec(zs, 10, z)
    r_r = vec_sub([x[0] for x in pair_r], mat_vec(get_mat(keep2, 25), z))
    r_l = vec_sub([x[0] for x in pair_l], mat_vec(get_mat(keep2, 50), line.vroll(z, 4)))
    steps = line.count.bit_length() - 1
    for level in range(steps):
        z = mat_vec(get_mat(keep3, 0, (level,)), vec_add(r_l, r_r))
        back = 4 << level
        r_l = vec_sub(r_l, mat_vec(get_mat(keep3, 25, (level,)), line.vroll(z, back)))
        r_r = vec_sub(r_r, mat_vec(get_mat(keep3, 50, (level,)), line.vroll(z, -back)))
    put_vec(zs, 15, vec_add(r_l, r_r))
    return r_r, r_l


def line_backward(line, first, last, keep1, keep2, tail, zs):
    inner = vec_sub(
        mat_vec(get_mat(tail, 0), get_vec(zs, 15)),
        vec_add(mat_vec(get_mat(tail, 25), first), mat_vec(get_mat(tail, 50), last)),
    )
    even = vec_map(lambda x, y: jnp.where(line.group == 0, y, x), inner, first)
    ahead = vec_map(
        lambda x, y: jnp.where(line.at >= line.n - 4, y, x), line.vroll(even, -4), last
    )
    odd = vec_sub(
        get_vec(zs, 10),
        vec_add(
            mat_vec(get_mat(keep2, 75), even), mat_vec(get_mat(keep2, 100), ahead)
        ),
    )
    pairs = [line.unpack2(x, y) for x, y in zip(even, odd)]
    out = []
    for t in range(2):
        even = [p[t] for p in pairs]
        ends = line.vroll(last, 2) if t == 0 else last
        ahead = line.vroll(even, -2)
        odd = vec_sub(
            get_vec(zs, 5 * t),
            vec_add(
                mat_vec(get_mat(keep1, 75, (t,)), even),
                mat_vec(get_mat(keep1, 100, (t,)), ahead),
            ),
        )
        odd = vec_map(lambda x, y: jnp.where(line.inner, x, y), odd, ends)
        spans = [line.unpack1(x, y) for x, y in zip(even, odd)]
        out.append([s[0] for s in spans])
        out.append([s[1] for s in spans])
    return out


def tail_kernel(ends, after, tail):
    low, mid_l, mid_r, upp = (get_mat(ends, 25 * at) for at in range(4))
    inverse = mat_inv(mat_add(mid_l, mid_r))
    put_mat(tail, 0, inverse)
    put_mat(tail, 25, mat_mul(inverse, low))
    put_mat(tail, 50, mat_mul(inverse, upp))


def odd_device(axis):
    return (lax.axis_index(axis) & 1) == 1


def either(flag, a, b):
    return jnp.where(flag, a, b)


def split_cells(cells):
    return cells.at[0:5], cells.at[5:9], cells.at[9], cells.at[10:12]


def enter_kernel(cells, pair, cross):
    state, metrics, step, spread = split_cells(cells)
    odd = odd_device("normal")

    def send(c, s, rows):
        first, last = rows(0), rows(7)
        pair[c, s : s + 1, :] = either(odd, first, last)
        cross[c, s : s + 1, :] = either(odd, last, first)

    for s in range(4):
        for c in range(5):
            send(c, s, lambda k: state[c, s, k : k + 1, :])
        for c in range(2):
            send(5 + c, s, lambda k: metrics[2 + c, s, k : k + 1, :])
        send(7, s, lambda k: step[s, k : k + 1, :])
        send(8, s, lambda k: spread[1, s, k : k + 1, :])


def load_cells(line, state, metrics, step, spread, t, metric_at, spread_at):
    first, second = 2 * t, 2 * t + 1
    pairs = [(state[c, first], state[c, second]) for c in range(5)]
    pairs += [(metrics[metric_at + c, first], metrics[metric_at + c, second]) for c in range(2)]
    pairs += [(step[first], step[second]), (spread[spread_at, first], spread[spread_at, second])]
    packed = [line.pack1(a, b) for a, b in pairs]
    return [p[0] for p in packed], [p[1] for p in packed]


def line_residual(line, after_e, after_o):
    flux_e, flux_o = after_e[3], after_o[3]
    flux_o = vec_map(lambda x: jnp.where(line.inner, x, 0.0), flux_o)
    return vec_sub(line.vroll(flux_o, 2), flux_e), vec_sub(flux_e, flux_o)


def wrap_kernel(cells, keep1, keep2, keep3, rhs, note, ends, work):
    state, metrics, step, spread = split_cells(cells)
    line = Line(1)
    states = []
    note[...] = jnp.zeros_like(note)
    packed = [jnp.zeros(TILE, jnp.float32) for _ in range(4)]
    lane_group = line.group
    for t in range(2):
        cells_e, cells_o = load_cells(line, state, metrics, step, spread, t, 0, 0)
        pick = line.at & 3
        mine = (pick >> 1) == t
        for c in range(9):
            k, g = divmod(100 + c, 32)
            moved = line.roll(cells_o[c], 4 * g + 2 * t - (line.n - 2))
            packed[k] = jnp.where((lane_group == g) & mine, moved, packed[k])
        for c in range(7):
            k, g = divmod(109 + c, 32)
            moved = line.roll(cells_e[c], 4 * g + 2 * t)
            packed[k] = jnp.where((lane_group == g) & mine, moved, packed[k])
        after_e, after_o = line_faces(line, cells_e, cells_o)
        rhs_e, rhs_o = line_residual(line, after_e, after_o)
        put_vec(rhs, 0, rhs_e, (t,))
        put_vec(rhs, 5, rhs_o, (t,))
        states.append(first_level(line, after_e, after_o, keep1, t))
    line_levels(line, states, keep1, keep2, keep3, ends, work)
    for place, at in enumerate((50, 75, 0, 25)):
        for c in range(25):
            k, g = divmod(25 * place + c, 32)
            packed[k] = jnp.where(lane_group == g, line.roll(ends[at + c], 4 * g), packed[k])
    for k in range(4):
        note[k] = packed[k]


def put_face(ref, lead, face):
    for which in range(3):
        at = 0
        for i in range(5):
            for j in range(i, 5):
                ref[lead + (15 * which + at,)] = face[which][i][j]
                at += 1


def get_face(ref, lead):
    out = []
    for which in range(3):
        m = [[None] * 5 for _ in range(5)]
        at = 0
        for i in range(5):
            for j in range(i, 5):
                m[i][j] = m[j][i] = ref[lead + (15 * which + at,)]
                at += 1
        out.append(m)
    return out + [None]


def wall_faces_kernel(cells, coefs, rhs):
    state, metrics, step, spread = split_cells(cells)
    line = Line(0)
    for t in range(2):
        cells_e, cells_o = load_cells(line, state, metrics, step, spread, t, 2, 1)
        after_e, after_o = line_faces(line, cells_e, cells_o)
        rhs_e, rhs_o = line_residual(line, after_e, after_o)
        for c in range(5):
            a, b = line.unpack1(rhs_e[c], rhs_o[c])
            rhs[2 * t, c] = a
            rhs[2 * t + 1, c] = b
        for half, face in enumerate((after_e, after_o)):
            put_face(coefs, (t, half), face)


def edge_faces(pair, cross, from_pair, from_cross):
    odd = odd_device("normal")
    left, right = [], []
    for c in range(9):
        below = either(odd, from_pair[c], from_cross[c])
        own = either(odd, cross[c], pair[c])
        left.append(jnp.concatenate([below, own], axis=0))
    for c in range(7):
        above = either(odd, from_cross[c], from_pair[c])
        own = either(odd, pair[c], cross[c])
        right.append(jnp.concatenate([own, above], axis=0))
    return face_values(left, right)


def wall_kernel(coefs, edge, keep1, keep2, keep3, ends, close, segment):
    line = Line(0)
    states = []
    for t in range(2):
        after_e, after_o = get_face(coefs, (t, 0)), get_face(coefs, (t, 1))
        states.append(first_level(line, after_e, after_o, keep1, t))
    line_levels(line, states, keep1, keep2, keep3, ends, None)
    damp_f, low_f, upp_f, _ = get_face(edge, ())
    low, mid_l, mid_r, upp = (get_mat(ends, 25 * at) for at in range(4))
    inverse = mat_inv(plus_eye(mat_add(mid_l, damp_f)))
    w_low = mat_mul(inverse, low)
    w_upp = mat_mul(inverse, upp_f)
    put_mat(close, 0, inverse)
    put_mat(close, 25, upp)
    put_mat(close, 50, low_f)
    put_mat(close, 75, w_low)
    put_mat(close, 100, w_upp)
    mid_r = mat_sub(mid_r, mat_mul(upp, w_low))
    upp = mat_neg(mat_mul(upp, w_upp))
    low = mat_neg(mat_mul(low_f, w_low))
    mid_l = mat_sub(damp_f, mat_mul(low_f, w_upp))
    for at, m in enumerate((mid_r, upp, low, mid_l)):
        put_mat(segment, 25 * at, mat_map(lambda x: x[0:4], m))


def segment_mats(ref):
    return [get_mat(ref, 25 * at) for at in range(4)]


def tree_bit(level):
    return ((lax.axis_index("normal") >> level) & 1) == 1


def merge_kernel(*refs, level, last):
    node, result = refs[-2:]
    if level == 0:
        lower, upper = segment_mats(refs[0].at[0]), segment_mats(refs[0].at[1])
    else:
        upside = tree_bit(level)
        mine, theirs = segment_mats(refs[0]), segment_mats(refs[1])
        lower = [mat_map(lambda a, b: either(upside, b, a), m, t) for m, t in zip(mine, theirs)]
        upper = [mat_map(lambda a, b: either(upside, a, b), m, t) for m, t in zip(mine, theirs)]
    inverse = mat_inv(mat_add(lower[3], upper[0]))
    w_low = mat_mul(inverse, lower[2])
    up_in = mat_mul(lower[1], inverse)
    low_in = mat_mul(upper[2], inverse)
    w_upp = mat_mul(inverse, upper[1])
    for at, m in enumerate((inverse, up_in, low_in, w_low, w_upp)):
        put_mat(node, 25 * at, m)
    mid_r = mat_sub(lower[0], mat_mul(lower[1], w_low))
    upp = mat_neg(mat_mul(lower[1], w_upp))
    low = mat_neg(mat_mul(upper[2], w_low))
    mid_l = mat_sub(upper[3], mat_mul(upper[2], w_upp))
    if last:
        top = tree_bit(level + 1)
        first = mat_inv(mid_r)
        through = mat_mul(low, first)
        core = mat_map(
            lambda a, b: either(top, a, b), mid_r, mat_sub(mid_l, mat_mul(through, upp))
        )
        parts = (core, through, first, upp)
    else:
        parts = (mid_r, upp, low, mid_l)
    for at, m in enumerate(parts):
        put_mat(result, 25 * at, m)


def merge_loads(upside, up_in, low_in, mine, theirs):
    lower = [vec_map(lambda a, b: either(upside, b, a), m, t) for m, t in zip(mine, theirs)]
    upper = [vec_map(lambda a, b: either(upside, a, b), m, t) for m, t in zip(mine, theirs)]
    load = vec_add(lower[1], upper[0])
    right = vec_sub(lower[0], mat_vec(up_in, load))
    left = vec_sub(upper[1], mat_vec(low_in, load))
    return load, (right, left)


def in_order(position, count):
    def pick(values, q):
        ks = sorted({c ^ ((c + q) % count) for c in range(count)})
        wanted = position ^ ((position + q) % count)
        out = values[ks[0]]
        for k in ks[1:]:
            out = jnp.where(wanted == k, values[k], out)
        return out

    return pick


def wrap_rhs_kernel(
    pair, cross, from_pair, from_cross, rhs_wall, rhs_wrap, note, keep1, keep2, keep3, zs, sent, edge
):
    line, wall = Line(1), Line(0)
    face = edge_faces(pair, cross, from_pair, from_cross)
    through = face[3]
    put_face(edge, (), [mat_map(lambda x: wall.roll(x, 4), m) for m in face[:3]])
    rhs_e, rhs_o = [], []
    for t in range(2):
        spans = []
        for s in (2 * t, 2 * t + 1):
            values = []
            for c in range(5):
                x = rhs_wall[s, c]
                x = jnp.where(wall.at == 0, x + wall.roll(through[c], -s), x)
                x = jnp.where(wall.at == 7, x - wall.roll(through[c], 3 - s), x)
                values.append(x)
            spans.append(values)
        packed = [line.pack1(a, b) for a, b in zip(*spans)]
        rhs_e.append([packed[c][0] + rhs_wrap[t, c] for c in range(5)])
        rhs_o.append([packed[c][1] + rhs_wrap[t, 5 + c] for c in range(5)])
    r_r, r_l = line_forward(line, rhs_e, rhs_o, keep1, keep2, keep3, zs)
    for k in range(3):
        sent[k] = note[k]
    tail = note[3]
    for c in range(10):
        g = 116 + c - 96
        value = r_r[c] if c < 5 else r_l[c - 5]
        tail = jnp.where(line.group == g, line.roll(value, 4 * g), tail)
    sent[3] = tail


def cycle_kernel(*refs, count):
    arrived = refs[:count]
    (keep1, keep2, tail, zs, wkeep1, wkeep2, wkeep3, close) = refs[count : count + 8]
    sent, wzs, closed = refs[count + 8 :]
    pick = in_order(lax.axis_index("wrap"), count)
    notes = [
        [pick([ref[k] for ref in arrived], q) for k in range(4)] for q in range(count)
    ]
    line = Line(1)
    period = 4 * count
    repeat = line.at % period
    channels = [None] * 126
    for k in range(4):
        rolled = [line.roll(notes[q][k], 4 * q) for q in range(count)]
        for a in range(count):
            which = (line.group - a) % count
            mixed = rolled[0]
            for q in range(1, count):
                mixed = jnp.where(which == q, rolled[q], mixed)
            for c in range(a, 32, count):
                if 32 * k + c < 126:
                    index = (repeat + 4 * c) & (LANES - 1)
                    channels[32 * k + c] = jnp.take_along_axis(mixed, index, axis=1)

    def mat_at(at):
        return [[channels[at + 5 * i + j] for j in range(5)] for i in range(5)]

    mid_r, upp, low, mid_l = (mat_at(25 * i) for i in range(4))
    left = channels[100:109]
    right = line.vroll(channels[109:116], -4)
    r_r, r_l = channels[116:121], channels[121:126]
    damp_f, low_f, upp_f, flux = face_values(left, right)
    inverse = mat_inv(plus_eye(mat_add(mid_l, damp_f)))
    w_low = mat_mul(inverse, low)
    w_upp = mat_mul(inverse, upp_f)
    zb = mat_vec(inverse, vec_sub(r_l, flux))
    mid = mat_add(
        mat_sub(mid_r, mat_mul(upp, w_low)),
        line.mroll(mat_sub(damp_f, mat_mul(low_f, w_upp)), 4),
    )
    ahead = mat_neg(mat_mul(upp, w_upp))
    back = mat_neg(line.mroll(mat_mul(low_f, w_low), 4))
    load = vec_add(
        vec_sub(r_r, mat_vec(upp, zb)), line.vroll(vec_sub(flux, mat_vec(low_f, zb)), 4)
    )
    reach = 1
    while 2 * reach < count:
        inverse = mat_inv(mid)
        wb, wa, z = mat_mul(inverse, back), mat_mul(inverse, ahead), mat_vec(inverse, load)
        by = 4 * reach
        mid = mat_sub(
            mid,
            mat_add(
                mat_mul(back, line.mroll(wa, by)), mat_mul(ahead, line.mroll(wb, -by))
            ),
        )
        load = vec_sub(
            load,
            vec_add(mat_vec(back, line.vroll(z, by)), mat_vec(ahead, line.vroll(z, -by))),
        )
        back, ahead = (
            mat_neg(mat_mul(back, line.mroll(wb, by))),
            mat_neg(mat_mul(ahead, line.mroll(wa, -by))),
        )
        reach *= 2
    both = mat_add(back, ahead)
    inverse = mat_inv(mid)
    w, z = mat_mul(inverse, both), mat_vec(inverse, load)
    by = 4 * reach
    mid = mat_sub(mid, mat_mul(both, line.mroll(w, by)))
    load = vec_sub(load, mat_vec(both, line.vroll(z, by)))
    x = mat_vec(mat_inv(mid), load)
    b = vec_sub(zb, vec_add(mat_vec(w_low, x), mat_vec(w_upp, line.vroll(x, -4))))
    spread = line.at & 3
    first = [jnp.take_along_axis(y, spread, axis=1) for y in x]
    last = [jnp.take_along_axis(y, spread, axis=1) for y in b]
    swept = line_backward(line, first, last, keep1, keep2, tail, zs)

    wall = Line(0)
    rhs_e, rhs_o = [], []
    for t in range(2):
        packed = [wall.pack1(p, q) for p, q in zip(swept[2 * t], swept[2 * t + 1])]
        rhs_e.append([p[0] for p in packed])
        rhs_o.append([p[1] for p in packed])
    r_r, r_l = line_forward(wall, rhs_e, rhs_o, wkeep1, wkeep2, wkeep3, wzs)
    zb = mat_vec(get_mat(close, 0), r_l)
    put_vec(closed, 0, zb)
    out_r = vec_sub(r_r, mat_vec(get_mat(close, 25), zb))
    out_l = vec_map(lambda y: -y, mat_vec(get_mat(close, 50), zb))
    put_vec(sent, 0, [y[0:4] for y in out_r])
    put_vec(sent, 5, [y[0:4] for y in out_l])


def joint_rhs_kernel(own, other, node, *refs, level, last):
    mine = (get_vec(own, 0), get_vec(own, 5))
    theirs = (get_vec(other, 0), get_vec(other, 5))
    load, (right, left) = merge_loads(
        tree_bit(level), get_mat(node, 25), get_mat(node, 50), mine, theirs
    )
    if not last:
        middle, sent = refs
        put_vec(middle, 0, mat_vec(get_mat(node, 0), load))
        put_vec(sent, 0, right)
        put_vec(sent, 5, left)
        return
    half, middle, sent = refs
    put_vec(middle, 0, mat_vec(get_mat(node, 0), load))
    put_vec(middle, 5, right)
    top = tree_bit(level + 1)
    closed = vec_sub(left, mat_vec(get_mat(half, 25), right))
    for c in range(25):
        sent[c] = half[c]
    put_vec(sent, 25, vec_map(lambda a, b: either(top, a, b), right, closed))


def mat_solve(matrix, load):
    a = [list(row) + [x] for row, x in zip(matrix, load)]
    for k in range(5):
        over = 1.0 / a[k][k]
        for j in range(k + 1, 6):
            a[k][j] = a[k][j] * over
        for i in range(k + 1, 5):
            for j in range(k + 1, 6):
                a[i][j] = a[i][j] - a[i][k] * a[k][j]
    x = [None] * 5
    for i in reversed(range(5)):
        total = a[i][5]
        for j in range(i + 1, 5):
            total = total - a[i][j] * x[j]
        x[i] = total
    return x


def finish_kernel(own, other, half, *refs, levels):
    nodes, middles = refs[: levels - 1], refs[levels - 1 : 2 * levels - 2]
    (keep1, keep2, tail, close, closed, zs, field) = refs[2 * levels - 2 :]
    line = Line(0)
    between = mat_solve(
        mat_add(get_mat(own, 0), get_mat(other, 0)),
        vec_add(get_vec(own, 25), get_vec(other, 25)),
    )
    below = mat_vec(
        get_mat(half, 50),
        vec_sub(get_vec(middles[-1], 5), mat_vec(get_mat(half, 75), between)),
    )
    top = tree_bit(levels - 1)
    below, above = (
        vec_map(lambda a, b: either(top, b, a), below, between),
        vec_map(lambda b: either(top, 0.0, b), between),
    )
    for level in reversed(range(levels - 1)):
        node = nodes[level]
        between = vec_sub(
            get_vec(middles[level], 0),
            vec_add(mat_vec(get_mat(node, 75), below), mat_vec(get_mat(node, 100), above)),
        )
        upside = tree_bit(level)
        below, above = (
            vec_map(lambda a, b: either(upside, b, a), below, between),
            vec_map(lambda a, b: either(upside, b, a), between, above),
        )
    first, nexts = below, above
    first = [jnp.concatenate([x, x], axis=0) for x in first]
    nexts = [jnp.concatenate([x, x], axis=0) for x in nexts]
    last = vec_sub(
        get_vec(closed, 0),
        vec_add(mat_vec(get_mat(close, 75), first), mat_vec(get_mat(close, 100), nexts)),
    )
    last = [jnp.where(line.at < 4, x, line.roll(x, 4)) for x in last]
    out = line_backward(line, first, last, keep1, keep2, tail, zs)
    for s in range(4):
        for c in range(5):
            field[c, s] = out[s][c]


def call(kernel, name, shapes, flops, *args, scratch=()):
    place = pl.BlockSpec(memory_space=pltpu.VMEM)
    return pl.pallas_call(
        kernel,
        name=name,
        out_shape=[jax.ShapeDtypeStruct(s, jnp.float32) for s in shapes],
        in_specs=[pl.BlockSpec(memory_space=pltpu.VMEM)] * len(args),
        out_specs=[place] * len(shapes),
        scratch_shapes=[
            pltpu.VMEM(s, jnp.float32) if isinstance(s, tuple) else s for s in scratch
        ],
        compiler_params=pltpu.CompilerParams(vmem_limit_bytes=VMEM_LIMIT),
        cost_estimate=pl.CostEstimate(flops=flops, bytes_accessed=1 << 20, transcendentals=0),
    )(*args)


def swapped(x, axis, count, by):
    return lax.ppermute(x, axis, [(i, i ^ by) for i in range(count)])


def on_device(state, metrics, time_step, dissipation, *, wrap_count, wall_count):
    levels = wall_count.bit_length() - 1
    row = (4, LANES)
    cells = jnp.concatenate([state, metrics, time_step[None], dissipation], axis=0)
    pair, cross = call(enter_kernel, "enter", [(9,) + row, (9,) + row], 1 << 12, cells)
    across = [(i, i + 1) for i in range(1, wall_count - 1, 2)]
    across += [(b, a) for a, b in across]
    from_pair = swapped(pair, "normal", wall_count, 1)
    from_cross = lax.ppermute(cross, "normal", across)
    coefs, rhs_wall = call(
        wall_faces_kernel, "wall_faces", [(2, 2, 45) + TILE, (4, 5) + TILE], 8 << 20, cells
    )
    keep1, keep2, keep3, rhs_wrap, note, ends = call(
        wrap_kernel,
        "wrap",
        [
            (2, 125) + TILE,
            (125,) + TILE,
            (5, 75) + TILE,
            (2, 10) + TILE,
            (4,) + TILE,
            (100,) + TILE,
        ],
        40 << 20,
        cells,
        scratch=[(100,) + TILE],
    )
    zs, own, edge = call(
        wrap_rhs_kernel,
        "wrap_rhs",
        [(20,) + TILE, (4,) + TILE, (45,) + TILE],
        8 << 20,
        pair,
        cross,
        from_pair,
        from_cross,
        rhs_wall,
        rhs_wrap,
        note,
        keep1,
        keep2,
        keep3,
    )
    notes = [own] + [None] * (wrap_count - 1)
    for k in [1, 3, 2] + list(range(4, wrap_count)):
        notes[k] = swapped(own, "wrap", wrap_count, k)
    wkeep1, wkeep2, wkeep3, wends, close, segment = call(
        wall_kernel,
        "wall",
        [
            (2, 125) + TILE,
            (125,) + TILE,
            (1, 75) + TILE,
            (100,) + TILE,
            (125,) + TILE,
            (100,) + row,
        ],
        20 << 20,
        coefs,
        edge,
    )
    joined = [
        lax.all_gather(
            segment, "normal", axis_index_groups=[[i, i + 1] for i in range(0, wall_count, 2)]
        )
    ]
    (tail,) = call(tail_kernel, "tail", [(75,) + TILE], 3 << 20, ends, own)
    sent, wzs, closed = call(
        lambda *refs: cycle_kernel(*refs, count=wrap_count),
        "cycle",
        [(10,) + row, (20,) + TILE, (5,) + TILE],
        10 << 20,
        *notes,
        keep1,
        keep2,
        tail,
        zs,
        wkeep1,
        wkeep2,
        wkeep3,
        close,
    )
    nodes = []
    for level in range(levels - 1):
        last = level == levels - 2
        node, result = call(
            lambda *refs: merge_kernel(*refs, level=level, last=last),
            "merge_%d" % level,
            [(125,) + row, (100,) + row],
            4 << 20,
            *joined,
            *(notes[1:] if level == 0 else []),
        )
        nodes.append(node)
        if not last:
            joined = [result, swapped(result, "normal", wall_count, 2 << level)]
    middles = []
    for level in range(levels - 1):
        last = level == levels - 2
        partner = swapped(sent, "normal", wall_count, 1 << level)
        middle, sent = call(
            lambda *refs: joint_rhs_kernel(*refs, level=level, last=last),
            "joint_rhs_%d" % level,
            [(10 if last else 5,) + row, (30 if last else 10,) + row],
            1 << 16,
            sent,
            partner,
            nodes[level],
            *([result] if last else []),
        )
        middles.append(middle)
    (wtail,) = call(tail_kernel, "wall_tail", [(75,) + TILE], 3 << 20, wends, sent)
    partner = swapped(sent, "normal", wall_count, 1 << (levels - 1))
    (field,) = call(
        lambda *refs: finish_kernel(*refs, levels=levels),
        "finish",
        [(5, 4) + TILE],
        4 << 20,
        sent,
        partner,
        result,
        *nodes,
        *middles,
        wkeep1,
        wkeep2,
        wtail,
        close,
        closed,
        wzs,
    )
    return field


def solution(mesh):
    placed = (
        P(None, None, "normal", "wrap"),
        P(None, None, "normal", "wrap"),
        P(None, "normal", "wrap"),
        P(None, None, "normal", "wrap"),
    )

    def body(state, metrics, time_step, dissipation):
        return on_device(
            state,
            metrics,
            time_step,
            dissipation,
            wrap_count=mesh.shape["wrap"],
            wall_count=mesh.shape["normal"],
        )

    return jax.shard_map(
        body,
        mesh=mesh,
        in_specs=placed,
        out_specs=P(None, None, "normal", "wrap"),
        check_vma=False,
    )
```

```python
import jax
import jax.numpy as jnp
from jax import lax
from jax.experimental import pallas as pl
from jax.experimental.pallas import tpu as pltpu
from jax.sharding import PartitionSpec as P

GAMMA = 1.4
LESS = GAMMA - 1.0
VMEM_LIMIT = 16 * 1024 * 1024
TILE = (8, 128)
LANES = 128


def mat_mul(a, b):
    out = []
    for i in range(5):
        row = []
        for j in range(5):
            total = a[i][0] * b[0][j]
            for k in range(1, 5):
                total = total + a[i][k] * b[k][j]
            row.append(total)
        out.append(row)
    return out


def mat_vec(a, x):
    out = []
    for i in range(5):
        total = a[i][0] * x[0]
        for k in range(1, 5):
            total = total + a[i][k] * x[k]
        out.append(total)
    return out


def mat_map(fn, *mats):
    return [[fn(*(m[i][j] for m in mats)) for j in range(5)] for i in range(5)]


def vec_map(fn, *vecs):
    return [fn(*(v[i] for v in vecs)) for i in range(5)]


def mat_add(a, b):
    return mat_map(lambda x, y: x + y, a, b)


def mat_sub(a, b):
    return mat_map(lambda x, y: x - y, a, b)


def mat_neg(a):
    return mat_map(lambda x: -x, a)


def vec_add(a, b):
    return vec_map(lambda x, y: x + y, a, b)


def vec_sub(a, b):
    return vec_map(lambda x, y: x - y, a, b)


def plus_eye(a):
    return [[a[i][j] + 1.0 if i == j else a[i][j] for j in range(5)] for i in range(5)]


def mat_inv(matrix):
    a = [list(row) for row in matrix]
    for k in range(5):
        pivot = 1.0 / a[k][k]
        row = [a[k][j] * pivot if j != k else pivot for j in range(5)]
        for i in range(5):
            if i == k:
                continue
            factor = a[i][k]
            for j in range(5):
                a[i][j] = -(factor * pivot) if j == k else a[i][j] - factor * row[j]
        a[k] = row
    return a


def face_values(left, right):
    state = [0.5 * (left[i] + right[i]) for i in range(5)]
    m1 = 0.5 * (left[5] + right[5])
    m2 = 0.5 * (left[6] + right[6])
    step, spread = left[7], left[8]
    over = 1.0 / state[0]
    u, v, w, e = (state[i] * over for i in range(1, 5))
    t = m1 * u + m2 * v
    f = (0.5 * LESS) * (u * u + v * v + w * w)
    h = GAMMA * e - f
    jac = [
        [None, m1, m2, None, None],
        [
            m1 * f - u * t,
            t - (GAMMA - 2.0) * m1 * u,
            m2 * u - LESS * m1 * v,
            -LESS * m1 * w,
            LESS * m1,
        ],
        [
            m2 * f - v * t,
            m1 * v - LESS * m2 * u,
            t - (GAMMA - 2.0) * m2 * v,
            -LESS * m2 * w,
            LESS * m2,
        ],
        [-w * t, m1 * w, m2 * w, t, None],
        [
            t * (2.0 * f - GAMMA * e),
            m1 * h - LESS * u * t,
            m2 * h - LESS * v * t,
            -LESS * w * t,
            GAMMA * t,
        ],
    ]
    widest = None
    for row in jac:
        total = None
        for x in row:
            if x is not None:
                total = jnp.abs(x) if total is None else total + jnp.abs(x)
        widest = total if widest is None else jnp.maximum(widest, total)
    scale = 1.0 / widest
    norm = [[None if x is None else x * scale for x in row] for row in jac]
    half_step = 0.5 * step
    weight = half_step * spread
    convect = [[None] * 5 for _ in range(5)]
    damping = [[None] * 5 for _ in range(5)]
    for i in range(5):
        for j in range(i, 5):
            parts = [x for x in (norm[i][j], norm[j][i]) if x is not None]
            if parts:
                c = half_step * (parts[0] + parts[1] if len(parts) == 2 else parts[0])
            else:
                c = jnp.zeros_like(step)
            total = None
            for k in range(5):
                if norm[k][i] is None or norm[k][j] is None:
                    continue
                term = norm[k][i] * norm[k][j]
                total = term if total is None else total + term
            if i == j:
                total = total + 1.0
            d = weight * total
            convect[i][j] = convect[j][i] = c
            damping[i][j] = damping[j][i] = d
    jump = [right[i] - left[i] for i in range(5)]
    flux = vec_sub(mat_vec(convect, state), mat_vec(damping, jump))
    lower = mat_map(lambda c, d: -0.5 * c - d, convect, damping)
    upper = mat_map(lambda c, d: 0.5 * c - d, convect, damping)
    for i in range(5):
        for j in range(i):
            lower[i][j] = lower[j][i]
            upper[i][j] = upper[j][i]
    return damping, lower, upper, flux


def put_mat(ref, at, a, lead=()):
    for i in range(5):
        for j in range(5):
            ref[lead + (at + 5 * i + j,)] = a[i][j]


def get_mat(ref, at, lead=()):
    return [[ref[lead + (at + 5 * i + j,)] for j in range(5)] for i in range(5)]


def put_vec(ref, at, x, lead=()):
    for i in range(5):
        ref[lead + (at + i,)] = x[i]


def get_vec(ref, at, lead=()):
    return [ref[lead + (at + i,)] for i in range(5)]


class Line:
    def __init__(self, dim):
        self.dim = dim
        self.n = TILE[dim]
        self.count = self.n // 4
        self.at = lax.broadcasted_iota(jnp.int32, TILE, dim)
        self.even1 = (self.at & 1) == 0
        self.even2 = (self.at & 2) == 0
        self.inner = self.at < self.n - 2
        self.group = self.at >> 2

    def roll(self, x, by):
        if isinstance(by, int):
            by = by % self.n
            if by == 0:
                return x
        return pltpu.roll(x, by, self.dim)

    def vroll(self, v, by):
        return [self.roll(x, by) for x in v]

    def mroll(self, m, by):
        return [self.vroll(row, by) for row in m]

    def pack1(self, a, b):
        first = jnp.where(self.even1, a, self.roll(b, 1))
        second = jnp.where(self.even1, self.roll(a, -1), b)
        return first, second

    def unpack1(self, first, second):
        a = jnp.where(self.even1, first, self.roll(second, 1))
        b = jnp.where(self.even1, self.roll(first, -1), second)
        return a, b

    def pack2(self, a, b):
        first = jnp.where(self.even2, a, self.roll(b, 2))
        second = jnp.where(self.even2, self.roll(a, -2), b)
        return first, second

    def unpack2(self, first, second):
        a = jnp.where(self.even2, first, self.roll(second, 2))
        b = jnp.where(self.even2, self.roll(first, -2), second)
        return a, b


def line_faces(line, cells_e, cells_o):
    after_e = face_values(cells_e, cells_o)
    nexts = [line.roll(x, -2) for x in cells_e[:7]]
    after_o = face_values(cells_o, nexts)
    return after_e, after_o


def first_level(line, after_e, after_o, keep_ref, t):
    damp_e, low_e, upp_e, _ = after_e
    damp_o, low_o, upp_o, _ = after_o
    inverse = mat_inv(plus_eye(mat_add(damp_e, damp_o)))
    w_low = mat_mul(inverse, low_e)
    w_upp = mat_mul(inverse, upp_o)
    put_mat(keep_ref, 0, inverse, (t,))
    put_mat(keep_ref, 25, upp_e, (t,))
    put_mat(keep_ref, 50, low_o, (t,))
    put_mat(keep_ref, 75, w_low, (t,))
    put_mat(keep_ref, 100, w_upp, (t,))
    inner = line.inner
    low = mat_map(lambda x, y: jnp.where(inner, -x, y), mat_mul(low_o, w_low), low_e)
    mid_l = mat_map(
        lambda x, y, z: jnp.where(inner, y - x, z), mat_mul(low_o, w_upp), damp_o, damp_e
    )
    upp = mat_map(lambda x, y: jnp.where(inner, -x, y), mat_mul(upp_e, w_upp), upp_e)
    mid_r = mat_map(
        lambda x, y: jnp.where(inner, y - x, y), mat_mul(upp_e, w_low), plus_eye(damp_e)
    )
    return line.mroll(low, 2), line.mroll(mid_l, 2), mid_r, upp


def second_level(line, level_a, level_b, keep_ref):
    packed = [
        [[line.pack2(x, y) for x, y in zip(ra, rb)] for ra, rb in zip(ma, mb)]
        for ma, mb in zip(level_a, level_b)
    ]
    evens = [mat_map(lambda p: p[0], m) for m in packed]
    odds = [mat_map(lambda p: p[1], m) for m in packed]
    inverse = mat_inv(mat_add(odds[1], odds[2]))
    w_low = mat_mul(inverse, odds[0])
    w_upp = mat_mul(inverse, odds[3])
    put_mat(keep_ref, 0, inverse)
    put_mat(keep_ref, 25, evens[3])
    put_mat(keep_ref, 50, evens[0])
    put_mat(keep_ref, 75, w_low)
    put_mat(keep_ref, 100, w_upp)
    left_low = line.mroll(w_low, 4)
    left_upp = line.mroll(w_upp, 4)
    low = mat_neg(mat_mul(evens[0], left_low))
    mid_l = mat_sub(evens[1], mat_mul(evens[0], left_upp))
    mid_r = mat_sub(evens[2], mat_mul(evens[3], w_low))
    upp = mat_neg(mat_mul(evens[3], w_upp))
    return low, mid_l, mid_r, upp


def later_level(line, low, mid_l, mid_r, upp, reach, keep_ref, level):
    left_ok = (line.group > reach) | (line.group == 0)
    right_ok = line.group + reach < line.count
    inverse = mat_inv(mat_add(mid_l, mid_r))
    w_low = mat_mul(inverse, low)
    w_upp = mat_mul(inverse, upp)
    low_in = mat_map(lambda x: jnp.where(left_ok, x, 0.0), low)
    upp_in = mat_map(lambda x: jnp.where(right_ok, x, 0.0), upp)
    put_mat(keep_ref, 0, inverse, (level,))
    put_mat(keep_ref, 25, low_in, (level,))
    put_mat(keep_ref, 50, upp_in, (level,))
    back = 4 * reach
    ahead = line.n - 4 * reach
    left_low, left_upp = line.mroll(w_low, back), line.mroll(w_upp, back)
    right_low, right_upp = line.mroll(w_low, ahead), line.mroll(w_upp, ahead)
    new_low = mat_map(
        lambda x, y: jnp.where(left_ok, -x, y), mat_mul(low_in, left_low), low
    )
    new_mid_l = mat_sub(mid_l, mat_mul(low_in, left_upp))
    new_upp = mat_map(
        lambda x, y: jnp.where(right_ok, -x, y), mat_mul(upp_in, right_upp), upp
    )
    new_mid_r = mat_sub(mid_r, mat_mul(upp_in, right_low))
    return new_low, new_mid_l, new_mid_r, new_upp


def line_levels(line, states, keep1, keep2, keep3, ends, work):
    low, mid_l, mid_r, upp = second_level(line, states[0], states[1], keep2)
    steps = line.count.bit_length() - 1
    if steps == 1:
        low, mid_l, mid_r, upp = later_level(line, low, mid_l, mid_r, upp, 1, keep3, 0)
    else:
        for at, m in enumerate((low, mid_l, mid_r, upp)):
            put_mat(work, 25 * at, m)

        def body(level, carry):
            now = [get_mat(work, 25 * at) for at in range(4)]
            reach = lax.shift_left(jnp.int32(1), level)
            new = later_level(line, *now, reach, keep3, level)
            for at, m in enumerate(new):
                put_mat(work, 25 * at, m)
            return carry

        lax.fori_loop(0, steps, body, 0)
        low, mid_l, mid_r, upp = (get_mat(work, 25 * at) for at in range(4))
    for at, m in enumerate((low, mid_l, mid_r, upp)):
        put_mat(ends, 25 * at, m)


def line_forward(line, rhs_e, rhs_o, keep1, keep2, keep3, zs):
    right, left = [], []
    for t in range(2):
        z = mat_vec(get_mat(keep1, 0, (t,)), rhs_o[t])
        put_vec(zs, 5 * t, z)
        from_r = mat_vec(get_mat(keep1, 25, (t,)), z)
        from_l = mat_vec(get_mat(keep1, 50, (t,)), z)
        right.append(
            vec_map(lambda r, x: jnp.where(line.inner, r - x, r), rhs_e[t], from_r)
        )
        left.append(
            line.vroll(vec_map(lambda r, x: jnp.where(line.inner, -x, r), rhs_o[t], from_l), 2)
        )
    pair_r = [line.pack2(x, y) for x, y in zip(right[0], right[1])]
    pair_l = [line.pack2(x, y) for x, y in zip(left[0], left[1])]
    odd = [x[1] + y[1] for x, y in zip(pair_r, pair_l)]
    z = mat_vec(get_mat(keep2, 0), odd)
    put_vec(zs, 10, z)
    r_r = vec_sub([x[0] for x in pair_r], mat_vec(get_mat(keep2, 25), z))
    r_l = vec_sub([x[0] for x in pair_l], mat_vec(get_mat(keep2, 50), line.vroll(z, 4)))
    steps = line.count.bit_length() - 1
    for level in range(steps):
        z = mat_vec(get_mat(keep3, 0, (level,)), vec_add(r_l, r_r))
        back = 4 << level
        r_l = vec_sub(r_l, mat_vec(get_mat(keep3, 25, (level,)), line.vroll(z, back)))
        r_r = vec_sub(r_r, mat_vec(get_mat(keep3, 50, (level,)), line.vroll(z, -back)))
    put_vec(zs, 15, vec_add(r_l, r_r))
    return r_r, r_l


def line_backward(line, first, last, keep1, keep2, tail, zs):
    inner = vec_sub(
        mat_vec(get_mat(tail, 0), get_vec(zs, 15)),
        vec_add(mat_vec(get_mat(tail, 25), first), mat_vec(get_mat(tail, 50), last)),
    )
    even = vec_map(lambda x, y: jnp.where(line.group == 0, y, x), inner, first)
    ahead = vec_map(
        lambda x, y: jnp.where(line.at >= line.n - 4, y, x), line.vroll(even, -4), last
    )
    odd = vec_sub(
        get_vec(zs, 10),
        vec_add(
            mat_vec(get_mat(keep2, 75), even), mat_vec(get_mat(keep2, 100), ahead)
        ),
    )
    pairs = [line.unpack2(x, y) for x, y in zip(even, odd)]
    for t in range(2):
        even = [p[t] for p in pairs]
        ends = line.vroll(last, 2) if t == 0 else last
        ahead = line.vroll(even, -2)
        odd = vec_sub(
            get_vec(zs, 5 * t),
            vec_add(
                mat_vec(get_mat(keep1, 75, (t,)), even),
                mat_vec(get_mat(keep1, 100, (t,)), ahead),
            ),
        )
        odd = vec_map(lambda x, y: jnp.where(line.inner, x, y), odd, ends)
        spans = [line.unpack1(x, y) for x, y in zip(even, odd)]
        yield [s[0] for s in spans], [s[1] for s in spans]


def tail_kernel(ends, after, tail):
    low, mid_l, mid_r, upp = (get_mat(ends, 25 * at) for at in range(4))
    inverse = mat_inv(mat_add(mid_l, mid_r))
    put_mat(tail, 0, inverse)
    put_mat(tail, 25, mat_mul(inverse, low))
    put_mat(tail, 50, mat_mul(inverse, upp))


def odd_device(axis):
    return (lax.axis_index(axis) & 1) == 1


def either(flag, a, b):
    return jnp.where(flag, a, b)


def split_cells(cells):
    return cells.at[0:5], cells.at[5:9], cells.at[9], cells.at[10:12]


def enter_kernel(cells, pair, cross):
    state, metrics, step, spread = split_cells(cells)
    odd = odd_device("normal")

    def send(c, s, rows):
        first, last = rows(0), rows(7)
        pair[c, s : s + 1, :] = either(odd, first, last)
        cross[c, s : s + 1, :] = either(odd, last, first)

    for s in range(4):
        for c in range(5):
            send(c, s, lambda k: state[c, s, k : k + 1, :])
        for c in range(2):
            send(5 + c, s, lambda k: metrics[2 + c, s, k : k + 1, :])
        send(7, s, lambda k: step[s, k : k + 1, :])
        send(8, s, lambda k: spread[1, s, k : k + 1, :])


def load_cells(line, state, metrics, step, spread, t, metric_at, spread_at):
    first, second = 2 * t, 2 * t + 1
    pairs = [(state[c, first], state[c, second]) for c in range(5)]
    pairs += [(metrics[metric_at + c, first], metrics[metric_at + c, second]) for c in range(2)]
    pairs += [(step[first], step[second]), (spread[spread_at, first], spread[spread_at, second])]
    packed = [line.pack1(a, b) for a, b in pairs]
    return [p[0] for p in packed], [p[1] for p in packed]


def line_residual(line, after_e, after_o):
    flux_e, flux_o = after_e[3], after_o[3]
    flux_o = vec_map(lambda x: jnp.where(line.inner, x, 0.0), flux_o)
    return vec_sub(line.vroll(flux_o, 2), flux_e), vec_sub(flux_e, flux_o)


def wrap_kernel(cells, keep1, keep2, keep3, rhs, note, ends, work):
    state, metrics, step, spread = split_cells(cells)
    line = Line(1)
    states = []
    note[...] = jnp.zeros_like(note)
    packed = [jnp.zeros(TILE, jnp.float32) for _ in range(4)]
    lane_group = line.group
    for t in range(2):
        cells_e, cells_o = load_cells(line, state, metrics, step, spread, t, 0, 0)
        pick = line.at & 3
        mine = (pick >> 1) == t
        for c in range(9):
            k, g = divmod(100 + c, 32)
            moved = line.roll(cells_o[c], 4 * g + 2 * t - (line.n - 2))
            packed[k] = jnp.where((lane_group == g) & mine, moved, packed[k])
        for c in range(7):
            k, g = divmod(109 + c, 32)
            moved = line.roll(cells_e[c], 4 * g + 2 * t)
            packed[k] = jnp.where((lane_group == g) & mine, moved, packed[k])
        after_e, after_o = line_faces(line, cells_e, cells_o)
        rhs_e, rhs_o = line_residual(line, after_e, after_o)
        put_vec(rhs, 0, rhs_e, (t,))
        put_vec(rhs, 5, rhs_o, (t,))
        states.append(first_level(line, after_e, after_o, keep1, t))
    line_levels(line, states, keep1, keep2, keep3, ends, work)
    for place, at in enumerate((50, 75, 0, 25)):
        for c in range(25):
            k, g = divmod(25 * place + c, 32)
            packed[k] = jnp.where(lane_group == g, line.roll(ends[at + c], 4 * g), packed[k])
    for k in range(4):
        note[k] = packed[k]


def put_face(ref, lead, face):
    for which in range(3):
        at = 0
        for i in range(5):
            for j in range(i, 5):
                ref[lead + (15 * which + at,)] = face[which][i][j]
                at += 1


def get_face(ref, lead):
    out = []
    for which in range(3):
        m = [[None] * 5 for _ in range(5)]
        at = 0
        for i in range(5):
            for j in range(i, 5):
                m[i][j] = m[j][i] = ref[lead + (15 * which + at,)]
                at += 1
        out.append(m)
    return out + [None]


def wall_faces_kernel(cells, coefs, rhs):
    state, metrics, step, spread = split_cells(cells)
    line = Line(0)
    for t in range(2):
        cells_e, cells_o = load_cells(line, state, metrics, step, spread, t, 2, 1)
        after_e, after_o = line_faces(line, cells_e, cells_o)
        rhs_e, rhs_o = line_residual(line, after_e, after_o)
        for c in range(5):
            a, b = line.unpack1(rhs_e[c], rhs_o[c])
            rhs[2 * t, c] = a
            rhs[2 * t + 1, c] = b
        for half, face in enumerate((after_e, after_o)):
            put_face(coefs, (t, half), face)


def edge_faces(pair, cross, from_pair, from_cross):
    odd = odd_device("normal")
    left, right = [], []
    for c in range(9):
        below = either(odd, from_pair[c], from_cross[c])
        own = either(odd, cross[c], pair[c])
        left.append(jnp.concatenate([below, own], axis=0))
    for c in range(7):
        above = either(odd, from_cross[c], from_pair[c])
        own = either(odd, pair[c], cross[c])
        right.append(jnp.concatenate([own, above], axis=0))
    return face_values(left, right)


def wall_kernel(coefs, edge, keep1, keep2, keep3, ends, close, segment):
    line = Line(0)
    states = []
    for t in range(2):
        after_e, after_o = get_face(coefs, (t, 0)), get_face(coefs, (t, 1))
        states.append(first_level(line, after_e, after_o, keep1, t))
    line_levels(line, states, keep1, keep2, keep3, ends, None)
    damp_f, low_f, upp_f, _ = get_face(edge, ())
    low, mid_l, mid_r, upp = (get_mat(ends, 25 * at) for at in range(4))
    inverse = mat_inv(plus_eye(mat_add(mid_l, damp_f)))
    w_low = mat_mul(inverse, low)
    w_upp = mat_mul(inverse, upp_f)
    put_mat(close, 0, inverse)
    put_mat(close, 25, upp)
    put_mat(close, 50, low_f)
    put_mat(close, 75, w_low)
    put_mat(close, 100, w_upp)
    mid_r = mat_sub(mid_r, mat_mul(upp, w_low))
    upp = mat_neg(mat_mul(upp, w_upp))
    low = mat_neg(mat_mul(low_f, w_low))
    mid_l = mat_sub(damp_f, mat_mul(low_f, w_upp))
    for at, m in enumerate((mid_r, upp, low, mid_l)):
        put_mat(segment, 25 * at, mat_map(lambda x: x[0:4], m))


def segment_mats(ref):
    return [get_mat(ref, 25 * at) for at in range(4)]


def tree_bit(level):
    return ((lax.axis_index("normal") >> level) & 1) == 1


def merge_kernel(*refs, level, last):
    node, result = refs[-2:]
    if level == 0:
        lower, upper = segment_mats(refs[0].at[0]), segment_mats(refs[0].at[1])
    else:
        upside = tree_bit(level)
        mine, theirs = segment_mats(refs[0]), segment_mats(refs[1])
        lower = [mat_map(lambda a, b: either(upside, b, a), m, t) for m, t in zip(mine, theirs)]
        upper = [mat_map(lambda a, b: either(upside, a, b), m, t) for m, t in zip(mine, theirs)]
    inverse = mat_inv(mat_add(lower[3], upper[0]))
    w_low = mat_mul(inverse, lower[2])
    up_in = mat_mul(lower[1], inverse)
    low_in = mat_mul(upper[2], inverse)
    w_upp = mat_mul(inverse, upper[1])
    for at, m in enumerate((inverse, up_in, low_in, w_low, w_upp)):
        put_mat(node, 25 * at, m)
    mid_r = mat_sub(lower[0], mat_mul(lower[1], w_low))
    upp = mat_neg(mat_mul(lower[1], w_upp))
    low = mat_neg(mat_mul(upper[2], w_low))
    mid_l = mat_sub(upper[3], mat_mul(upper[2], w_upp))
    if last:
        top = tree_bit(level + 1)
        first = mat_inv(mid_r)
        through = mat_mul(low, first)
        core = mat_map(
            lambda a, b: either(top, a, b), mid_r, mat_sub(mid_l, mat_mul(through, upp))
        )
        parts = (core, through, first, upp)
    else:
        parts = (mid_r, upp, low, mid_l)
    for at, m in enumerate(parts):
        put_mat(result, 25 * at, m)


def merge_loads(upside, up_in, low_in, mine, theirs):
    lower = [vec_map(lambda a, b: either(upside, b, a), m, t) for m, t in zip(mine, theirs)]
    upper = [vec_map(lambda a, b: either(upside, a, b), m, t) for m, t in zip(mine, theirs)]
    load = vec_add(lower[1], upper[0])
    right = vec_sub(lower[0], mat_vec(up_in, load))
    left = vec_sub(upper[1], mat_vec(low_in, load))
    return load, (right, left)


def in_order(position, count):
    def pick(values, q):
        ks = sorted({c ^ ((c + q) % count) for c in range(count)})
        wanted = position ^ ((position + q) % count)
        out = values[ks[0]]
        for k in ks[1:]:
            out = jnp.where(wanted == k, values[k], out)
        return out

    return pick


def wrap_rhs_kernel(
    pair, cross, from_pair, from_cross, rhs_wall, rhs_wrap, note, keep1, keep2, keep3, zs, sent, edge
):
    line, wall = Line(1), Line(0)
    face = edge_faces(pair, cross, from_pair, from_cross)
    through = face[3]
    put_face(edge, (), [mat_map(lambda x: wall.roll(x, 4), m) for m in face[:3]])
    rhs_e, rhs_o = [], []
    for t in range(2):
        spans = []
        for s in (2 * t, 2 * t + 1):
            values = []
            for c in range(5):
                x = rhs_wall[s, c]
                x = jnp.where(wall.at == 0, x + wall.roll(through[c], -s), x)
                x = jnp.where(wall.at == 7, x - wall.roll(through[c], 3 - s), x)
                values.append(x)
            spans.append(values)
        packed = [line.pack1(a, b) for a, b in zip(*spans)]
        rhs_e.append([packed[c][0] + rhs_wrap[t, c] for c in range(5)])
        rhs_o.append([packed[c][1] + rhs_wrap[t, 5 + c] for c in range(5)])
    r_r, r_l = line_forward(line, rhs_e, rhs_o, keep1, keep2, keep3, zs)
    for k in range(3):
        sent[k] = note[k]
    tail = note[3]
    for c in range(10):
        g = 116 + c - 96
        value = r_r[c] if c < 5 else r_l[c - 5]
        tail = jnp.where(line.group == g, line.roll(value, 4 * g), tail)
    sent[3] = tail


def cycle_kernel(*refs, count):
    arrived = refs[:count]
    (keep1, keep2, tail, zs, wkeep1, wkeep2, wkeep3, close) = refs[count : count + 8]
    sent, wzs, closed = refs[count + 8 :]
    pick = in_order(lax.axis_index("wrap"), count)
    notes = [
        [pick([ref[k] for ref in arrived], q) for k in range(4)] for q in range(count)
    ]
    line = Line(1)
    period = 4 * count
    repeat = line.at % period
    channels = [None] * 126
    for k in range(4):
        rolled = [line.roll(notes[q][k], 4 * q) for q in range(count)]
        for a in range(count):
            which = (line.group - a) % count
            mixed = rolled[0]
            for q in range(1, count):
                mixed = jnp.where(which == q, rolled[q], mixed)
            for c in range(a, 32, count):
                if 32 * k + c < 126:
                    index = (repeat + 4 * c) & (LANES - 1)
                    channels[32 * k + c] = jnp.take_along_axis(mixed, index, axis=1)

    def mat_at(at):
        return [[channels[at + 5 * i + j] for j in range(5)] for i in range(5)]

    mid_r, upp, low, mid_l = (mat_at(25 * i) for i in range(4))
    left = channels[100:109]
    right = line.vroll(channels[109:116], -4)
    r_r, r_l = channels[116:121], channels[121:126]
    damp_f, low_f, upp_f, flux = face_values(left, right)
    inverse = mat_inv(plus_eye(mat_add(mid_l, damp_f)))
    w_low = mat_mul(inverse, low)
    w_upp = mat_mul(inverse, upp_f)
    zb = mat_vec(inverse, vec_sub(r_l, flux))
    mid = mat_add(
        mat_sub(mid_r, mat_mul(upp, w_low)),
        line.mroll(mat_sub(damp_f, mat_mul(low_f, w_upp)), 4),
    )
    ahead = mat_neg(mat_mul(upp, w_upp))
    back = mat_neg(line.mroll(mat_mul(low_f, w_low), 4))
    load = vec_add(
        vec_sub(r_r, mat_vec(upp, zb)), line.vroll(vec_sub(flux, mat_vec(low_f, zb)), 4)
    )
    reach = 1
    while 2 * reach < count:
        inverse = mat_inv(mid)
        wb, wa, z = mat_mul(inverse, back), mat_mul(inverse, ahead), mat_vec(inverse, load)
        by = 4 * reach
        mid = mat_sub(
            mid,
            mat_add(
                mat_mul(back, line.mroll(wa, by)), mat_mul(ahead, line.mroll(wb, -by))
            ),
        )
        load = vec_sub(
            load,
            vec_add(mat_vec(back, line.vroll(z, by)), mat_vec(ahead, line.vroll(z, -by))),
        )
        back, ahead = (
            mat_neg(mat_mul(back, line.mroll(wb, by))),
            mat_neg(mat_mul(ahead, line.mroll(wa, -by))),
        )
        reach *= 2
    both = mat_add(back, ahead)
    inverse = mat_inv(mid)
    w, z = mat_mul(inverse, both), mat_vec(inverse, load)
    by = 4 * reach
    mid = mat_sub(mid, mat_mul(both, line.mroll(w, by)))
    load = vec_sub(load, mat_vec(both, line.vroll(z, by)))
    x = mat_vec(mat_inv(mid), load)
    b = vec_sub(zb, vec_add(mat_vec(w_low, x), mat_vec(w_upp, line.vroll(x, -4))))
    spread = line.at & 3
    first = [jnp.take_along_axis(y, spread, axis=1) for y in x]
    last = [jnp.take_along_axis(y, spread, axis=1) for y in b]
    swept = [x for pair in line_backward(line, first, last, keep1, keep2, tail, zs) for x in pair]

    wall = Line(0)
    rhs_e, rhs_o = [], []
    for t in range(2):
        packed = [wall.pack1(p, q) for p, q in zip(swept[2 * t], swept[2 * t + 1])]
        rhs_e.append([p[0] for p in packed])
        rhs_o.append([p[1] for p in packed])
    r_r, r_l = line_forward(wall, rhs_e, rhs_o, wkeep1, wkeep2, wkeep3, wzs)
    zb = mat_vec(get_mat(close, 0), r_l)
    put_vec(closed, 0, zb)
    out_r = vec_sub(r_r, mat_vec(get_mat(close, 25), zb))
    out_l = vec_map(lambda y: -y, mat_vec(get_mat(close, 50), zb))
    put_vec(sent, 0, [y[0:4] for y in out_r])
    put_vec(sent, 5, [y[0:4] for y in out_l])


def joint_rhs_kernel(own, other, node, *refs, level, last):
    mine = (get_vec(own, 0), get_vec(own, 5))
    theirs = (get_vec(other, 0), get_vec(other, 5))
    load, (right, left) = merge_loads(
        tree_bit(level), get_mat(node, 25), get_mat(node, 50), mine, theirs
    )
    if not last:
        middle, sent = refs
        put_vec(middle, 0, mat_vec(get_mat(node, 0), load))
        put_vec(sent, 0, right)
        put_vec(sent, 5, left)
        return
    half, middle, sent = refs
    put_vec(middle, 0, mat_vec(get_mat(node, 0), load))
    put_vec(middle, 5, right)
    top = tree_bit(level + 1)
    closed = vec_sub(left, mat_vec(get_mat(half, 25), right))
    for c in range(25):
        sent[c] = half[c]
    put_vec(sent, 25, vec_map(lambda a, b: either(top, a, b), right, closed))


def mat_solve(matrix, load):
    a = [list(row) + [x] for row, x in zip(matrix, load)]
    for k in range(5):
        over = 1.0 / a[k][k]
        for j in range(k + 1, 6):
            a[k][j] = a[k][j] * over
        for i in range(k + 1, 5):
            for j in range(k + 1, 6):
                a[i][j] = a[i][j] - a[i][k] * a[k][j]
    x = [None] * 5
    for i in reversed(range(5)):
        total = a[i][5]
        for j in range(i + 1, 5):
            total = total - a[i][j] * x[j]
        x[i] = total
    return x


def finish_kernel(own, other, half, *refs, levels):
    nodes, middles = refs[: levels - 1], refs[levels - 1 : 2 * levels - 2]
    (keep1, keep2, tail, close, closed, zs, field, held, sems) = refs[2 * levels - 2 :]
    line = Line(0)
    between = mat_solve(
        mat_add(get_mat(own, 0), get_mat(other, 0)),
        vec_add(get_vec(own, 25), get_vec(other, 25)),
    )
    below = mat_vec(
        get_mat(half, 50),
        vec_sub(get_vec(middles[-1], 5), mat_vec(get_mat(half, 75), between)),
    )
    top = tree_bit(levels - 1)
    below, above = (
        vec_map(lambda a, b: either(top, b, a), below, between),
        vec_map(lambda b: either(top, 0.0, b), between),
    )
    for level in reversed(range(levels - 1)):
        node = nodes[level]
        between = vec_sub(
            get_vec(middles[level], 0),
            vec_add(mat_vec(get_mat(node, 75), below), mat_vec(get_mat(node, 100), above)),
        )
        upside = tree_bit(level)
        below, above = (
            vec_map(lambda a, b: either(upside, b, a), below, between),
            vec_map(lambda a, b: either(upside, b, a), between, above),
        )
    first, nexts = below, above
    first = [jnp.concatenate([x, x], axis=0) for x in first]
    nexts = [jnp.concatenate([x, x], axis=0) for x in nexts]
    last = vec_sub(
        get_vec(closed, 0),
        vec_add(mat_vec(get_mat(close, 75), first), mat_vec(get_mat(close, 100), nexts)),
    )
    last = [jnp.where(line.at < 4, x, line.roll(x, 4)) for x in last]
    copies = []
    for t, pair in enumerate(line_backward(line, first, last, keep1, keep2, tail, zs)):
        for s in range(2):
            for c in range(5):
                held[t, c, s] = pair[s][c]
        copies.append(
            pltpu.make_async_copy(held.at[t], field.at[:, 2 * t : 2 * t + 2], sems.at[t])
        )
        copies[-1].start()
    for copy in copies:
        copy.wait()


def call(kernel, name, shapes, flops, *args, scratch=(), output=pltpu.VMEM):
    return pl.pallas_call(
        kernel,
        name=name,
        out_shape=[jax.ShapeDtypeStruct(s, jnp.float32) for s in shapes],
        in_specs=[pl.BlockSpec(memory_space=pltpu.VMEM)] * len(args),
        out_specs=[pl.BlockSpec(memory_space=output)] * len(shapes),
        scratch_shapes=[
            pltpu.VMEM(s, jnp.float32) if isinstance(s, tuple) else s for s in scratch
        ],
        compiler_params=pltpu.CompilerParams(vmem_limit_bytes=VMEM_LIMIT),
        cost_estimate=pl.CostEstimate(flops=flops, bytes_accessed=1 << 20, transcendentals=0),
    )(*args)


def swapped(x, axis, count, by):
    return lax.ppermute(x, axis, [(i, i ^ by) for i in range(count)])


def on_device(state, metrics, time_step, dissipation, *, wrap_count, wall_count):
    levels = wall_count.bit_length() - 1
    row = (4, LANES)
    cells = jnp.concatenate([state, metrics, time_step[None], dissipation], axis=0)
    pair, cross = call(enter_kernel, "enter", [(9,) + row, (9,) + row], 1 << 12, cells)
    across = [(i, i + 1) for i in range(1, wall_count - 1, 2)]
    across += [(b, a) for a, b in across]
    from_pair = swapped(pair, "normal", wall_count, 1)
    from_cross = lax.ppermute(cross, "normal", across)
    coefs, rhs_wall = call(
        wall_faces_kernel, "wall_faces", [(2, 2, 45) + TILE, (4, 5) + TILE], 8 << 20, cells
    )
    keep1, keep2, keep3, rhs_wrap, note, ends = call(
        wrap_kernel,
        "wrap",
        [
            (2, 125) + TILE,
            (125,) + TILE,
            (5, 75) + TILE,
            (2, 10) + TILE,
            (4,) + TILE,
            (100,) + TILE,
        ],
        40 << 20,
        cells,
        scratch=[(100,) + TILE],
    )
    zs, own, edge = call(
        wrap_rhs_kernel,
        "wrap_rhs",
        [(20,) + TILE, (4,) + TILE, (45,) + TILE],
        8 << 20,
        pair,
        cross,
        from_pair,
        from_cross,
        rhs_wall,
        rhs_wrap,
        note,
        keep1,
        keep2,
        keep3,
    )
    notes = [own] + [None] * (wrap_count - 1)
    for k in [1, 3, 2] + list(range(4, wrap_count)):
        notes[k] = swapped(own, "wrap", wrap_count, k)
    wkeep1, wkeep2, wkeep3, wends, close, segment = call(
        wall_kernel,
        "wall",
        [
            (2, 125) + TILE,
            (125,) + TILE,
            (1, 75) + TILE,
            (100,) + TILE,
            (125,) + TILE,
            (100,) + row,
        ],
        20 << 20,
        coefs,
        edge,
    )
    joined = [
        lax.all_gather(
            segment, "normal", axis_index_groups=[[i, i + 1] for i in range(0, wall_count, 2)]
        )
    ]
    (tail,) = call(tail_kernel, "tail", [(75,) + TILE], 3 << 20, ends, own)
    sent, wzs, closed = call(
        lambda *refs: cycle_kernel(*refs, count=wrap_count),
        "cycle",
        [(10,) + row, (20,) + TILE, (5,) + TILE],
        10 << 20,
        *notes,
        keep1,
        keep2,
        tail,
        zs,
        wkeep1,
        wkeep2,
        wkeep3,
        close,
    )
    nodes = []
    for level in range(levels - 1):
        last = level == levels - 2
        node, result = call(
            lambda *refs: merge_kernel(*refs, level=level, last=last),
            "merge_%d" % level,
            [(125,) + row, (100,) + row],
            4 << 20,
            *joined,
            *(notes[1:] if level == 0 else []),
        )
        nodes.append(node)
        if not last:
            joined = [result, swapped(result, "normal", wall_count, 2 << level)]
    middles = []
    for level in range(levels - 1):
        last = level == levels - 2
        partner = swapped(sent, "normal", wall_count, 1 << level)
        middle, sent = call(
            lambda *refs: joint_rhs_kernel(*refs, level=level, last=last),
            "joint_rhs_%d" % level,
            [(10 if last else 5,) + row, (30 if last else 10,) + row],
            1 << 16,
            sent,
            partner,
            nodes[level],
            *([result] if last else []),
        )
        middles.append(middle)
    (wtail,) = call(tail_kernel, "wall_tail", [(75,) + TILE], 3 << 20, wends, sent)
    partner = swapped(sent, "normal", wall_count, 1 << (levels - 1))
    (field,) = call(
        lambda *refs: finish_kernel(*refs, levels=levels),
        "finish",
        [(5, 4) + TILE],
        4 << 20,
        sent,
        partner,
        result,
        *nodes,
        *middles,
        wkeep1,
        wkeep2,
        wtail,
        close,
        closed,
        wzs,
        scratch=[(2, 5, 2) + TILE, pltpu.SemaphoreType.DMA((2,))],
        output=pltpu.HBM,
    )
    return field


def solution(mesh):
    placed = (
        P(None, None, "normal", "wrap"),
        P(None, None, "normal", "wrap"),
        P(None, "normal", "wrap"),
        P(None, None, "normal", "wrap"),
    )

    def body(state, metrics, time_step, dissipation):
        return on_device(
            state,
            metrics,
            time_step,
            dissipation,
            wrap_count=mesh.shape["wrap"],
            wall_count=mesh.shape["normal"],
        )

    return jax.shard_map(
        body,
        mesh=mesh,
        in_specs=placed,
        out_specs=P(None, None, "normal", "wrap"),
        check_vma=False,
    )
```
